32 devices in a mesh: blk: 32 (over z, y, x, core).
Axes of the slice: x: 2, y: 2, z: 4, core: 2. Of those that a mesh axis runs over, the one named last changes fastest.
Arguments:
- probe_vecs: bfloat16 [4096, 16, 128], P('blk'), may hold values from -6 to 6
- coeffs: bfloat16 [4096, 4, 128, 128], P('blk'), may hold values from -0.25 to 0.25
- cond_prec: bfloat16 [4096, 128, 128], P('blk'), may hold values from -1 to 5, as said below
- neighbours: int32 [4096, 4], P('blk'), may hold values from 0 to 4095, as said below
Outputs:
- qv: float32 [4096, 16, 128], P('blk')
The draws below stay inside these ranges and needn't reach their ends.
Inputs may be any that keep to these rules, and one draw needn't show every extreme that they name: `neighbours`: columns 0 to 2 name three different blocks 1 to 16 places before the block, counting cyclically over all 4096 blocks. Column 3 names a block outside the block's own group of 128 consecutive blocks; it may coincide with a near neighbour. Of the blocks of one group, at most 5 name column-3 blocks in one same other group, and in every group some other group is named exactly 5 times. No two blocks of one group name the same column-3 block; blocks of different groups may name the same block, and all their far terms are added. `cond_prec`: each block is a diagonal matrix with entries between 0.25 and 4 plus off-diagonal noise (also on the diagonal) of magnitude at most 1.8 / sqrt(128).
All inputs are finite; a program needn't handle non-finite values.
Results may differ from the reference program's by a relative error of at most 0.0035.
Values may be sent and summed in bfloat16 or wider, within the bound.
No kernel may reach another device: no remote copies, remote signals or barrier semaphores. Data moves between devices by JAX's collectives and lax.ppermute only.
A program may use at most 128 MiB of HBM per device.

```python
import jax
import jax.numpy as jnp
from jax import lax

M = 128
PROBES = 16
NBR = 4
NEAR = 16
BLK_DEV = 128
NBLOCKS = 4096
FAR_CAP = 5


def draw_cond_prec(key, part):
    key_diag = jax.random.fold_in(key, 11)
    key_off = jax.random.fold_in(key, 12)
    diag_vals = jnp.exp(jax.random.uniform(key_diag, (NBLOCKS, M, 1), jnp.float32, jnp.log(0.5), jnp.log(2.0)))
    off_vals = jnp.clip(jax.random.normal(key_off, (NBLOCKS, M, M), jnp.float32), -3.0, 3.0) * (0.6 / M ** 0.5)
    eye_mat = (jnp.arange(M)[:, None] == jnp.arange(M)[None, :]).astype(jnp.float32)
    return (off_vals + eye_mat[None] * diag_vals).astype(jnp.bfloat16)


def draw_neighbours(key, part):
    group_count = NBLOCKS // BLK_DEV
    key_near = jax.random.fold_in(key, 21)
    key_far = jax.random.fold_in(key, 22)
    near_scores = jax.random.randint(key_near, (NBLOCKS, NEAR), 0, 1 << 20) * NEAR + jnp.arange(NEAR, dtype=jnp.int32)[None, :]
    _, near_pick = lax.top_k(near_scores, 3)
    block_ids = jnp.arange(NBLOCKS, dtype=jnp.int32)
    near_ids = (block_ids[:, None] - (near_pick.astype(jnp.int32) + 1)) % NBLOCKS
    slot_total = (group_count - 1) * FAR_CAP

    def one_group(group_no):
        group_key = jax.random.fold_in(key_far, group_no)
        key_perm = jax.random.fold_in(group_key, 1)
        key_full = jax.random.fold_in(group_key, 2)
        key_shuffle = jax.random.fold_in(group_key, 3)
        key_base = jax.random.fold_in(group_key, 4)
        slot_perm = jax.random.permutation(key_perm, slot_total).astype(jnp.int32)
        drawn_owner = jax.random.randint(key_full, (), 0, group_count - 1).astype(jnp.int32)
        full_owner = jnp.where(group_no == 0, group_count - 2, drawn_owner).astype(jnp.int32)
        slot_ids = jnp.arange(slot_total, dtype=jnp.int32)
        slot_scores = slot_perm + jnp.where(slot_ids // FAR_CAP == full_owner, slot_total, 0).astype(jnp.int32)
        _, chosen = lax.top_k(slot_scores, BLK_DEV)
        chosen = jax.random.permutation(key_shuffle, chosen.astype(jnp.int32))
        offset_ids = chosen // FAR_CAP + 1
        slot_rank = chosen % FAR_CAP
        owner_dev = (group_no + offset_ids) % group_count
        base_pos = jax.random.randint(key_base, (group_count,), 0, BLK_DEV)
        local_pos = (base_pos[offset_ids] + slot_rank) % BLK_DEV
        return owner_dev * BLK_DEV + local_pos
    far_ids = jax.vmap(one_group)(jnp.arange(group_count, dtype=jnp.int32)).reshape(NBLOCKS)
    return jnp.concatenate([near_ids, far_ids[:, None]], axis=1).astype(jnp.int32)


def block_scale(rng, extent, shards, smallest, high):
    gain = 1.0
    for axis_at, shards_of in shards:
        draws = jax.random.uniform(jax.random.fold_in(jax.random.fold_in(rng, 6), axis_at), (shards_of,), jnp.float32, smallest / len(shards), high / len(shards))
        gain = gain * jnp.repeat(jnp.exp(draws), extent[axis_at] // shards_of).reshape((-1,) + (1,) * (len(extent) - 1 - axis_at))
    return gain


def bell_draw(key, dims, deviation, reach, pieces=(), kind=jnp.bfloat16):
    entries = deviation * jax.random.normal(key, dims, jnp.float32)
    if pieces:
        entries = entries * block_scale(key, dims, pieces, -0.22, 0.18)
    return jnp.clip(entries, -reach, reach).astype(kind)


def setup_inputs(seed: int = 0) -> dict:
    splits = jax.random.split(jax.random.key(seed), 5)
    return {
        "probe_vecs": bell_draw(splits[0], (NBLOCKS, PROBES, M), 1.0, 6.0, ((0, 32),)),
        "coeffs": bell_draw(splits[1], (NBLOCKS, NBR, M, M), (NBR * M) ** -0.5, 0.25, ((0, 32),)),
        "cond_prec": draw_cond_prec(jax.random.fold_in(splits[4], 71), 0),
        "neighbours": draw_neighbours(jax.random.fold_in(splits[4], 71), 0),
    }


def reference(probe_vecs, coeffs, cond_prec, neighbours):
    group_count = NBLOCKS // BLK_DEV

    def one_group(accumulator, step_no):
        first_block = step_no * BLK_DEV
        own_vecs = lax.dynamic_slice_in_dim(probe_vecs, first_block, BLK_DEV, 0)
        own_coeffs = lax.dynamic_slice_in_dim(coeffs, first_block, BLK_DEV, 0).astype(jnp.float32)
        own_prec = lax.dynamic_slice_in_dim(cond_prec, first_block, BLK_DEV, 0).astype(jnp.float32)
        own_nbrs = lax.dynamic_slice_in_dim(neighbours, first_block, BLK_DEV, 0)
        nbr_tiles = probe_vecs[own_nbrs].astype(jnp.float32)
        mixed_sums = jnp.einsum("bkpn,bknm->bpm", nbr_tiles, own_coeffs)
        whitened = (own_vecs.astype(jnp.float32) - mixed_sums).astype(jnp.bfloat16)
        scaled = jnp.einsum("bpm,bmn->bpn", whitened.astype(jnp.float32), own_prec).astype(jnp.bfloat16)
        scaled_f = scaled.astype(jnp.float32)
        back_terms = jnp.einsum("bpn,bkmn->bkpm", scaled_f, own_coeffs)
        far_part = lax.optimization_barrier(back_terms[:, 3].astype(jnp.bfloat16)).astype(jnp.float32)
        near_part = back_terms[:, :3]
        accumulator = accumulator.at[own_nbrs[:, :3].reshape(-1)].add(-near_part.reshape(-1, PROBES, M))
        accumulator = accumulator.at[own_nbrs[:, 3]].add(-far_part)
        current = lax.dynamic_slice_in_dim(accumulator, first_block, BLK_DEV, 0)
        accumulator = lax.dynamic_update_slice_in_dim(accumulator, current + scaled_f, first_block, 0)
        return accumulator, None

    start_acc = jnp.zeros((NBLOCKS, PROBES, M), jnp.float32)
    result, _ = lax.scan(one_group, start_acc, jnp.arange(group_count, dtype=jnp.int32))
    return result
```

```python
import functools

import jax
import jax.numpy as jnp
from jax import lax
from jax.experimental import pallas as pl
from jax.experimental.pallas import tpu as pltpu
from jax.sharding import PartitionSpec as P

REACH = 16
CHUNK = 16
VMEM = pl.BlockSpec(memory_space=pltpu.VMEM)
SMEM = pl.BlockSpec(memory_space=pltpu.SMEM)
HBM = pl.BlockSpec(memory_space=pl.ANY)
NT = (((1,), (1,)), ((), ()))


def params(mib):
    return pltpu.CompilerParams(vmem_limit_bytes=mib * 2**20)


def passed_along(block, axis, distance):
    size = lax.axis_size(axis)
    return lax.ppermute(block, axis, [((i - distance) % size, i) for i in range(size)])


def earlier_matrix(blocks):
    row = lax.broadcasted_iota(jnp.int32, (blocks, blocks), 0)
    col = lax.broadcasted_iota(jnp.int32, (blocks, blocks), 1)
    return (row < col).astype(jnp.float32).astype(jnp.bfloat16)


def ranks_in(mask, blocks):
    chosen = mask.astype(jnp.float32).astype(jnp.bfloat16)
    return jnp.dot(chosen, earlier_matrix(blocks), preferred_element_type=jnp.float32).astype(jnp.int32)


def pick_kernel(capacity, ids_ref, probe_ref, out_ref, picks_ref, picks_smem, sem):
    groups, blocks = ids_ref.shape
    me = lax.axis_index("blk")
    local = ids_ref[...] - me * blocks
    mask = (local >= 0) & (local < blocks)
    rank = ranks_in(mask, blocks)
    lane = lax.broadcasted_iota(jnp.int32, (groups, blocks), 1)
    picks = jnp.zeros((groups, blocks), jnp.int32)
    for r in range(capacity):
        found = jnp.sum(jnp.where(mask & (rank == r), local + 1, 0), axis=1, keepdims=True)
        picks = jnp.where(lane == r, found, picks)
    picks_ref[...] = picks
    copy = pltpu.make_async_copy(picks_ref, picks_smem, sem)
    copy.start()
    copy.wait()

    @pl.loop(0, groups, unroll=8)
    def _(g):
        for r in range(capacity):
            out_ref[g * capacity + r] = probe_ref[jnp.maximum(picks_smem[g, r] - 1, 0)]


def near_place(ids_ref, k, i, first, count):
    place = ids_ref[k, i] - first + REACH
    return jnp.where(place >= count, place - count, place)


def near_forward_kernel(
    groups, capacity, ids_ref, far_ref, halo_ref, probe_ref, coeffs_ref, out_ref, slot_ref, ext, coeffs, sems
):
    blocks = probe_ref.shape[0]
    chunks = blocks // CHUNK

    def load(c):
        own = pl.ds(c * CHUNK, CHUNK)
        return pltpu.make_async_copy(coeffs_ref.at[own, pl.ds(0, 3)], coeffs.at[own], sems.at[c])

    for c in range(chunks):
        load(c).start()
    ext[pl.ds(0, REACH)] = halo_ref[...]
    ext[pl.ds(REACH, blocks)] = probe_ref[...]
    owner = far_ref[...] // blocks
    mask = lax.broadcasted_iota(jnp.int32, (groups, blocks), 0) == owner
    rank = jnp.sum(jnp.where(mask, ranks_in(mask, blocks), 0), axis=0, keepdims=True)
    slot_ref[...] = owner * capacity + rank
    first = lax.axis_index("blk") * blocks

    @pl.loop(0, chunks)
    def _(c):
        load(c).wait()
        for b in range(CHUNK):
            i = c * CHUNK + b
            tiles = [ext[near_place(ids_ref, k, i, first, groups * blocks)] for k in range(3)]
            mat = coeffs[i].reshape(3 * coeffs.shape[2], coeffs.shape[3])
            mixed = jnp.dot(jnp.concatenate(tiles, axis=1), mat, preferred_element_type=jnp.float32)
            out_ref[i] = probe_ref[i].astype(jnp.float32) - mixed


def far_kernel(slot_ref, part_ref, far_ref, coeffs_ref, prec_ref, scaled_ref, parcel_ref, coeffs, prec, sems):
    blocks = part_ref.shape[0]
    chunks = blocks // CHUNK

    def loads(c):
        own = pl.ds(c * CHUNK, CHUNK)
        return (
            pltpu.make_async_copy(coeffs_ref.at[own, 3], coeffs.at[own], sems.at[0, c]),
            pltpu.make_async_copy(prec_ref.at[own], prec.at[own], sems.at[1, c]),
        )

    for c in range(chunks):
        for load in loads(c):
            load.start()
    parcel_ref[...] = jnp.zeros_like(parcel_ref)

    @pl.loop(0, chunks)
    def _(c):
        for load in loads(c):
            load.wait()
        white = []
        for b in range(CHUNK):
            i = c * CHUNK + b
            mixed = jnp.dot(far_ref[slot_ref[0, i]], coeffs[i], preferred_element_type=jnp.float32)
            white.append((part_ref[i] - mixed).astype(jnp.bfloat16))
        scaled = []
        for b in range(CHUNK):
            i = c * CHUNK + b
            scaled.append(jnp.dot(white[b], prec[i], preferred_element_type=jnp.float32).astype(jnp.bfloat16))
            scaled_ref[i] = scaled[b]
        for b in range(CHUNK):
            i = c * CHUNK + b
            term = lax.dot_general(scaled[b], coeffs[i], NT, preferred_element_type=jnp.float32)
            parcel_ref[slot_ref[0, i]] = term.astype(jnp.bfloat16)


def near_back_kernel(groups, ids_ref, scaled_ref, coeffs_ref, base_ref, halo_ref, total, coeffs, sems):
    blocks = scaled_ref.shape[0]
    points = scaled_ref.shape[2]
    chunks = blocks // CHUNK

    def load(c):
        own = pl.ds(c * CHUNK, CHUNK)
        return pltpu.make_async_copy(coeffs_ref.at[own, pl.ds(0, 3)], coeffs.at[own], sems.at[c])

    for c in range(chunks):
        load(c).start()
    total[pl.ds(0, REACH)] = jnp.zeros((REACH,) + total.shape[1:], jnp.float32)
    total[pl.ds(REACH, blocks)] = scaled_ref[...].astype(jnp.float32)
    first = lax.axis_index("blk") * blocks

    @pl.loop(0, chunks)
    def _(c):
        load(c).wait()
        terms = []
        for b in range(CHUNK):
            i = c * CHUNK + b
            mat = coeffs[i].reshape(3 * coeffs.shape[2], coeffs.shape[3])
            terms.append(lax.dot_general(scaled_ref[i], mat, NT, preferred_element_type=jnp.float32))
        for b in range(CHUNK):
            i = c * CHUNK + b
            for k in range(3):
                place = near_place(ids_ref, k, i, first, groups * blocks)
                total[place] = total[place] - terms[b][:, k * points : (k + 1) * points]

    halo_ref[...] = total[pl.ds(0, REACH)]
    base_ref[...] = total[pl.ds(REACH, blocks)]


def sum_kernel(capacity, picks_ref, base_ref, halo_ref, back_ref, out_ref, total):
    groups = picks_ref.shape[0]
    blocks = base_ref.shape[0]
    total[pl.ds(0, blocks)] = base_ref[...]
    last = pl.ds(blocks - REACH, REACH)
    total[last] = total[last] + halo_ref[...]

    @pl.loop(0, groups, unroll=8)
    def _(g):
        for r in range(capacity):
            pick = picks_ref[g, r]
            place = jnp.where(pick > 0, pick - 1, blocks)
            total[place] = total[place] - back_ref[g * capacity + r].astype(jnp.float32)

    out_ref[...] = total[pl.ds(0, blocks)]


def per_device(probe_vecs, coeffs, cond_prec, neighbours):
    blocks, probes, points = probe_vecs.shape
    groups = lax.axis_size("blk")
    capacity = max(2, blocks // (groups - 1) + 1)
    slots = groups * capacity
    chunks = blocks // CHUNK
    bf16, f32 = jnp.bfloat16, jnp.float32
    tile = (probes, points)
    flops = 2 * blocks * probes * points * points

    def exchange(x):
        return lax.all_to_all(x, "blk", split_axis=0, concat_axis=0, tiled=True)

    ids = neighbours.T
    far_ids = ids[3:]
    halo = passed_along(probe_vecs[blocks - REACH :], "blk", 1)
    all_ids = exchange(jnp.broadcast_to(far_ids, (groups, blocks)))
    outgoing, picks = pl.pallas_call(
        functools.partial(pick_kernel, capacity),
        name="pick_tiles",
        out_shape=(
            jax.ShapeDtypeStruct((slots,) + tile, bf16),
            jax.ShapeDtypeStruct((groups, blocks), jnp.int32),
        ),
        in_specs=[VMEM, VMEM],
        out_specs=(VMEM, VMEM),
        scratch_shapes=[pltpu.SMEM((groups, blocks), jnp.int32), pltpu.SemaphoreType.DMA],
        cost_estimate=pl.CostEstimate(flops=0, bytes_accessed=2 * slots * 4096, transcendentals=0),
    )(all_ids, probe_vecs)
    arrived = exchange(outgoing.reshape((groups, capacity) + tile)).reshape((slots,) + tile)
    part, slot_of = pl.pallas_call(
        functools.partial(near_forward_kernel, groups, capacity),
        name="near_forward",
        out_shape=(
            jax.ShapeDtypeStruct((blocks,) + tile, f32),
            jax.ShapeDtypeStruct((1, blocks), jnp.int32),
        ),
        in_specs=[SMEM, VMEM, VMEM, VMEM, HBM],
        out_specs=(VMEM, VMEM),
        scratch_shapes=[
            pltpu.VMEM((REACH + blocks,) + tile, bf16),
            pltpu.VMEM((blocks, 3, points, points), bf16),
            pltpu.SemaphoreType.DMA((chunks,)),
        ],
        compiler_params=params(24),
        cost_estimate=pl.CostEstimate(flops=3 * flops, bytes_accessed=14 * 2**20, transcendentals=0),
    )(ids, far_ids, halo, probe_vecs, coeffs)
    scaled, parcel = pl.pallas_call(
        far_kernel,
        name="far_and_scale",
        out_shape=(
            jax.ShapeDtypeStruct((blocks,) + tile, bf16),
            jax.ShapeDtypeStruct((slots,) + tile, bf16),
        ),
        in_specs=[SMEM, VMEM, VMEM, HBM, HBM],
        out_specs=(VMEM, VMEM),
        scratch_shapes=[
            pltpu.VMEM((blocks, points, points), bf16),
            pltpu.VMEM((blocks, points, points), bf16),
            pltpu.SemaphoreType.DMA((2, chunks)),
        ],
        compiler_params=params(24),
        cost_estimate=pl.CostEstimate(flops=3 * flops, bytes_accessed=11 * 2**20, transcendentals=0),
    )(slot_of, part, arrived, coeffs, cond_prec)
    returned = exchange(parcel.reshape((groups, capacity) + tile)).reshape((slots,) + tile)
    base, halo_back = pl.pallas_call(
        functools.partial(near_back_kernel, groups),
        name="near_back",
        out_shape=(
            jax.ShapeDtypeStruct((blocks,) + tile, f32),
            jax.ShapeDtypeStruct((REACH,) + tile, f32),
        ),
        in_specs=[SMEM, VMEM, HBM],
        out_specs=(VMEM, VMEM),
        scratch_shapes=[
            pltpu.VMEM((REACH + blocks,) + tile, f32),
            pltpu.VMEM((blocks, 3, points, points), bf16),
            pltpu.SemaphoreType.DMA((chunks,)),
        ],
        compiler_params=params(24),
        cost_estimate=pl.CostEstimate(flops=3 * flops, bytes_accessed=14 * 2**20, transcendentals=0),
    )(ids, scaled, coeffs)
    halo_sum = passed_along(halo_back, "blk", -1)
    return pl.pallas_call(
        functools.partial(sum_kernel, capacity),
        name="final_sum",
        out_shape=jax.ShapeDtypeStruct((blocks,) + tile, f32),
        in_specs=[SMEM, VMEM, VMEM, VMEM],
        out_specs=VMEM,
        scratch_shapes=[pltpu.VMEM((blocks + 1,) + tile, f32)],
        cost_estimate=pl.CostEstimate(flops=0, bytes_accessed=3 * 2**20, transcendentals=0),
    )(picks, base, halo_sum, returned)


def solution(mesh):
    in_specs = (
        P("blk", None, None),
        P("blk", None, None, None),
        P("blk", None, None),
        P("blk", None),
    )
    return jax.shard_map(
        per_device, mesh=mesh, in_specs=in_specs, out_specs=P("blk", None, None), check_vma=False
    )
```

```python
import functools

import jax
import jax.numpy as jnp
from jax import lax
from jax.experimental import pallas as pl
from jax.experimental.pallas import tpu as pltpu
from jax.sharding import PartitionSpec as P

REACH = 16
CHUNK = 16
VMEM = pl.BlockSpec(memory_space=pltpu.VMEM)
SMEM = pl.BlockSpec(memory_space=pltpu.SMEM)
HBM = pl.BlockSpec(memory_space=pl.ANY)
NT = (((1,), (1,)), ((), ()))


def params(mib):
    return pltpu.CompilerParams(vmem_limit_bytes=mib * 2**20)


def passed_along(block, axis, distance):
    size = lax.axis_size(axis)
    return lax.ppermute(block, axis, [((i - distance) % size, i) for i in range(size)])


def earlier_matrix(blocks):
    row = lax.broadcasted_iota(jnp.int32, (blocks, blocks), 0)
    col = lax.broadcasted_iota(jnp.int32, (blocks, blocks), 1)
    return (row < col).astype(jnp.float32).astype(jnp.bfloat16)


def ranks_in(mask, blocks):
    chosen = mask.astype(jnp.float32).astype(jnp.bfloat16)
    return jnp.dot(chosen, earlier_matrix(blocks), preferred_element_type=jnp.float32).astype(jnp.int32)


def pick_kernel(capacity, ids_ref, probe_ref, out_ref, picks_ref, picks_smem, sem):
    groups, blocks = ids_ref.shape
    me = lax.axis_index("blk")
    local = ids_ref[...] - me * blocks
    mask = (local >= 0) & (local < blocks)
    rank = ranks_in(mask, blocks)
    lane = lax.broadcasted_iota(jnp.int32, (groups, blocks), 1)
    picks = jnp.zeros((groups, blocks), jnp.int32)
    for r in range(capacity):
        found = jnp.sum(jnp.where(mask & (rank == r), local + 1, 0), axis=1, keepdims=True)
        picks = jnp.where(lane == r, found, picks)
    picks_ref[...] = picks
    copy = pltpu.make_async_copy(picks_ref, picks_smem, sem)
    copy.start()
    copy.wait()

    @pl.loop(0, groups, unroll=8)
    def _(g):
        for r in range(capacity):
            out_ref[g * capacity + r] = probe_ref[jnp.maximum(picks_smem[g, r] - 1, 0)]


def near_place(ids_ref, k, i, first, count):
    place = ids_ref[k, i] - first + REACH
    return jnp.where(place >= count, place - count, place)


def near_forward_kernel(
    groups, capacity, ids_ref, far_ref, halo_ref, probe_ref, coeffs_ref, out_ref, slot_ref, ext, coeffs, sems
):
    blocks = probe_ref.shape[0]
    chunks = blocks // CHUNK

    def load(c):
        own = pl.ds(c * CHUNK, CHUNK)
        return pltpu.make_async_copy(coeffs_ref.at[own, pl.ds(0, 3)], coeffs.at[own], sems.at[c])

    for c in range(chunks):
        load(c).start()
    ext[pl.ds(0, REACH)] = halo_ref[...]
    ext[pl.ds(REACH, blocks)] = probe_ref[...]
    owner = far_ref[...] // blocks
    mask = lax.broadcasted_iota(jnp.int32, (groups, blocks), 0) == owner
    rank = jnp.sum(jnp.where(mask, ranks_in(mask, blocks), 0), axis=0, keepdims=True)
    slot_ref[...] = owner * capacity + rank
    first = lax.axis_index("blk") * blocks

    @pl.loop(0, chunks)
    def _(c):
        load(c).wait()
        for b in range(CHUNK):
            i = c * CHUNK + b
            tiles = [ext[near_place(ids_ref, k, i, first, groups * blocks)] for k in range(3)]
            mat = coeffs[i].reshape(3 * coeffs.shape[2], coeffs.shape[3])
            mixed = jnp.dot(jnp.concatenate(tiles, axis=1), mat, preferred_element_type=jnp.float32)
            out_ref[i] = probe_ref[i].astype(jnp.float32) - mixed


def far_kernel(slot_ref, part_ref, far_ref, coeffs_ref, prec_ref, scaled_ref, parcel_ref, coeffs, prec, sems):
    blocks = part_ref.shape[0]
    chunks = blocks // CHUNK

    def loads(c):
        own = pl.ds(c * CHUNK, CHUNK)
        return (
            pltpu.make_async_copy(coeffs_ref.at[own, 3], coeffs.at[own], sems.at[0, c]),
            pltpu.make_async_copy(prec_ref.at[own], prec.at[own], sems.at[1, c]),
        )

    for c in range(chunks):
        for load in loads(c):
            load.start()
    parcel_ref[...] = jnp.zeros_like(parcel_ref)

    @pl.loop(0, chunks)
    def _(c):
        for load in loads(c):
            load.wait()
        white = []
        for b in range(CHUNK):
            i = c * CHUNK + b
            mixed = jnp.dot(far_ref[slot_ref[0, i]], coeffs[i], preferred_element_type=jnp.float32)
            white.append((part_ref[i] - mixed).astype(jnp.bfloat16))
        scaled = []
        for b in range(CHUNK):
            i = c * CHUNK + b
            scaled.append(jnp.dot(white[b], prec[i], preferred_element_type=jnp.float32).astype(jnp.bfloat16))
            scaled_ref[i] = scaled[b]
        for b in range(CHUNK):
            i = c * CHUNK + b
            term = lax.dot_general(scaled[b], coeffs[i], NT, preferred_element_type=jnp.float32)
            parcel_ref[slot_ref[0, i]] = term.astype(jnp.bfloat16)


def near_back_kernel(groups, ids_ref, scaled_ref, coeffs_ref, base_ref, halo_ref, total, coeffs, sems):
    blocks = scaled_ref.shape[0]
    points = scaled_ref.shape[2]
    chunks = blocks // CHUNK

    def load(c):
        own = pl.ds(c * CHUNK, CHUNK)
        return pltpu.make_async_copy(coeffs_ref.at[own, pl.ds(0, 3)], coeffs.at[own], sems.at[c])

    for c in range(chunks):
        load(c).start()
    total[pl.ds(0, REACH)] = jnp.zeros((REACH,) + total.shape[1:], jnp.float32)
    total[pl.ds(REACH, blocks)] = scaled_ref[...].astype(jnp.float32)
    first = lax.axis_index("blk") * blocks

    @pl.loop(0, chunks)
    def _(c):
        load(c).wait()
        terms = []
        for b in range(CHUNK):
            i = c * CHUNK + b
            mat = coeffs[i].reshape(3 * coeffs.shape[2], coeffs.shape[3])
            terms.append(lax.dot_general(scaled_ref[i], mat, NT, preferred_element_type=jnp.float32))
        for b in range(CHUNK):
            i = c * CHUNK + b
            places = [near_place(ids_ref, k, i, first, groups * blocks) for k in range(3)]
            olds = [total[place] for place in places]
            for k in range(3):
                total[places[k]] = olds[k] - terms[b][:, k * points : (k + 1) * points]

    halo_ref[...] = total[pl.ds(0, REACH)]
    base_ref[...] = total[pl.ds(REACH, blocks)]


def sum_kernel(capacity, picks_ref, base_ref, halo_ref, back_ref, out_ref, total):
    groups = picks_ref.shape[0]
    blocks = base_ref.shape[0]
    total[pl.ds(0, blocks)] = base_ref[...]
    last = pl.ds(blocks - REACH, REACH)
    total[last] = total[last] + halo_ref[...]

    @pl.loop(0, groups, unroll=8)
    def _(g):
        picks = [picks_ref[g, r] for r in range(capacity)]
        places = [jnp.where(pick > 0, pick - 1, blocks) for pick in picks]
        olds = [total[place] for place in places]
        for r in range(capacity):
            total[places[r]] = olds[r] - back_ref[g * capacity + r].astype(jnp.float32)

    out_ref[...] = total[pl.ds(0, blocks)]


def per_device(probe_vecs, coeffs, cond_prec, neighbours):
    blocks, probes, points = probe_vecs.shape
    groups = lax.axis_size("blk")
    capacity = max(2, blocks // (groups - 1) + 1)
    slots = groups * capacity
    chunks = blocks // CHUNK
    bf16, f32 = jnp.bfloat16, jnp.float32
    tile = (probes, points)
    flops = 2 * blocks * probes * points * points

    def exchange(x):
        return lax.all_to_all(x, "blk", split_axis=0, concat_axis=0, tiled=True)

    ids = neighbours.T
    far_ids = ids[3:]
    halo = passed_along(probe_vecs[blocks - REACH :], "blk", 1)
    all_ids = lax.all_gather(far_ids, "blk", axis=0, tiled=True)
    all_ids, halo = lax.optimization_barrier((all_ids, halo))
    outgoing, picks = pl.pallas_call(
        functools.partial(pick_kernel, capacity),
        name="pick_tiles",
        out_shape=(
            jax.ShapeDtypeStruct((slots,) + tile, bf16),
            jax.ShapeDtypeStruct((groups, blocks), jnp.int32),
        ),
        in_specs=[VMEM, VMEM],
        out_specs=(VMEM, VMEM),
        scratch_shapes=[pltpu.SMEM((groups, blocks), jnp.int32), pltpu.SemaphoreType.DMA],
        compiler_params=params(8),
        cost_estimate=pl.CostEstimate(flops=0, bytes_accessed=2 * slots * 4096, transcendentals=0),
    )(all_ids, probe_vecs)
    arrived = exchange(outgoing.reshape((groups, capacity) + tile)).reshape((slots,) + tile)
    part, slot_of = pl.pallas_call(
        functools.partial(near_forward_kernel, groups, capacity),
        name="near_forward",
        out_shape=(
            jax.ShapeDtypeStruct((blocks,) + tile, f32),
            jax.ShapeDtypeStruct((1, blocks), jnp.int32),
        ),
        in_specs=[SMEM, VMEM, VMEM, VMEM, HBM],
        out_specs=(VMEM, VMEM),
        scratch_shapes=[
            pltpu.VMEM((REACH + blocks,) + tile, bf16),
            pltpu.VMEM((blocks, 3, points, points), bf16),
            pltpu.SemaphoreType.DMA((chunks,)),
        ],
        compiler_params=params(60),
        cost_estimate=pl.CostEstimate(flops=3 * flops, bytes_accessed=14 * 2**20, transcendentals=0),
    )(ids, far_ids, halo, probe_vecs, coeffs)
    scaled, parcel = pl.pallas_call(
        far_kernel,
        name="far_and_scale",
        out_shape=(
            jax.ShapeDtypeStruct((blocks,) + tile, bf16),
            jax.ShapeDtypeStruct((slots,) + tile, bf16),
        ),
        in_specs=[SMEM, VMEM, VMEM, HBM, HBM],
        out_specs=(VMEM, VMEM),
        scratch_shapes=[
            pltpu.VMEM((blocks, points, points), bf16),
            pltpu.VMEM((blocks, points, points), bf16),
            pltpu.SemaphoreType.DMA((2, chunks)),
        ],
        compiler_params=params(60),
        cost_estimate=pl.CostEstimate(flops=3 * flops, bytes_accessed=11 * 2**20, transcendentals=0),
    )(slot_of, part, arrived, coeffs, cond_prec)
    returned = exchange(parcel.reshape((groups, capacity) + tile)).reshape((slots,) + tile)
    base, halo_back = pl.pallas_call(
        functools.partial(near_back_kernel, groups),
        name="near_back",
        out_shape=(
            jax.ShapeDtypeStruct((blocks,) + tile, f32),
            jax.ShapeDtypeStruct((REACH,) + tile, f32),
        ),
        in_specs=[SMEM, VMEM, HBM],
        out_specs=(VMEM, VMEM),
        scratch_shapes=[
            pltpu.VMEM((REACH + blocks,) + tile, f32),
            pltpu.VMEM((blocks, 3, points, points), bf16),
            pltpu.SemaphoreType.DMA((chunks,)),
        ],
        compiler_params=params(60),
        cost_estimate=pl.CostEstimate(flops=3 * flops, bytes_accessed=14 * 2**20, transcendentals=0),
    )(ids, scaled, coeffs)
    halo_sum = passed_along(halo_back, "blk", -1)
    return pl.pallas_call(
        functools.partial(sum_kernel, capacity),
        name="final_sum",
        out_shape=jax.ShapeDtypeStruct((blocks,) + tile, f32),
        in_specs=[SMEM, VMEM, VMEM, VMEM],
        out_specs=VMEM,
        scratch_shapes=[pltpu.VMEM((blocks + 1,) + tile, f32)],
        compiler_params=params(8),
        cost_estimate=pl.CostEstimate(flops=0, bytes_accessed=3 * 2**20, transcendentals=0),
    )(picks, base, halo_sum, returned)


def solution(mesh):
    in_specs = (
        P("blk", None, None),
        P("blk", None, None, None),
        P("blk", None, None),
        P("blk", None),
    )
    return jax.shard_map(
        per_device, mesh=mesh, in_specs=in_specs, out_specs=P("blk", None, None), check_vma=False
    )
```

```python
import functools

import jax
import jax.numpy as jnp
from jax import lax
from jax.experimental import pallas as pl
from jax.experimental.pallas import tpu as pltpu
from jax.sharding import PartitionSpec as P

REACH = 16
CHUNK = 16
AHEAD = 4
STORES = 4
VMEM = pl.BlockSpec(memory_space=pltpu.VMEM)
SMEM = pl.BlockSpec(memory_space=pltpu.SMEM)
HBM = pl.BlockSpec(memory_space=pl.ANY)
NT = (((1,), (1,)), ((), ()))


def params(mib):
    return pltpu.CompilerParams(vmem_limit_bytes=mib * 2**20)


def in_hbm(x):
    return pltpu.with_memory_space_constraint(x, pltpu.HBM)


def passed_along(block, axis, distance):
    size = lax.axis_size(axis)
    return lax.ppermute(block, axis, [((i - distance) % size, i) for i in range(size)])


def earlier_matrix(blocks):
    row = lax.broadcasted_iota(jnp.int32, (blocks, blocks), 0)
    col = lax.broadcasted_iota(jnp.int32, (blocks, blocks), 1)
    return (row < col).astype(jnp.float32).astype(jnp.bfloat16)


def ranks_in(mask, blocks):
    chosen = mask.astype(jnp.float32).astype(jnp.bfloat16)
    return jnp.dot(chosen, earlier_matrix(blocks), preferred_element_type=jnp.float32).astype(jnp.int32)


def pick_kernel(capacity, ids_ref, probe_ref, out_ref, picks_ref, probe, out, picks_smem, sems):
    groups, blocks = ids_ref.shape
    load = pltpu.make_async_copy(probe_ref, probe, sems.at[0])
    load.start()
    me = lax.axis_index("blk")
    local = ids_ref[...] - me * blocks
    mask = (local >= 0) & (local < blocks)
    rank = ranks_in(mask, blocks)
    lane = lax.broadcasted_iota(jnp.int32, (groups, blocks), 1)
    picks = jnp.zeros((groups, blocks), jnp.int32)
    for r in range(capacity):
        found = jnp.sum(jnp.where(mask & (rank == r), local + 1, 0), axis=1, keepdims=True)
        picks = jnp.where(lane == r, found, picks)
    picks_ref[...] = picks
    copy = pltpu.make_async_copy(picks_ref, picks_smem, sems.at[1])
    copy.start()
    copy.wait()
    load.wait()
    part = groups // STORES

    def store(p):
        rows = pl.ds(p * part * capacity, part * capacity)
        return pltpu.make_async_copy(out.at[rows], out_ref.at[rows], sems.at[2 + p])

    for p in range(STORES):

        @pl.loop(p * part, (p + 1) * part, unroll=8)
        def _(g):
            for r in range(capacity):
                out[g * capacity + r] = probe[jnp.maximum(picks_smem[g, r] - 1, 0)]

        store(p).start()
    for p in range(STORES):
        store(p).wait()


def near_place(ids_ref, k, i, first, count):
    place = ids_ref[k, i] - first + REACH
    return jnp.where(place >= count, place - count, place)


def near_forward_kernel(
    groups, capacity, ids_ref, far_ref, halo_ref, probe_ref, coeffs_ref, out_ref, slot_ref, ext, coeffs, sems
):
    blocks = probe_ref.shape[0]
    chunks = blocks // CHUNK

    def load(c):
        own = pl.ds(c * CHUNK, CHUNK)
        return pltpu.make_async_copy(coeffs_ref.at[own, pl.ds(0, 3)], coeffs.at[own], sems.at[c])

    for c in range(chunks):
        load(c).start()
    ext[pl.ds(0, REACH)] = halo_ref[...]
    ext[pl.ds(REACH, blocks)] = probe_ref[...]
    owner = far_ref[...] // blocks
    mask = lax.broadcasted_iota(jnp.int32, (groups, blocks), 0) == owner
    rank = jnp.sum(jnp.where(mask, ranks_in(mask, blocks), 0), axis=0, keepdims=True)
    slot_ref[...] = owner * capacity + rank
    first = lax.axis_index("blk") * blocks

    @pl.loop(0, chunks)
    def _(c):
        load(c).wait()
        for b in range(CHUNK):
            i = c * CHUNK + b
            tiles = [ext[near_place(ids_ref, k, i, first, groups * blocks)] for k in range(3)]
            mat = coeffs[i].reshape(3 * coeffs.shape[2], coeffs.shape[3])
            mixed = jnp.dot(jnp.concatenate(tiles, axis=1), mat, preferred_element_type=jnp.float32)
            out_ref[i] = probe_ref[i].astype(jnp.float32) - mixed


def far_kernel(slot_ref, part_ref, far_ref, coeffs_ref, prec_ref, scaled_ref, parcel_ref, coeffs, prec, white, sems):
    blocks = part_ref.shape[0]
    chunks = blocks // CHUNK

    def loads(c):
        own = pl.ds(c * CHUNK, CHUNK)
        return (
            pltpu.make_async_copy(coeffs_ref.at[own, 3], coeffs.at[own], sems.at[0, c]),
            pltpu.make_async_copy(prec_ref.at[own], prec.at[own], sems.at[1, c]),
        )

    for c in range(chunks):
        for load in loads(c):
            load.start()
    parcel_ref[...] = jnp.zeros_like(parcel_ref)

    def mix(c):
        for b in range(CHUNK):
            i = c * CHUNK + b
            mixed = jnp.dot(far_ref[slot_ref[0, i]], coeffs[i], preferred_element_type=jnp.float32)
            white[i] = (part_ref[i] - mixed).astype(jnp.bfloat16)

    def scale(c):
        for b in range(CHUNK):
            i = c * CHUNK + b
            scaled_ref[i] = jnp.dot(white[i], prec[i], preferred_element_type=jnp.float32).astype(jnp.bfloat16)

    def back(c):
        for b in range(CHUNK):
            i = c * CHUNK + b
            term = lax.dot_general(scaled_ref[i], coeffs[i], NT, preferred_element_type=jnp.float32)
            parcel_ref[slot_ref[0, i]] = term.astype(jnp.bfloat16)

    def ready(c):
        for load in loads(c):
            load.wait()

    ready(0)
    mix(0)
    ready(1)
    scale(0)
    mix(1)

    @pl.loop(2, chunks)
    def _(c):
        ready(c)
        back(c - 2)
        scale(c - 1)
        mix(c)

    back(chunks - 2)
    scale(chunks - 1)
    back(chunks - 1)


def near_back_kernel(groups, ids_ref, scaled_ref, coeffs_ref, base_ref, halo_ref, total, coeffs, sems):
    blocks = scaled_ref.shape[0]
    points = scaled_ref.shape[2]
    chunks = blocks // CHUNK

    def load(c):
        own = pl.ds(c * CHUNK, CHUNK)
        return pltpu.make_async_copy(coeffs_ref.at[own, pl.ds(0, 3)], coeffs.at[own], sems.at[c])

    for c in range(chunks):
        load(c).start()
    total[pl.ds(0, REACH)] = jnp.zeros((REACH,) + total.shape[1:], jnp.float32)
    total[pl.ds(REACH, blocks)] = scaled_ref[...].astype(jnp.float32)
    first = lax.axis_index("blk") * blocks

    @pl.loop(0, chunks)
    def _(c):
        load(c).wait()
        terms = []
        for b in range(CHUNK + AHEAD):
            if b < CHUNK:
                i = c * CHUNK + b
                mat = coeffs[i].reshape(3 * coeffs.shape[2], coeffs.shape[3])
                terms.append(lax.dot_general(scaled_ref[i], mat, NT, preferred_element_type=jnp.float32))
            if b >= AHEAD:
                i = c * CHUNK + b - AHEAD
                places = [near_place(ids_ref, k, i, first, groups * blocks) for k in range(3)]
                olds = [total[place] for place in places]
                for k in range(3):
                    total[places[k]] = olds[k] - terms[b - AHEAD][:, k * points : (k + 1) * points]

    halo_ref[...] = total[pl.ds(0, REACH)].astype(halo_ref.dtype)
    base_ref[...] = total[pl.ds(REACH, blocks)]


def sum_kernel(capacity, picks_ref, base_ref, halo_ref, back_ref, out_ref, total, sem):
    groups = picks_ref.shape[0]
    blocks = base_ref.shape[0]
    total[pl.ds(0, blocks)] = base_ref[...]
    last = pl.ds(blocks - REACH, REACH)
    total[last] = total[last] + halo_ref[...].astype(jnp.float32)

    @pl.loop(0, groups, unroll=8)
    def _(g):
        picks = [picks_ref[g, r] for r in range(capacity)]
        places = [jnp.where(pick > 0, pick - 1, blocks) for pick in picks]
        olds = [total[place] for place in places]
        for r in range(capacity):
            total[places[r]] = olds[r] - back_ref[g * capacity + r].astype(jnp.float32)

    store = pltpu.make_async_copy(total.at[pl.ds(0, blocks)], out_ref, sem)
    store.start()
    store.wait()


def per_device(probe_vecs, coeffs, cond_prec, neighbours):
    blocks, probes, points = probe_vecs.shape
    groups = lax.axis_size("blk")
    capacity = max(2, blocks // (groups - 1) + 1)
    slots = groups * capacity
    chunks = blocks // CHUNK
    bf16, f32 = jnp.bfloat16, jnp.float32
    tile = (probes, points)
    flops = 2 * blocks * probes * points * points

    def exchange(x):
        return lax.all_to_all(x, "blk", split_axis=0, concat_axis=0, tiled=True)

    ids = neighbours.T
    far_ids = ids[3:]
    halo = passed_along(probe_vecs[blocks - REACH :], "blk", 1)
    all_ids = exchange(jnp.broadcast_to(far_ids, (groups, blocks)))
    all_ids, halo = lax.optimization_barrier((all_ids, halo))
    outgoing, picks = pl.pallas_call(
        functools.partial(pick_kernel, capacity),
        name="pick_tiles",
        out_shape=(
            jax.ShapeDtypeStruct((slots,) + tile, bf16),
            jax.ShapeDtypeStruct((groups, blocks), jnp.int32),
        ),
        in_specs=[VMEM, HBM],
        out_specs=(HBM, VMEM),
        scratch_shapes=[
            pltpu.VMEM((blocks,) + tile, bf16),
            pltpu.VMEM((slots,) + tile, bf16),
            pltpu.SMEM((groups, blocks), jnp.int32),
            pltpu.SemaphoreType.DMA((2 + STORES,)),
        ],
        compiler_params=params(8),
        cost_estimate=pl.CostEstimate(flops=0, bytes_accessed=2 * slots * 4096, transcendentals=0),
    )(all_ids, in_hbm(probe_vecs))
    arrived = exchange(outgoing.reshape((groups, capacity) + tile)).reshape((slots,) + tile)
    part, slot_of = pl.pallas_call(
        functools.partial(near_forward_kernel, groups, capacity),
        name="near_forward",
        out_shape=(
            jax.ShapeDtypeStruct((blocks,) + tile, f32),
            jax.ShapeDtypeStruct((1, blocks), jnp.int32),
        ),
        in_specs=[SMEM, VMEM, VMEM, VMEM, HBM],
        out_specs=(VMEM, VMEM),
        scratch_shapes=[
            pltpu.VMEM((REACH + blocks,) + tile, bf16),
            pltpu.VMEM((blocks, 3, points, points), bf16),
            pltpu.SemaphoreType.DMA((chunks,)),
        ],
        compiler_params=params(24),
        cost_estimate=pl.CostEstimate(flops=3 * flops, bytes_accessed=14 * 2**20, transcendentals=0),
    )(ids, far_ids, halo, probe_vecs, in_hbm(coeffs))
    scaled, parcel = pl.pallas_call(
        far_kernel,
        name="far_and_scale",
        out_shape=(
            jax.ShapeDtypeStruct((blocks,) + tile, bf16),
            jax.ShapeDtypeStruct((slots,) + tile, bf16),
        ),
        in_specs=[SMEM, VMEM, VMEM, HBM, HBM],
        out_specs=(VMEM, VMEM),
        scratch_shapes=[
            pltpu.VMEM((blocks, points, points), bf16),
            pltpu.VMEM((blocks, points, points), bf16),
            pltpu.VMEM((blocks,) + tile, bf16),
            pltpu.SemaphoreType.DMA((2, chunks)),
        ],
        compiler_params=params(24),
        cost_estimate=pl.CostEstimate(flops=3 * flops, bytes_accessed=11 * 2**20, transcendentals=0),
    )(slot_of, part, arrived, in_hbm(coeffs), in_hbm(cond_prec))
    returned = exchange(parcel.reshape((groups, capacity) + tile)).reshape((slots,) + tile)
    base, halo_back = pl.pallas_call(
        functools.partial(near_back_kernel, groups),
        name="near_back",
        out_shape=(
            jax.ShapeDtypeStruct((blocks,) + tile, f32),
            jax.ShapeDtypeStruct((REACH,) + tile, bf16),
        ),
        in_specs=[SMEM, VMEM, HBM],
        out_specs=(VMEM, VMEM),
        scratch_shapes=[
            pltpu.VMEM((REACH + blocks,) + tile, f32),
            pltpu.VMEM((blocks, 3, points, points), bf16),
            pltpu.SemaphoreType.DMA((chunks,)),
        ],
        compiler_params=params(24),
        cost_estimate=pl.CostEstimate(flops=3 * flops, bytes_accessed=14 * 2**20, transcendentals=0),
    )(ids, scaled, in_hbm(coeffs))
    halo_sum = passed_along(halo_back, "blk", -1)
    return pl.pallas_call(
        functools.partial(sum_kernel, capacity),
        name="final_sum",
        out_shape=jax.ShapeDtypeStruct((blocks,) + tile, f32),
        in_specs=[SMEM, VMEM, VMEM, VMEM],
        out_specs=HBM,
        scratch_shapes=[pltpu.VMEM((blocks + 1,) + tile, f32), pltpu.SemaphoreType.DMA],
        compiler_params=params(8),
        cost_estimate=pl.CostEstimate(flops=0, bytes_accessed=3 * 2**20, transcendentals=0),
    )(picks, base, halo_sum, returned)


def solution(mesh):
    in_specs = (
        P("blk", None, None),
        P("blk", None, None, None),
        P("blk", None, None),
        P("blk", None),
    )
    return jax.shard_map(
        per_device, mesh=mesh, in_specs=in_specs, out_specs=P("blk", None, None), check_vma=False
    )
```

```python
import functools

import jax
import jax.numpy as jnp
from jax import lax
from jax.experimental import pallas as pl
from jax.experimental.pallas import tpu as pltpu
from jax.sharding import PartitionSpec as P

REACH = 16
CHUNK = 16
AHEAD = 4
STORES = 4
VMEM = pl.BlockSpec(memory_space=pltpu.VMEM)
SMEM = pl.BlockSpec(memory_space=pltpu.SMEM)
HBM = pl.BlockSpec(memory_space=pl.ANY)
NT = (((1,), (1,)), ((), ()))


def params(mib):
    return pltpu.CompilerParams(vmem_limit_bytes=mib * 2**20)


def in_hbm(x):
    return pltpu.with_memory_space_constraint(x, pltpu.HBM)


def passed_along(block, axis, distance):
    size = lax.axis_size(axis)
    return lax.ppermute(block, axis, [((i - distance) % size, i) for i in range(size)])


def earlier_matrix(blocks):
    row = lax.broadcasted_iota(jnp.int32, (blocks, blocks), 0)
    col = lax.broadcasted_iota(jnp.int32, (blocks, blocks), 1)
    return (row < col).astype(jnp.float32).astype(jnp.bfloat16)


def ranks_in(mask, blocks):
    chosen = mask.astype(jnp.float32).astype(jnp.bfloat16)
    return jnp.dot(chosen, earlier_matrix(blocks), preferred_element_type=jnp.float32).astype(jnp.int32)


def pick_kernel(capacity, ids_ref, probe_ref, out_ref, picks_ref, probe, out, picks_smem, sems):
    groups, blocks = ids_ref.shape
    load = pltpu.make_async_copy(probe_ref, probe, sems.at[0])
    load.start()
    me = lax.axis_index("blk")
    local = ids_ref[...] - me * blocks
    mask = (local >= 0) & (local < blocks)
    rank = ranks_in(mask, blocks)
    lane = lax.broadcasted_iota(jnp.int32, (groups, blocks), 1)
    picks = jnp.zeros((groups, blocks), jnp.int32)
    for r in range(capacity):
        found = jnp.sum(jnp.where(mask & (rank == r), local + 1, 0), axis=1, keepdims=True)
        picks = jnp.where(lane == r, found, picks)
    picks_ref[...] = picks
    copy = pltpu.make_async_copy(picks_ref, picks_smem, sems.at[1])
    copy.start()
    copy.wait()
    load.wait()
    part = groups // STORES

    def store(p):
        rows = pl.ds(p * part * capacity, part * capacity)
        return pltpu.make_async_copy(out.at[rows], out_ref.at[rows], sems.at[2 + p])

    for p in range(STORES):

        @pl.loop(p * part, (p + 1) * part, unroll=8)
        def _(g):
            for r in range(capacity):
                out[g * capacity + r] = probe[jnp.maximum(picks_smem[g, r] - 1, 0)]

        store(p).start()
    for p in range(STORES):
        store(p).wait()


def stacked(mats):
    return mats.reshape(-1, mats.shape[-1])


def apart(left0, left1, mats):
    zero = jnp.zeros_like(left0)
    left = jnp.concatenate(
        [jnp.concatenate([left0, zero], axis=1), jnp.concatenate([zero, left1], axis=1)], axis=0
    )
    out = jnp.dot(left, mats, preferred_element_type=jnp.float32)
    return out.reshape((2,) + (left0.shape[0], mats.shape[1]))


def apart_back(lefts, mats):
    rows, half = lefts.shape[1], mats.shape[0] // 2
    out = lax.dot_general(lefts.reshape(2 * rows, lefts.shape[2]), mats, NT, preferred_element_type=jnp.float32)
    return out[:rows, :half], out[rows:, half:]


def near_place(ids_ref, k, i, first, count):
    place = ids_ref[k, i] - first + REACH
    return jnp.where(place >= count, place - count, place)


def near_forward_kernel(
    groups, capacity, ids_ref, far_ref, halo_ref, probe_ref, coeffs_ref, out_ref, slot_ref, ext, coeffs, sems
):
    blocks = probe_ref.shape[0]
    chunks = blocks // CHUNK

    def load(c):
        own = pl.ds(c * CHUNK, CHUNK)
        return pltpu.make_async_copy(coeffs_ref.at[own, pl.ds(0, 3)], coeffs.at[own], sems.at[c])

    for c in range(chunks):
        load(c).start()
    ext[pl.ds(0, REACH)] = halo_ref[...]
    ext[pl.ds(REACH, blocks)] = probe_ref[...]
    owner = far_ref[...] // blocks
    mask = lax.broadcasted_iota(jnp.int32, (groups, blocks), 0) == owner
    rank = jnp.sum(jnp.where(mask, ranks_in(mask, blocks), 0), axis=0, keepdims=True)
    slot_ref[...] = owner * capacity + rank
    first = lax.axis_index("blk") * blocks

    @pl.loop(0, chunks)
    def _(c):
        load(c).wait()
        for b in range(0, CHUNK, 2):
            i = c * CHUNK + b
            rows = []
            for j in range(2):
                tiles = [ext[near_place(ids_ref, k, i + j, first, groups * blocks)] for k in range(3)]
                rows.append(jnp.concatenate(tiles, axis=1))
            mixed = apart(rows[0], rows[1], stacked(coeffs[pl.ds(i, 2)]))
            out_ref[pl.ds(i, 2)] = probe_ref[pl.ds(i, 2)].astype(jnp.float32) - mixed


def far_kernel(slot_ref, part_ref, far_ref, coeffs_ref, prec_ref, scaled_ref, parcel_ref, coeffs, prec, white, sems):
    blocks = part_ref.shape[0]
    chunks = blocks // CHUNK

    def loads(c):
        own = pl.ds(c * CHUNK, CHUNK)
        return (
            pltpu.make_async_copy(coeffs_ref.at[own, 3], coeffs.at[own], sems.at[0, c]),
            pltpu.make_async_copy(prec_ref.at[own], prec.at[own], sems.at[1, c]),
        )

    for c in range(chunks):
        for load in loads(c):
            load.start()
    parcel_ref[...] = jnp.zeros_like(parcel_ref)

    def mix(c):
        for b in range(0, CHUNK, 2):
            i = c * CHUNK + b
            mixed = apart(far_ref[slot_ref[0, i]], far_ref[slot_ref[0, i + 1]], stacked(coeffs[pl.ds(i, 2)]))
            white[pl.ds(i, 2)] = (part_ref[pl.ds(i, 2)] - mixed).astype(jnp.bfloat16)

    def scale(c):
        for b in range(0, CHUNK, 2):
            i = c * CHUNK + b
            scaled_ref[pl.ds(i, 2)] = apart(white[i], white[i + 1], stacked(prec[pl.ds(i, 2)])).astype(jnp.bfloat16)

    def back(c):
        for b in range(0, CHUNK, 2):
            i = c * CHUNK + b
            terms = apart_back(scaled_ref[pl.ds(i, 2)], stacked(coeffs[pl.ds(i, 2)]))
            for j in range(2):
                parcel_ref[slot_ref[0, i + j]] = terms[j].astype(jnp.bfloat16)

    def ready(c):
        for load in loads(c):
            load.wait()

    ready(0)
    mix(0)
    ready(1)
    scale(0)
    mix(1)

    @pl.loop(2, chunks)
    def _(c):
        ready(c)
        back(c - 2)
        scale(c - 1)
        mix(c)

    back(chunks - 2)
    scale(chunks - 1)
    back(chunks - 1)


def near_back_kernel(groups, ids_ref, scaled_ref, coeffs_ref, base_ref, halo_ref, total, coeffs, sems):
    blocks = scaled_ref.shape[0]
    points = scaled_ref.shape[2]
    chunks = blocks // CHUNK

    def load(c):
        own = pl.ds(c * CHUNK, CHUNK)
        return pltpu.make_async_copy(coeffs_ref.at[own, pl.ds(0, 3)], coeffs.at[own], sems.at[c])

    for c in range(chunks):
        load(c).start()
    total[pl.ds(0, REACH)] = jnp.zeros((REACH,) + total.shape[1:], jnp.float32)
    total[pl.ds(REACH, blocks)] = scaled_ref[...].astype(jnp.float32)
    first = lax.axis_index("blk") * blocks

    @pl.loop(0, chunks)
    def _(c):
        load(c).wait()
        terms = []
        for b in range(CHUNK + AHEAD):
            if b < CHUNK and b % 2 == 0:
                i = c * CHUNK + b
                terms.extend(apart_back(scaled_ref[pl.ds(i, 2)], stacked(coeffs[pl.ds(i, 2)])))
            if b >= AHEAD:
                i = c * CHUNK + b - AHEAD
                places = [near_place(ids_ref, k, i, first, groups * blocks) for k in range(3)]
                olds = [total[place] for place in places]
                for k in range(3):
                    total[places[k]] = olds[k] - terms[b - AHEAD][:, k * points : (k + 1) * points]

    halo_ref[...] = total[pl.ds(0, REACH)].astype(halo_ref.dtype)
    base_ref[...] = total[pl.ds(REACH, blocks)]


def sum_kernel(capacity, picks_ref, base_ref, halo_ref, back_ref, out_ref, total, sem):
    groups = picks_ref.shape[0]
    blocks = base_ref.shape[0]
    total[pl.ds(0, blocks)] = base_ref[...]
    last = pl.ds(blocks - REACH, REACH)
    total[last] = total[last] + halo_ref[...].astype(jnp.float32)

    @pl.loop(0, groups, unroll=8)
    def _(g):
        picks = [picks_ref[g, r] for r in range(capacity)]
        places = [jnp.where(pick > 0, pick - 1, blocks) for pick in picks]
        olds = [total[place] for place in places]
        for r in range(capacity):
            total[places[r]] = olds[r] - back_ref[g * capacity + r].astype(jnp.float32)

    store = pltpu.make_async_copy(total.at[pl.ds(0, blocks)], out_ref, sem)
    store.start()
    store.wait()


def per_device(probe_vecs, coeffs, cond_prec, neighbours):
    blocks, probes, points = probe_vecs.shape
    groups = lax.axis_size("blk")
    capacity = max(2, blocks // (groups - 1) + 1)
    slots = groups * capacity
    chunks = blocks // CHUNK
    bf16, f32 = jnp.bfloat16, jnp.float32
    tile = (probes, points)
    flops = 2 * blocks * probes * points * points

    def exchange(x):
        return lax.all_to_all(x, "blk", split_axis=0, concat_axis=0, tiled=True)

    ids = neighbours.T
    far_ids = ids[3:]
    halo = passed_along(probe_vecs[blocks - REACH :], "blk", 1)
    all_ids = exchange(jnp.broadcast_to(far_ids, (groups, blocks)))
    all_ids, halo = lax.optimization_barrier((all_ids, halo))
    outgoing, picks = pl.pallas_call(
        functools.partial(pick_kernel, capacity),
        name="pick_tiles",
        out_shape=(
            jax.ShapeDtypeStruct((slots,) + tile, bf16),
            jax.ShapeDtypeStruct((groups, blocks), jnp.int32),
        ),
        in_specs=[VMEM, HBM],
        out_specs=(HBM, VMEM),
        scratch_shapes=[
            pltpu.VMEM((blocks,) + tile, bf16),
            pltpu.VMEM((slots,) + tile, bf16),
            pltpu.SMEM((groups, blocks), jnp.int32),
            pltpu.SemaphoreType.DMA((2 + STORES,)),
        ],
        compiler_params=params(8),
        cost_estimate=pl.CostEstimate(flops=0, bytes_accessed=2 * slots * 4096, transcendentals=0),
    )(all_ids, in_hbm(probe_vecs))
    arrived = exchange(outgoing.reshape((groups, capacity) + tile)).reshape((slots,) + tile)
    part, slot_of = pl.pallas_call(
        functools.partial(near_forward_kernel, groups, capacity),
        name="near_forward",
        out_shape=(
            jax.ShapeDtypeStruct((blocks,) + tile, f32),
            jax.ShapeDtypeStruct((1, blocks), jnp.int32),
        ),
        in_specs=[SMEM, VMEM, VMEM, VMEM, HBM],
        out_specs=(VMEM, VMEM),
        scratch_shapes=[
            pltpu.VMEM((REACH + blocks,) + tile, bf16),
            pltpu.VMEM((blocks, 3, points, points), bf16),
            pltpu.SemaphoreType.DMA((chunks,)),
        ],
        compiler_params=params(24),
        cost_estimate=pl.CostEstimate(flops=3 * flops, bytes_accessed=14 * 2**20, transcendentals=0),
    )(ids, far_ids, halo, probe_vecs, in_hbm(coeffs))
    scaled, parcel = pl.pallas_call(
        far_kernel,
        name="far_and_scale",
        out_shape=(
            jax.ShapeDtypeStruct((blocks,) + tile, bf16),
            jax.ShapeDtypeStruct((slots,) + tile, bf16),
        ),
        in_specs=[SMEM, VMEM, VMEM, HBM, HBM],
        out_specs=(VMEM, VMEM),
        scratch_shapes=[
            pltpu.VMEM((blocks, points, points), bf16),
            pltpu.VMEM((blocks, points, points), bf16),
            pltpu.VMEM((blocks,) + tile, bf16),
            pltpu.SemaphoreType.DMA((2, chunks)),
        ],
        compiler_params=params(24),
        cost_estimate=pl.CostEstimate(flops=3 * flops, bytes_accessed=11 * 2**20, transcendentals=0),
    )(slot_of, part, arrived, in_hbm(coeffs), in_hbm(cond_prec))
    returned = exchange(parcel.reshape((groups, capacity) + tile)).reshape((slots,) + tile)
    base, halo_back = pl.pallas_call(
        functools.partial(near_back_kernel, groups),
        name="near_back",
        out_shape=(
            jax.ShapeDtypeStruct((blocks,) + tile, f32),
            jax.ShapeDtypeStruct((REACH,) + tile, bf16),
        ),
        in_specs=[SMEM, VMEM, HBM],
        out_specs=(VMEM, VMEM),
        scratch_shapes=[
            pltpu.VMEM((REACH + blocks,) + tile, f32),
            pltpu.VMEM((blocks, 3, points, points), bf16),
            pltpu.SemaphoreType.DMA((chunks,)),
        ],
        compiler_params=params(24),
        cost_estimate=pl.CostEstimate(flops=3 * flops, bytes_accessed=14 * 2**20, transcendentals=0),
    )(ids, scaled, in_hbm(coeffs))
    halo_sum = passed_along(halo_back, "blk", -1)
    return pl.pallas_call(
        functools.partial(sum_kernel, capacity),
        name="final_sum",
        out_shape=jax.ShapeDtypeStruct((blocks,) + tile, f32),
        in_specs=[SMEM, VMEM, VMEM, VMEM],
        out_specs=HBM,
        scratch_shapes=[pltpu.VMEM((blocks + 1,) + tile, f32), pltpu.SemaphoreType.DMA],
        compiler_params=params(8),
        cost_estimate=pl.CostEstimate(flops=0, bytes_accessed=3 * 2**20, transcendentals=0),
    )(picks, base, halo_sum, returned)


def solution(mesh):
    in_specs = (
        P("blk", None, None),
        P("blk", None, None, None),
        P("blk", None, None),
        P("blk", None),
    )
    return jax.shard_map(
        per_device, mesh=mesh, in_specs=in_specs, out_specs=P("blk", None, None), check_vma=False
    )
```

```python
import functools

import jax
import jax.numpy as jnp
from jax import lax
from jax.experimental import pallas as pl
from jax.experimental.pallas import tpu as pltpu
from jax.sharding import PartitionSpec as P

REACH = 16
CHUNK = 16
AHEAD = 4
VMEM = pl.BlockSpec(memory_space=pltpu.VMEM)
SMEM = pl.BlockSpec(memory_space=pltpu.SMEM)
HBM = pl.BlockSpec(memory_space=pl.ANY)
NT = (((1,), (1,)), ((), ()))


def params(mib):
    return pltpu.CompilerParams(vmem_limit_bytes=mib * 2**20)


def in_hbm(x):
    return pltpu.with_memory_space_constraint(x, pltpu.HBM)


def passed_along(block, axis, distance):
    size = lax.axis_size(axis)
    return lax.ppermute(block, axis, [((i - distance) % size, i) for i in range(size)])


def earlier_matrix(blocks):
    row = lax.broadcasted_iota(jnp.int32, (blocks, blocks), 0)
    col = lax.broadcasted_iota(jnp.int32, (blocks, blocks), 1)
    return (row < col).astype(jnp.float32).astype(jnp.bfloat16)


def ranks_in(mask, blocks):
    chosen = mask.astype(jnp.float32).astype(jnp.bfloat16)
    return jnp.dot(chosen, earlier_matrix(blocks), preferred_element_type=jnp.float32).astype(jnp.int32)


def pick_kernel(shares, ids_ref, probe_ref, *refs):
    out_refs, picks_ref, probe, outs = refs[:2], refs[2], refs[3], refs[4:6]
    picks_smem, sems = refs[6:]
    groups, blocks = ids_ref.shape
    load = pltpu.make_async_copy(probe_ref, probe, sems.at[0])
    load.start()
    me = lax.axis_index("blk")
    local = ids_ref[...] - me * blocks
    mask = (local >= 0) & (local < blocks)
    rank = ranks_in(mask, blocks)
    lane = lax.broadcasted_iota(jnp.int32, (groups, blocks), 1)
    picks = jnp.zeros((groups, blocks), jnp.int32)
    for r in range(sum(shares)):
        found = jnp.sum(jnp.where(mask & (rank == r), local + 1, 0), axis=1, keepdims=True)
        picks = jnp.where(lane == r, found, picks)
    picks_ref[...] = picks
    copy = pltpu.make_async_copy(picks_ref, picks_smem, sems.at[1])
    copy.start()
    copy.wait()
    load.wait()

    def store(p):
        return pltpu.make_async_copy(outs[p], out_refs[p], sems.at[2 + p])

    for p, share in enumerate(shares):

        @pl.loop(0, groups, unroll=8)
        def _(g):
            for r in range(share):
                pick = picks_smem[g, sum(shares[:p]) + r]
                outs[p][g * share + r] = probe[jnp.maximum(pick - 1, 0)]

        store(p).start()
    for p in range(2):
        store(p).wait()


def stacked(mats):
    return mats.reshape(-1, mats.shape[-1])


def apart(left0, left1, mats):
    zero = jnp.zeros_like(left0)
    left = jnp.concatenate(
        [jnp.concatenate([left0, zero], axis=1), jnp.concatenate([zero, left1], axis=1)], axis=0
    )
    out = jnp.dot(left, mats, preferred_element_type=jnp.float32)
    return out.reshape((2,) + (left0.shape[0], mats.shape[1]))


def apart_back(lefts, mats):
    rows, half = lefts.shape[1], mats.shape[0] // 2
    out = lax.dot_general(lefts.reshape(2 * rows, lefts.shape[2]), mats, NT, preferred_element_type=jnp.float32)
    return out[:rows, :half], out[rows:, half:]


def near_place(ids_ref, k, i, first, count):
    place = ids_ref[k, i] - first + REACH
    return jnp.where(place >= count, place - count, place)


def near_forward_kernel(
    groups, shares, ids_ref, halo_ref, probe_ref, coeffs_ref, out_ref, slot_ref, block_ref, counts, ext, coeffs, sems
):
    blocks = probe_ref.shape[0]
    chunks = blocks // CHUNK

    def load(c):
        own = pl.ds(c * CHUNK, CHUNK)
        return pltpu.make_async_copy(coeffs_ref.at[own, pl.ds(0, 3)], coeffs.at[own], sems.at[c])

    for c in range(chunks):
        load(c).start()
    ext[pl.ds(0, REACH)] = halo_ref[...]
    ext[pl.ds(REACH, blocks)] = probe_ref[...]

    @pl.loop(0, groups, unroll=8)
    def _(g):
        counts[g] = 0

    @pl.loop(0, groups * sum(shares), unroll=8)
    def _(s):
        block_ref[0, s] = 0

    @pl.loop(0, blocks, unroll=4)
    def _(i):
        owner = lax.div(ids_ref[3, i], blocks)
        rank = counts[owner]
        counts[owner] = rank + 1
        late = groups * shares[0] + owner * shares[1] + rank - shares[0]
        slot = jnp.where(rank < shares[0], owner * shares[0] + rank, late)
        slot_ref[0, i] = slot
        block_ref[0, slot] = i

    first = lax.axis_index("blk") * blocks

    @pl.loop(0, chunks)
    def _(c):
        load(c).wait()
        for b in range(0, CHUNK, 2):
            i = c * CHUNK + b
            rows = []
            for j in range(2):
                tiles = [ext[near_place(ids_ref, k, i + j, first, groups * blocks)] for k in range(3)]
                rows.append(jnp.concatenate(tiles, axis=1))
            mixed = apart(rows[0], rows[1], stacked(coeffs[pl.ds(i, 2)]))
            out_ref[pl.ds(i, 2)] = probe_ref[pl.ds(i, 2)].astype(jnp.float32) - mixed


def far_kernel(start, block_ref, part_ref, far_ref, coeffs_ref, prec_ref, scaled_ref, parcel_ref, coeffs, prec, white, sems):
    chunks = far_ref.shape[0] // CHUNK

    def fetch(c):
        for b in range(CHUNK):
            s = c * CHUNK + b
            i = block_ref[0, start + s]
            pltpu.make_async_copy(coeffs_ref.at[i, 3], coeffs.at[s], sems.at[0, c]).start()
            pltpu.make_async_copy(prec_ref.at[i], prec.at[s], sems.at[1, c]).start()

    def ready(c):
        own = pl.ds(c * CHUNK, CHUNK)
        pltpu.make_async_copy(prec_ref.at[pl.ds(0, CHUNK)], coeffs.at[own], sems.at[0, c]).wait()
        pltpu.make_async_copy(prec_ref.at[pl.ds(0, CHUNK)], prec.at[own], sems.at[1, c]).wait()

    def mix(c):
        for b in range(0, CHUNK, 2):
            s = c * CHUNK + b
            mixed = apart(far_ref[s], far_ref[s + 1], stacked(coeffs[pl.ds(s, 2)]))
            for j in range(2):
                white[s + j] = (part_ref[block_ref[0, start + s + j]] - mixed[j]).astype(jnp.bfloat16)

    def scale(c):
        for b in range(0, CHUNK, 2):
            s = c * CHUNK + b
            scaled_ref[pl.ds(s, 2)] = apart(white[s], white[s + 1], stacked(prec[pl.ds(s, 2)])).astype(jnp.bfloat16)

    def back(c):
        for b in range(0, CHUNK, 2):
            s = c * CHUNK + b
            terms = apart_back(scaled_ref[pl.ds(s, 2)], stacked(coeffs[pl.ds(s, 2)]))
            for j in range(2):
                parcel_ref[s + j] = terms[j].astype(jnp.bfloat16)

    @pl.loop(0, min(3, chunks))
    def _(c):
        fetch(c)

    ready(0)
    mix(0)
    ready(1)
    scale(0)
    mix(1)

    @pl.loop(2, chunks)
    def _(c):
        @pl.when(c + 1 < chunks)
        def _():
            fetch(c + 1)

        ready(c)
        back(c - 2)
        scale(c - 1)
        mix(c)

    back(chunks - 2)
    scale(chunks - 1)
    back(chunks - 1)


def near_back_kernel(
    groups, ids_ref, slot_ref, early_ref, late_ref, coeffs_ref, base_ref, halo_ref, total, scaled, coeffs, sems
):
    blocks = base_ref.shape[0]
    points = base_ref.shape[2]
    early = early_ref.shape[0]
    chunks = blocks // CHUNK

    def load(c):
        own = pl.ds(c * CHUNK, CHUNK)
        return pltpu.make_async_copy(coeffs_ref.at[own, pl.ds(0, 3)], coeffs.at[own], sems.at[c])

    for c in range(chunks):
        load(c).start()
    scaled[pl.ds(0, early)] = early_ref[...]
    scaled[pl.ds(early, late_ref.shape[0])] = late_ref[...]
    total[pl.ds(0, REACH)] = jnp.zeros((REACH,) + total.shape[1:], jnp.float32)

    @pl.loop(0, blocks, unroll=8)
    def _(i):
        total[REACH + i] = scaled[slot_ref[0, i]].astype(jnp.float32)

    first = lax.axis_index("blk") * blocks

    @pl.loop(0, chunks)
    def _(c):
        load(c).wait()
        terms = []
        for b in range(CHUNK + AHEAD):
            if b < CHUNK and b % 2 == 0:
                i = c * CHUNK + b
                pair = jnp.concatenate([scaled[slot_ref[0, i]][None], scaled[slot_ref[0, i + 1]][None]], axis=0)
                terms.extend(apart_back(pair, stacked(coeffs[pl.ds(i, 2)])))
            if b >= AHEAD:
                i = c * CHUNK + b - AHEAD
                places = [near_place(ids_ref, k, i, first, groups * blocks) for k in range(3)]
                olds = [total[place] for place in places]
                for k in range(3):
                    total[places[k]] = olds[k] - terms[b - AHEAD][:, k * points : (k + 1) * points]

    halo_ref[...] = total[pl.ds(0, REACH)].astype(halo_ref.dtype)
    base_ref[...] = total[pl.ds(REACH, blocks)]


def subtract_far(column, share, picks_ref, back_ref, total):
    groups = picks_ref.shape[0]
    empty = total.shape[0] - 1

    @pl.loop(0, groups, unroll=8)
    def _(g):
        picks = [picks_ref[g, column + r] for r in range(share)]
        places = [jnp.where(pick > 0, pick - 1, empty) for pick in picks]
        olds = [total[place] for place in places]
        for r in range(share):
            total[places[r]] = olds[r] - back_ref[g * share + r].astype(jnp.float32)


def early_sum_kernel(shares, picks_ref, base_ref, halo_ref, back_ref, out_ref, total):
    blocks = base_ref.shape[0]
    total[pl.ds(0, blocks)] = base_ref[...]
    last = pl.ds(blocks - REACH, REACH)
    total[last] = total[last] + halo_ref[...].astype(jnp.float32)
    subtract_far(0, shares[0], picks_ref, back_ref, total)
    out_ref[...] = total[pl.ds(0, blocks)]


def late_sum_kernel(shares, picks_ref, base_ref, back_ref, out_ref, total, sem):
    blocks = base_ref.shape[0]
    total[pl.ds(0, blocks)] = base_ref[...]
    subtract_far(shares[0], shares[1], picks_ref, back_ref, total)
    store = pltpu.make_async_copy(total.at[pl.ds(0, blocks)], out_ref, sem)
    store.start()
    store.wait()


def per_device(probe_vecs, coeffs, cond_prec, neighbours):
    blocks, probes, points = probe_vecs.shape
    groups = lax.axis_size("blk")
    capacity = max(2, blocks // (groups - 1) + 1)
    shares = ((capacity + 1) // 2, capacity // 2)
    slots = groups * capacity
    chunks = blocks // CHUNK
    bf16, f32, i32 = jnp.bfloat16, jnp.float32, jnp.int32
    tile = (probes, points)
    flops = 2 * blocks * probes * points * points

    def array(rows, kind):
        return jax.ShapeDtypeStruct((rows,) + tile, kind)

    def cost(flops, mib):
        return pl.CostEstimate(flops=flops, bytes_accessed=mib * 2**20, transcendentals=0)

    def exchange(x):
        return lax.all_to_all(x, "blk", split_axis=0, concat_axis=0, tiled=True)

    def exchange_tiles(x):
        return exchange(x.reshape((groups, -1) + tile)).reshape((-1,) + tile)

    ids = neighbours.T
    halo = passed_along(probe_vecs[blocks - REACH :], "blk", 1)
    all_ids = exchange(jnp.broadcast_to(ids[3:], (groups, blocks)))
    all_ids, halo = lax.optimization_barrier((all_ids, halo))
    *outgoing, picks = pl.pallas_call(
        functools.partial(pick_kernel, shares),
        name="pick_tiles",
        out_shape=[array(groups * share, bf16) for share in shares] + [jax.ShapeDtypeStruct((groups, blocks), i32)],
        in_specs=[VMEM, HBM],
        out_specs=[HBM, HBM, VMEM],
        scratch_shapes=[
            pltpu.VMEM((blocks,) + tile, bf16),
            pltpu.VMEM((groups * shares[0],) + tile, bf16),
            pltpu.VMEM((groups * shares[1],) + tile, bf16),
            pltpu.SMEM((groups, blocks), i32),
            pltpu.SemaphoreType.DMA((4,)),
        ],
        compiler_params=params(8),
        cost_estimate=cost(0, 1),
    )(all_ids, in_hbm(probe_vecs))
    arrived = [exchange_tiles(x) for x in outgoing]
    part, slot_of, block_of = pl.pallas_call(
        functools.partial(near_forward_kernel, groups, shares),
        name="near_forward",
        out_shape=(
            array(blocks, f32),
            jax.ShapeDtypeStruct((1, blocks), i32),
            jax.ShapeDtypeStruct((1, slots), i32),
        ),
        in_specs=[SMEM, VMEM, VMEM, HBM],
        out_specs=(VMEM, SMEM, SMEM),
        scratch_shapes=[
            pltpu.SMEM((groups,), i32),
            pltpu.VMEM((REACH + blocks,) + tile, bf16),
            pltpu.VMEM((blocks, 3, points, points), bf16),
            pltpu.SemaphoreType.DMA((chunks,)),
        ],
        compiler_params=params(24),
        cost_estimate=cost(3 * flops, 14),
    )(ids, halo, probe_vecs, in_hbm(coeffs))

    scaled, returned = [], []
    for p, share in enumerate(shares):
        count = groups * share
        mats = pltpu.VMEM((count, points, points), bf16)
        if scaled:
            arrived[p], scaled[0] = lax.optimization_barrier((arrived[p], scaled[0]))
        scaled_part, parcel = pl.pallas_call(
            functools.partial(far_kernel, p * groups * shares[0]),
            name=("far_early", "far_late")[p],
            out_shape=(array(count, bf16), array(count, bf16)),
            in_specs=[SMEM, VMEM, VMEM, HBM, HBM],
            out_specs=(VMEM, VMEM),
            scratch_shapes=[
                mats,
                mats,
                pltpu.VMEM((count,) + tile, bf16),
                pltpu.SemaphoreType.DMA((2, count // CHUNK)),
            ],
            compiler_params=params(24),
            cost_estimate=cost(2 * flops, 6),
        )(block_of, part, arrived[p], in_hbm(coeffs), in_hbm(cond_prec))
        scaled.append(scaled_part)
        returned.append(exchange_tiles(parcel))
    base, halo_back = pl.pallas_call(
        functools.partial(near_back_kernel, groups),
        name="near_back",
        out_shape=(array(blocks, f32), array(REACH, bf16)),
        in_specs=[SMEM, SMEM, VMEM, VMEM, HBM],
        out_specs=(VMEM, VMEM),
        scratch_shapes=[
            pltpu.VMEM((REACH + blocks,) + tile, f32),
            pltpu.VMEM((slots,) + tile, bf16),
            pltpu.VMEM((blocks, 3, points, points), bf16),
            pltpu.SemaphoreType.DMA((chunks,)),
        ],
        compiler_params=params(24),
        cost_estimate=cost(3 * flops, 14),
    )(ids, slot_of, *scaled, in_hbm(coeffs))
    halo_sum = passed_along(halo_back, "blk", -1)
    base = pl.pallas_call(
        functools.partial(early_sum_kernel, shares),
        name="early_sum",
        out_shape=array(blocks, f32),
        in_specs=[SMEM, VMEM, VMEM, VMEM],
        out_specs=VMEM,
        scratch_shapes=[pltpu.VMEM((blocks + 1,) + tile, f32)],
        compiler_params=params(8),
        cost_estimate=cost(0, 2),
    )(picks, base, halo_sum, returned[0])
    return pl.pallas_call(
        functools.partial(late_sum_kernel, shares),
        name="late_sum",
        out_shape=array(blocks, f32),
        in_specs=[SMEM, VMEM, VMEM],
        out_specs=HBM,
        scratch_shapes=[pltpu.VMEM((blocks + 1,) + tile, f32), pltpu.SemaphoreType.DMA],
        compiler_params=params(8),
        cost_estimate=cost(0, 2),
    )(picks, base, returned[1])


def solution(mesh):
    in_specs = (
        P("blk", None, None),
        P("blk", None, None, None),
        P("blk", None, None),
        P("blk", None),
    )
    return jax.shard_map(
        per_device, mesh=mesh, in_specs=in_specs, out_specs=P("blk", None, None), check_vma=False
    )
```

```python
import functools

import jax
import jax.numpy as jnp
from jax import lax
from jax.experimental import pallas as pl
from jax.experimental.pallas import tpu as pltpu
from jax.sharding import PartitionSpec as P

REACH = 16
CHUNK = 16
AHEAD = 4
STORES = 4
VMEM = pl.BlockSpec(memory_space=pltpu.VMEM)
SMEM = pl.BlockSpec(memory_space=pltpu.SMEM)
HBM = pl.BlockSpec(memory_space=pl.ANY)
NT = (((1,), (1,)), ((), ()))


def params(mib):
    return pltpu.CompilerParams(vmem_limit_bytes=mib * 2**20)


def in_hbm(x):
    return pltpu.with_memory_space_constraint(x, pltpu.HBM)


def passed_along(block, axis, distance):
    size = lax.axis_size(axis)
    return lax.ppermute(block, axis, [((i - distance) % size, i) for i in range(size)])


def turned(device, groups):
    bits = groups.bit_length() - 1
    if groups != 1 << bits:
        return device
    place = device * 0
    for bit in range(bits):
        place = place + ((device >> bit) & 1) * (1 << (bits - 1 - bit))
    return place


def earlier_matrix(blocks):
    row = lax.broadcasted_iota(jnp.int32, (blocks, blocks), 0)
    col = lax.broadcasted_iota(jnp.int32, (blocks, blocks), 1)
    return (row < col).astype(jnp.float32).astype(jnp.bfloat16)


def ranks_in(mask, blocks):
    chosen = mask.astype(jnp.float32).astype(jnp.bfloat16)
    return jnp.dot(chosen, earlier_matrix(blocks), preferred_element_type=jnp.float32).astype(jnp.int32)


def pick_kernel(capacity, ids_ref, probe_ref, out_ref, picks_ref, tail_ref, probe, out, picks_smem, sems):
    groups, blocks = ids_ref.shape
    load = pltpu.make_async_copy(probe_ref, probe, sems.at[0])
    load.start()
    me = lax.axis_index("blk")
    local = ids_ref[...] - me * blocks
    mask = (local >= 0) & (local < blocks)
    rank = ranks_in(mask, blocks)
    lane = lax.broadcasted_iota(jnp.int32, (groups, blocks), 1)
    picks = jnp.zeros((groups, blocks), jnp.int32)
    for r in range(capacity):
        found = jnp.sum(jnp.where(mask & (rank == r), local + 1, 0), axis=1, keepdims=True)
        picks = jnp.where(lane == r, found, picks)
    picks_ref[...] = picks
    copy = pltpu.make_async_copy(picks_ref, picks_smem, sems.at[1])
    copy.start()
    copy.wait()
    load.wait()
    part = groups // STORES

    def store(p):
        rows = pl.ds(p * part * capacity, part * capacity)
        return pltpu.make_async_copy(out.at[rows], out_ref.at[rows], sems.at[2 + p])

    for p in range(STORES):

        @pl.loop(p * part, (p + 1) * part, unroll=8)
        def _(g):
            for r in range(capacity):
                out[g * capacity + r] = probe[jnp.maximum(picks_smem[g, r] - 1, 0)]

        store(p).start()
    tail_ref[...] = probe[pl.ds(blocks - REACH, REACH)]
    for p in range(STORES):
        store(p).wait()


def stacked(mats):
    return mats.reshape(-1, mats.shape[-1])


def apart(left0, left1, mats):
    zero = jnp.zeros_like(left0)
    left = jnp.concatenate(
        [jnp.concatenate([left0, zero], axis=1), jnp.concatenate([zero, left1], axis=1)], axis=0
    )
    out = jnp.dot(left, mats, preferred_element_type=jnp.float32)
    return out.reshape((2,) + (left0.shape[0], mats.shape[1]))


def apart_back(lefts, mats):
    rows, half = lefts.shape[1], mats.shape[0] // 2
    out = lax.dot_general(lefts.reshape(2 * rows, lefts.shape[2]), mats, NT, preferred_element_type=jnp.float32)
    return out[:rows, :half], out[rows:, half:]


def near_place(ids_ref, k, i, first, count):
    place = ids_ref[k, i] - first + REACH
    return jnp.where(place >= count, place - count, place)


def near_mix(ids_ref, tiles, coeffs, i, at, first, count, shift):
    rows = []
    for j in range(2):
        places = [near_place(ids_ref, k, i + j, first, count) - shift for k in range(3)]
        rows.append(jnp.concatenate([tiles[place] for place in places], axis=1))
    return apart(rows[0], rows[1], stacked(coeffs[pl.ds(at, 2)]))


def near_forward_kernel(
    groups, capacity, ids_ref, far_ref, probe_ref, coeffs_ref, out_ref, slot_ref, coeffs, sems
):
    blocks = probe_ref.shape[0]
    chunks = blocks // CHUNK

    def load(c):
        own = pl.ds(c * CHUNK, CHUNK)
        return pltpu.make_async_copy(coeffs_ref.at[own, pl.ds(0, 3)], coeffs.at[own], sems.at[c])

    for c in range(1, chunks):
        load(c).start()
    owner = far_ref[...] // blocks
    mask = lax.broadcasted_iota(jnp.int32, (groups, blocks), 0) == owner
    rank = jnp.sum(jnp.where(mask, ranks_in(mask, blocks), 0), axis=0, keepdims=True)
    slot_ref[...] = turned(owner, groups) * capacity + rank
    first = lax.axis_index("blk") * blocks
    out_ref[pl.ds(0, REACH)] = probe_ref[pl.ds(0, REACH)].astype(jnp.float32)

    @pl.loop(1, chunks)
    def _(c):
        load(c).wait()
        for b in range(0, CHUNK, 2):
            i = c * CHUNK + b
            mixed = near_mix(ids_ref, probe_ref, coeffs, i, i, first, groups * blocks, REACH)
            out_ref[pl.ds(i, 2)] = probe_ref[pl.ds(i, 2)].astype(jnp.float32) - mixed


def far_kernel(
    groups, ids_ref, slot_ref, part_ref, far_ref, halo_ref, probe_ref, coeffs_ref, prec_ref,
    scaled_ref, parcel_ref, coeffs, prec, white, near, head, sems
):
    blocks = part_ref.shape[0]
    chunks = blocks // CHUNK
    order = list(range(1, chunks)) + [0]

    def loads(c):
        own = pl.ds(c * CHUNK, CHUNK)
        return (
            pltpu.make_async_copy(coeffs_ref.at[own, 3], coeffs.at[own], sems.at[0, c]),
            pltpu.make_async_copy(prec_ref.at[own], prec.at[own], sems.at[1, c]),
        )

    own_head = pltpu.make_async_copy(probe_ref.at[pl.ds(0, REACH)], head.at[pl.ds(REACH, REACH)], sems.at[2, 0])
    near_load = pltpu.make_async_copy(coeffs_ref.at[pl.ds(0, REACH), pl.ds(0, 3)], near, sems.at[2, 1])
    for c in order:
        for load in loads(c):
            load.start()
    own_head.start()
    near_load.start()
    head[pl.ds(0, REACH)] = halo_ref[...]
    parcel_ref[...] = jnp.zeros_like(parcel_ref)

    def mix(c, first_chunk=False):
        for b in range(0, CHUNK, 2):
            i = c * CHUNK + b
            mixed = apart(far_ref[slot_ref[0, i]], far_ref[slot_ref[0, i + 1]], stacked(coeffs[pl.ds(i, 2)]))
            if first_chunk:
                first = lax.axis_index("blk") * blocks
                mixed = mixed + near_mix(ids_ref, head, near, i, i, first, groups * blocks, 0)
            white[pl.ds(i, 2)] = (part_ref[pl.ds(i, 2)] - mixed).astype(jnp.bfloat16)

    def scale(c):
        for b in range(0, CHUNK, 2):
            i = c * CHUNK + b
            scaled_ref[pl.ds(i, 2)] = apart(white[i], white[i + 1], stacked(prec[pl.ds(i, 2)])).astype(jnp.bfloat16)

    def back(c):
        for b in range(0, CHUNK, 2):
            i = c * CHUNK + b
            terms = apart_back(scaled_ref[pl.ds(i, 2)], stacked(coeffs[pl.ds(i, 2)]))
            for j in range(2):
                parcel_ref[slot_ref[0, i + j]] = terms[j].astype(jnp.bfloat16)

    def ready(c):
        for load in loads(c):
            load.wait()

    ready(1)
    mix(1)
    ready(2)
    scale(1)
    mix(2)

    @pl.loop(3, chunks)
    def _(c):
        ready(c)
        back(c - 2)
        scale(c - 1)
        mix(c)

    ready(0)
    own_head.wait()
    near_load.wait()
    back(chunks - 2)
    scale(chunks - 1)
    mix(0, True)
    back(chunks - 1)
    scale(0)
    back(0)


def near_back_kernel(groups, ids_ref, scaled_ref, coeffs_ref, base_ref, halo_ref, total, coeffs, sems):
    blocks = scaled_ref.shape[0]
    points = scaled_ref.shape[2]
    chunks = blocks // CHUNK

    def load(c):
        own = pl.ds(c * CHUNK, CHUNK)
        return pltpu.make_async_copy(coeffs_ref.at[own, pl.ds(0, 3)], coeffs.at[own], sems.at[c])

    for c in range(chunks):
        load(c).start()
    total[pl.ds(0, REACH)] = jnp.zeros((REACH,) + total.shape[1:], jnp.float32)
    total[pl.ds(REACH, blocks)] = scaled_ref[...].astype(jnp.float32)
    first = lax.axis_index("blk") * blocks

    @pl.loop(0, chunks)
    def _(c):
        load(c).wait()
        terms = []
        for b in range(CHUNK + AHEAD):
            if b < CHUNK and b % 2 == 0:
                i = c * CHUNK + b
                terms.extend(apart_back(scaled_ref[pl.ds(i, 2)], stacked(coeffs[pl.ds(i, 2)])))
            if b >= AHEAD:
                i = c * CHUNK + b - AHEAD
                places = [near_place(ids_ref, k, i, first, groups * blocks) for k in range(3)]
                olds = [total[place] for place in places]
                for k in range(3):
                    total[places[k]] = olds[k] - terms[b - AHEAD][:, k * points : (k + 1) * points]

    halo_ref[...] = total[pl.ds(0, REACH)].astype(halo_ref.dtype)
    base_ref[...] = total[pl.ds(REACH, blocks)]


def sum_kernel(capacity, picks_ref, base_ref, halo_ref, back_ref, out_ref, total, sem):
    groups = picks_ref.shape[0]
    blocks = base_ref.shape[0]
    total[pl.ds(0, blocks)] = base_ref[...]
    last = pl.ds(blocks - REACH, REACH)
    total[last] = total[last] + halo_ref[...].astype(jnp.float32)

    @pl.loop(0, groups, unroll=8)
    def _(g):
        picks = [picks_ref[g, r] for r in range(capacity)]
        places = [jnp.where(pick > 0, pick - 1, blocks) for pick in picks]
        olds = [total[place] for place in places]
        for r in range(capacity):
            total[places[r]] = olds[r] - back_ref[g * capacity + r].astype(jnp.float32)

    store = pltpu.make_async_copy(total.at[pl.ds(0, blocks)], out_ref, sem)
    store.start()
    store.wait()


def per_device(probe_vecs, coeffs, cond_prec, neighbours):
    blocks, probes, points = probe_vecs.shape
    groups = lax.axis_size("blk")
    capacity = max(2, blocks // (groups - 1) + 1)
    slots = groups * capacity
    chunks = blocks // CHUNK
    bf16, f32 = jnp.bfloat16, jnp.float32
    tile = (probes, points)
    flops = 2 * blocks * probes * points * points

    def exchange(x):
        order = [turned(place, groups) for place in range(groups)]
        return lax.all_to_all(x, "blk", split_axis=0, concat_axis=0, tiled=True, axis_index_groups=[order])

    ids = neighbours.T
    far_ids = ids[3:]
    all_ids = exchange(jnp.broadcast_to(far_ids, (groups, blocks)))
    outgoing, picks, tail = pl.pallas_call(
        functools.partial(pick_kernel, capacity),
        name="pick_tiles",
        out_shape=(
            jax.ShapeDtypeStruct((slots,) + tile, bf16),
            jax.ShapeDtypeStruct((groups, blocks), jnp.int32),
            jax.ShapeDtypeStruct((REACH,) + tile, bf16),
        ),
        in_specs=[VMEM, HBM],
        out_specs=(HBM, VMEM, VMEM),
        scratch_shapes=[
            pltpu.VMEM((blocks,) + tile, bf16),
            pltpu.VMEM((slots,) + tile, bf16),
            pltpu.SMEM((groups, blocks), jnp.int32),
            pltpu.SemaphoreType.DMA((2 + STORES,)),
        ],
        compiler_params=params(8),
        cost_estimate=pl.CostEstimate(flops=0, bytes_accessed=2 * slots * 4096, transcendentals=0),
    )(all_ids, in_hbm(probe_vecs))
    arrived = exchange(outgoing.reshape((groups, capacity) + tile)).reshape((slots,) + tile)
    halo = passed_along(tail, "blk", 1)
    part, slot_of = pl.pallas_call(
        functools.partial(near_forward_kernel, groups, capacity),
        name="near_forward",
        out_shape=(
            jax.ShapeDtypeStruct((blocks,) + tile, f32),
            jax.ShapeDtypeStruct((1, blocks), jnp.int32),
        ),
        in_specs=[SMEM, VMEM, VMEM, HBM],
        out_specs=(VMEM, VMEM),
        scratch_shapes=[
            pltpu.VMEM((blocks, 3, points, points), bf16),
            pltpu.SemaphoreType.DMA((chunks,)),
        ],
        compiler_params=params(24),
        cost_estimate=pl.CostEstimate(flops=3 * flops, bytes_accessed=14 * 2**20, transcendentals=0),
    )(ids, far_ids, probe_vecs, in_hbm(coeffs))
    scaled, parcel = pl.pallas_call(
        functools.partial(far_kernel, groups),
        name="far_and_scale",
        out_shape=(
            jax.ShapeDtypeStruct((blocks,) + tile, bf16),
            jax.ShapeDtypeStruct((slots,) + tile, bf16),
        ),
        in_specs=[SMEM, SMEM, VMEM, VMEM, VMEM, HBM, HBM, HBM],
        out_specs=(VMEM, VMEM),
        scratch_shapes=[
            pltpu.VMEM((blocks, points, points), bf16),
            pltpu.VMEM((blocks, points, points), bf16),
            pltpu.VMEM((blocks,) + tile, bf16),
            pltpu.VMEM((REACH, 3, points, points), bf16),
            pltpu.VMEM((2 * REACH,) + tile, bf16),
            pltpu.SemaphoreType.DMA((3, chunks)),
        ],
        compiler_params=params(24),
        cost_estimate=pl.CostEstimate(flops=3 * flops, bytes_accessed=11 * 2**20, transcendentals=0),
    )(ids, slot_of, part, arrived, halo, in_hbm(probe_vecs), in_hbm(coeffs), in_hbm(cond_prec))
    returned = exchange(parcel.reshape((groups, capacity) + tile)).reshape((slots,) + tile)
    base, halo_back = pl.pallas_call(
        functools.partial(near_back_kernel, groups),
        name="near_back",
        out_shape=(
            jax.ShapeDtypeStruct((blocks,) + tile, f32),
            jax.ShapeDtypeStruct((REACH,) + tile, bf16),
        ),
        in_specs=[SMEM, VMEM, HBM],
        out_specs=(VMEM, VMEM),
        scratch_shapes=[
            pltpu.VMEM((REACH + blocks,) + tile, f32),
            pltpu.VMEM((blocks, 3, points, points), bf16),
            pltpu.SemaphoreType.DMA((chunks,)),
        ],
        compiler_params=params(24),
        cost_estimate=pl.CostEstimate(flops=3 * flops, bytes_accessed=14 * 2**20, transcendentals=0),
    )(ids, scaled, in_hbm(coeffs))
    halo_sum = passed_along(halo_back, "blk", -1)
    return pl.pallas_call(
        functools.partial(sum_kernel, capacity),
        name="final_sum",
        out_shape=jax.ShapeDtypeStruct((blocks,) + tile, f32),
        in_specs=[SMEM, VMEM, VMEM, VMEM],
        out_specs=HBM,
        scratch_shapes=[pltpu.VMEM((blocks + 1,) + tile, f32), pltpu.SemaphoreType.DMA],
        compiler_params=params(8),
        cost_estimate=pl.CostEstimate(flops=0, bytes_accessed=3 * 2**20, transcendentals=0),
    )(picks, base, halo_sum, returned)


def solution(mesh):
    in_specs = (
        P("blk", None, None),
        P("blk", None, None, None),
        P("blk", None, None),
        P("blk", None),
    )
    return jax.shard_map(
        per_device, mesh=mesh, in_specs=in_specs, out_specs=P("blk", None, None), check_vma=False
    )
```

```python
import functools

import jax
import jax.numpy as jnp
from jax import lax
from jax.experimental import pallas as pl
from jax.experimental.pallas import tpu as pltpu
from jax.sharding import PartitionSpec as P

REACH = 16
CHUNK = 16
AHEAD = 4
STORES = 4
VMEM = pl.BlockSpec(memory_space=pltpu.VMEM)
SMEM = pl.BlockSpec(memory_space=pltpu.SMEM)
HBM = pl.BlockSpec(memory_space=pl.ANY)
NT = (((1,), (1,)), ((), ()))


def params(mib):
    return pltpu.CompilerParams(vmem_limit_bytes=mib * 2**20)


def in_hbm(x):
    return pltpu.with_memory_space_constraint(x, pltpu.HBM)


def passed_along(block, axis, distance):
    size = lax.axis_size(axis)
    return lax.ppermute(block, axis, [((i - distance) % size, i) for i in range(size)])


def exchange_order(groups):
    return list(range(0, groups, 2)) + list(range(groups - 1, 0, -2))


def exchange_place(device, groups):
    return jnp.where(device % 2 == 0, device // 2, groups - 1 - device // 2)


def earlier_matrix(blocks):
    row = lax.broadcasted_iota(jnp.int32, (blocks, blocks), 0)
    col = lax.broadcasted_iota(jnp.int32, (blocks, blocks), 1)
    return (row < col).astype(jnp.float32).astype(jnp.bfloat16)


def ranks_in(mask, blocks):
    chosen = mask.astype(jnp.float32).astype(jnp.bfloat16)
    return jnp.dot(chosen, earlier_matrix(blocks), preferred_element_type=jnp.float32).astype(jnp.int32)


def prep_kernel(ids_ref, probe_ref, sent_ref, tail_ref, sem):
    blocks = probe_ref.shape[0]
    copy = pltpu.make_async_copy(probe_ref.at[pl.ds(blocks - REACH, REACH)], tail_ref, sem)
    copy.start()
    sent_ref[...] = jnp.broadcast_to(ids_ref[3:4, :], sent_ref.shape)
    copy.wait()


def pick_kernel(capacity, ids_ref, probe_ref, out_ref, picks_ref, probe, out, picks_smem, sems):
    groups, blocks = ids_ref.shape
    load = pltpu.make_async_copy(probe_ref, probe, sems.at[0])
    load.start()
    me = lax.axis_index("blk")
    local = ids_ref[...] - me * blocks
    mask = (local >= 0) & (local < blocks)
    rank = ranks_in(mask, blocks)
    lane = lax.broadcasted_iota(jnp.int32, (groups, blocks), 1)
    picks = jnp.zeros((groups, blocks), jnp.int32)
    for r in range(capacity):
        found = jnp.sum(jnp.where(mask & (rank == r), local + 1, 0), axis=1, keepdims=True)
        picks = jnp.where(lane == r, found, picks)
    picks_ref[...] = picks
    copy = pltpu.make_async_copy(picks_ref, picks_smem, sems.at[1])
    copy.start()
    copy.wait()
    load.wait()
    part = groups // STORES

    def store(p):
        rows = pl.ds(p * part * capacity, part * capacity)
        return pltpu.make_async_copy(out.at[rows], out_ref.at[rows], sems.at[2 + p])

    for p in range(STORES):

        @pl.loop(p * part, (p + 1) * part, unroll=8)
        def _(g):
            for r in range(capacity):
                out[g * capacity + r] = probe[jnp.maximum(picks_smem[g, r] - 1, 0)]

        store(p).start()
    for p in range(STORES):
        store(p).wait()


def stacked(mats):
    return mats.reshape(-1, mats.shape[-1])


def apart(left0, left1, mats):
    zero = jnp.zeros_like(left0)
    left = jnp.concatenate(
        [jnp.concatenate([left0, zero], axis=1), jnp.concatenate([zero, left1], axis=1)], axis=0
    )
    out = jnp.dot(left, mats, preferred_element_type=jnp.float32)
    return out.reshape((2,) + (left0.shape[0], mats.shape[1]))


def apart_back(lefts, mats):
    rows, half = lefts.shape[1], mats.shape[0] // 2
    out = lax.dot_general(lefts.reshape(2 * rows, lefts.shape[2]), mats, NT, preferred_element_type=jnp.float32)
    return out[:rows, :half], out[rows:, half:]


def near_place(ids_ref, k, i, first, count):
    place = ids_ref[k, i] - first + REACH
    return jnp.where(place >= count, place - count, place)


def near_forward_kernel(
    groups, capacity, ids_ref, ids_row_ref, halo_ref, probe_ref, coeffs_ref, prec_ref,
    out_ref, slot_ref, first_ref, back_ref, ext, coeffs, prec, back, sems
):
    blocks = probe_ref.shape[0]
    chunks = blocks // CHUNK

    def loads(c):
        own = pl.ds(c * CHUNK, CHUNK)
        return (
            pltpu.make_async_copy(coeffs_ref.at[own], coeffs.at[own], sems.at[0, c]),
            pltpu.make_async_copy(prec_ref.at[own], prec.at[own], sems.at[1, c]),
        )

    def store(c):
        own = pl.ds(c * CHUNK, CHUNK)
        return pltpu.make_async_copy(back.at[own], back_ref.at[own], sems.at[2, c])

    for c in range(chunks):
        for load in loads(c):
            load.start()
    ext[pl.ds(0, REACH)] = halo_ref[...]
    ext[pl.ds(REACH, blocks)] = probe_ref[...]
    owner = ids_row_ref[3:4, :] // blocks
    mask = lax.broadcasted_iota(jnp.int32, (groups, blocks), 0) == owner
    rank = jnp.sum(jnp.where(mask, ranks_in(mask, blocks), 0), axis=0, keepdims=True)
    slot_ref[...] = exchange_place(owner, groups) * capacity + rank
    first = lax.axis_index("blk") * blocks

    @pl.loop(0, chunks)
    def _(c):
        for load in loads(c):
            load.wait()
        for b in range(0, CHUNK, 2):
            i = c * CHUNK + b
            rows = []
            for j in range(2):
                tiles = [ext[near_place(ids_ref, k, i + j, first, groups * blocks)] for k in range(3)]
                rows.append(jnp.concatenate(tiles, axis=1))
            mats = [stacked(coeffs[i + j, pl.ds(0, 3)]) for j in range(2)]
            mixed = apart(rows[0], rows[1], jnp.concatenate(mats, axis=0))
            out_ref[pl.ds(i, 2)] = probe_ref[pl.ds(i, 2)].astype(jnp.float32) - mixed
            for j in range(2):
                folded = lax.dot_general(prec[i + j], coeffs[i + j, 3], NT, preferred_element_type=jnp.float32)
                back[i + j] = folded.astype(jnp.bfloat16)
        store(c).start()

    for c in range(chunks):
        store(c).wait()
    first_ref[0] = coeffs[pl.ds(0, CHUNK), 3]
    first_ref[1] = back[pl.ds(0, CHUNK)]


def far_kernel(
    slots_ref, part_ref, far_ref, first_ref, coeffs_ref, back_ref,
    white_ref, parcel_ref, coeffs, back, slot, sems
):
    blocks = part_ref.shape[0]
    chunks = blocks // CHUNK

    def loads(c):
        own = pl.ds(c * CHUNK, CHUNK)
        return (
            pltpu.make_async_copy(coeffs_ref.at[own, 3], coeffs.at[own], sems.at[0, c]),
            pltpu.make_async_copy(back_ref.at[own], back.at[own], sems.at[1, c]),
        )

    slot_copy = pltpu.make_async_copy(slots_ref, slot, sems.at[0, 0])
    slot_copy.start()
    for c in range(1, chunks):
        for load in loads(c):
            load.start()
    parcel_ref[...] = jnp.zeros_like(parcel_ref)
    slot_copy.wait()

    def mix(c, mats):
        for b in range(0, CHUNK, 2):
            i = c * CHUNK + b
            mixed = apart(far_ref[slot[0, i]], far_ref[slot[0, i + 1]], stacked(mats(c, b)))
            white_ref[pl.ds(i, 2)] = (part_ref[pl.ds(i, 2)] - mixed).astype(jnp.bfloat16)

    def send_back(c, mats):
        for b in range(0, CHUNK, 2):
            i = c * CHUNK + b
            terms = apart(white_ref[i], white_ref[i + 1], stacked(mats(c, b)))
            for j in range(2):
                parcel_ref[slot[0, i + j]] = terms[j].astype(jnp.bfloat16)

    def held(mats):
        return lambda c, b: mats[pl.ds(c * CHUNK + b, 2)]

    def ready(c):
        for load in loads(c):
            load.wait()

    mix(0, lambda c, b: first_ref[0, pl.ds(b, 2)])
    ready(1)
    send_back(0, lambda c, b: first_ref[1, pl.ds(b, 2)])
    mix(1, held(coeffs))

    @pl.loop(2, chunks)
    def _(c):
        ready(c)
        send_back(c - 1, held(back))
        mix(c, held(coeffs))

    send_back(chunks - 1, held(back))


def near_back_kernel(
    groups, ids_ref, white_ref, coeffs_ref, prec_ref, base_ref, halo_ref, total, scaled, coeffs, prec, sems
):
    blocks = white_ref.shape[0]
    points = white_ref.shape[2]
    chunks = blocks // CHUNK

    def load_prec(c):
        own = pl.ds(c * CHUNK, CHUNK)
        return pltpu.make_async_copy(prec_ref.at[own], prec.at[own], sems.at[1, c])

    def load_coeffs(c):
        own = pl.ds(c * CHUNK, CHUNK)
        return pltpu.make_async_copy(coeffs_ref.at[own, pl.ds(0, 3)], coeffs.at[own], sems.at[0, c])

    for c in range(chunks):
        load_prec(c).start()
        load_coeffs(c).start()
    total[pl.ds(0, REACH)] = jnp.zeros((REACH,) + total.shape[1:], jnp.float32)
    first = lax.axis_index("blk") * blocks

    def scale(c):
        load_prec(c).wait()
        for b in range(0, CHUNK, 2):
            i = c * CHUNK + b
            tiles = apart(white_ref[i], white_ref[i + 1], stacked(prec[pl.ds(i, 2)])).astype(jnp.bfloat16)
            scaled[pl.ds(i, 2)] = tiles
            total[pl.ds(REACH + i, 2)] = tiles.astype(jnp.float32)

    def back(c):
        load_coeffs(c).wait()
        terms = []
        for b in range(CHUNK + AHEAD):
            if b < CHUNK and b % 2 == 0:
                i = c * CHUNK + b
                terms.extend(apart_back(scaled[pl.ds(i, 2)], stacked(coeffs[pl.ds(i, 2)])))
            if b >= AHEAD:
                i = c * CHUNK + b - AHEAD
                places = [near_place(ids_ref, k, i, first, groups * blocks) for k in range(3)]
                olds = [total[place] for place in places]
                for k in range(3):
                    total[places[k]] = olds[k] - terms[b - AHEAD][:, k * points : (k + 1) * points]

    scale(0)

    @pl.loop(0, chunks - 1)
    def _(c):
        scale(c + 1)
        back(c)

    back(chunks - 1)
    halo_ref[...] = total[pl.ds(0, REACH)].astype(halo_ref.dtype)
    base_ref[...] = total[pl.ds(REACH, blocks)]


def sum_kernel(capacity, all_picks_ref, base_ref, halo_ref, back_ref, out_ref, total, picks_ref, sems):
    groups = all_picks_ref.shape[0]
    picks_copy = pltpu.make_async_copy(all_picks_ref, picks_ref, sems.at[0])
    picks_copy.start()
    blocks = base_ref.shape[0]
    total[pl.ds(0, blocks)] = base_ref[...]
    last = pl.ds(blocks - REACH, REACH)
    total[last] = total[last] + halo_ref[...].astype(jnp.float32)
    picks_copy.wait()

    @pl.loop(0, groups, unroll=8)
    def _(g):
        picks = [picks_ref[g, r] for r in range(capacity)]
        places = [jnp.where(pick > 0, pick - 1, blocks) for pick in picks]
        olds = [total[place] for place in places]
        for r in range(capacity):
            total[places[r]] = olds[r] - back_ref[g * capacity + r].astype(jnp.float32)

    store = pltpu.make_async_copy(total.at[pl.ds(0, blocks)], out_ref, sems.at[1])
    store.start()
    store.wait()


def per_device(probe_vecs, coeffs, cond_prec, neighbours):
    blocks, probes, points = probe_vecs.shape
    groups = lax.axis_size("blk")
    capacity = max(2, blocks // (groups - 1) + 1)
    slots = groups * capacity
    chunks = blocks // CHUNK
    bf16, f32 = jnp.bfloat16, jnp.float32
    tile = (probes, points)
    flops = 2 * blocks * probes * points * points

    def exchange(x):
        groups_of = [exchange_order(groups)]
        return lax.all_to_all(x, "blk", split_axis=0, concat_axis=0, tiled=True, axis_index_groups=groups_of)

    ids = neighbours.T
    sent_ids, tail = pl.pallas_call(
        prep_kernel,
        name="prep",
        out_shape=(
            jax.ShapeDtypeStruct((groups, blocks), jnp.int32),
            jax.ShapeDtypeStruct((REACH,) + tile, bf16),
        ),
        in_specs=[VMEM, HBM],
        out_specs=(VMEM, VMEM),
        scratch_shapes=[pltpu.SemaphoreType.DMA],
        compiler_params=params(8),
    )(ids, in_hbm(probe_vecs))
    halo = passed_along(tail, "blk", 1)
    all_ids = exchange(sent_ids)
    all_ids, halo = lax.optimization_barrier((all_ids, halo))
    outgoing, picks = pl.pallas_call(
        functools.partial(pick_kernel, capacity),
        name="pick_tiles",
        out_shape=(
            jax.ShapeDtypeStruct((slots,) + tile, bf16),
            jax.ShapeDtypeStruct((groups, blocks), jnp.int32),
        ),
        in_specs=[VMEM, HBM],
        out_specs=(HBM, VMEM),
        scratch_shapes=[
            pltpu.VMEM((blocks,) + tile, bf16),
            pltpu.VMEM((slots,) + tile, bf16),
            pltpu.SMEM((groups, blocks), jnp.int32),
            pltpu.SemaphoreType.DMA((2 + STORES,)),
        ],
        compiler_params=params(8),
        cost_estimate=pl.CostEstimate(flops=0, bytes_accessed=2 * slots * 4096, transcendentals=0),
    )(all_ids, in_hbm(probe_vecs))
    arrived = exchange(outgoing.reshape((groups, capacity) + tile)).reshape((slots,) + tile)
    mats = (blocks, points, points)
    part, slot_of, first_mats, back_mats = pl.pallas_call(
        functools.partial(near_forward_kernel, groups, capacity),
        name="near_forward",
        out_shape=(
            jax.ShapeDtypeStruct((blocks,) + tile, f32),
            jax.ShapeDtypeStruct((1, blocks), jnp.int32),
            jax.ShapeDtypeStruct((2, CHUNK, points, points), bf16),
            pltpu.HBM(mats, bf16),
        ),
        in_specs=[SMEM, VMEM, VMEM, VMEM, HBM, HBM],
        out_specs=(VMEM, VMEM, VMEM, HBM),
        scratch_shapes=[
            pltpu.VMEM((REACH + blocks,) + tile, bf16),
            pltpu.VMEM((blocks, 4, points, points), bf16),
            pltpu.VMEM(mats, bf16),
            pltpu.VMEM(mats, bf16),
            pltpu.SemaphoreType.DMA((3, chunks)),
        ],
        compiler_params=params(36),
        cost_estimate=pl.CostEstimate(flops=5 * flops, bytes_accessed=26 * 2**20, transcendentals=0),
    )(ids, ids, halo, probe_vecs, in_hbm(coeffs), in_hbm(cond_prec))
    white, parcel = pl.pallas_call(
        far_kernel,
        name="far_terms",
        out_shape=(
            jax.ShapeDtypeStruct((blocks,) + tile, bf16),
            jax.ShapeDtypeStruct((slots,) + tile, bf16),
        ),
        in_specs=[VMEM, VMEM, VMEM, VMEM, HBM, HBM],
        out_specs=(VMEM, VMEM),
        scratch_shapes=[
            pltpu.VMEM(mats, bf16),
            pltpu.VMEM(mats, bf16),
            pltpu.SMEM((1, blocks), jnp.int32),
            pltpu.SemaphoreType.DMA((2, chunks)),
        ],
        compiler_params=params(24),
        cost_estimate=pl.CostEstimate(flops=2 * flops, bytes_accessed=11 * 2**20, transcendentals=0),
    )(slot_of, part, arrived, first_mats, in_hbm(coeffs), in_hbm(back_mats))
    returned = exchange(parcel.reshape((groups, capacity) + tile)).reshape((slots,) + tile)
    base, halo_back = pl.pallas_call(
        functools.partial(near_back_kernel, groups),
        name="near_back",
        out_shape=(
            jax.ShapeDtypeStruct((blocks,) + tile, f32),
            jax.ShapeDtypeStruct((REACH,) + tile, bf16),
        ),
        in_specs=[SMEM, VMEM, HBM, HBM],
        out_specs=(VMEM, VMEM),
        scratch_shapes=[
            pltpu.VMEM((REACH + blocks,) + tile, f32),
            pltpu.VMEM((blocks,) + tile, bf16),
            pltpu.VMEM((blocks, 3, points, points), bf16),
            pltpu.VMEM(mats, bf16),
            pltpu.SemaphoreType.DMA((2, chunks)),
        ],
        compiler_params=params(28),
        cost_estimate=pl.CostEstimate(flops=4 * flops, bytes_accessed=18 * 2**20, transcendentals=0),
    )(ids, white, in_hbm(coeffs), in_hbm(cond_prec))
    halo_sum = passed_along(halo_back, "blk", -1)
    return pl.pallas_call(
        functools.partial(sum_kernel, capacity),
        name="final_sum",
        out_shape=jax.ShapeDtypeStruct((blocks,) + tile, f32),
        in_specs=[VMEM, VMEM, VMEM, VMEM],
        out_specs=HBM,
        scratch_shapes=[
            pltpu.VMEM((blocks + 1,) + tile, f32),
            pltpu.SMEM((groups, blocks), jnp.int32),
            pltpu.SemaphoreType.DMA((2,)),
        ],
        compiler_params=params(8),
        cost_estimate=pl.CostEstimate(flops=0, bytes_accessed=3 * 2**20, transcendentals=0),
    )(picks, base, halo_sum, returned)


def solution(mesh):
    in_specs = (
        P("blk", None, None),
        P("blk", None, None, None),
        P("blk", None, None),
        P("blk", None),
    )
    return jax.shard_map(
        per_device, mesh=mesh, in_specs=in_specs, out_specs=P("blk", None, None), check_vma=False
    )
```

```python
import functools

import jax
import jax.numpy as jnp
from jax import lax
from jax.experimental import pallas as pl
from jax.experimental.pallas import tpu as pltpu
from jax.sharding import PartitionSpec as P

REACH = 16
CHUNK = 16
AHEAD = 4
STORES = 4
VMEM = pl.BlockSpec(memory_space=pltpu.VMEM)
SMEM = pl.BlockSpec(memory_space=pltpu.SMEM)
HBM = pl.BlockSpec(memory_space=pl.ANY)
NT = (((1,), (1,)), ((), ()))


def params(mib):
    return pltpu.CompilerParams(vmem_limit_bytes=mib * 2**20)


def in_hbm(x):
    return pltpu.with_memory_space_constraint(x, pltpu.HBM)


def passed_along(block, axis, distance):
    size = lax.axis_size(axis)
    return lax.ppermute(block, axis, [((i - distance) % size, i) for i in range(size)])


def earlier_matrix(blocks):
    row = lax.broadcasted_iota(jnp.int32, (blocks, blocks), 0)
    col = lax.broadcasted_iota(jnp.int32, (blocks, blocks), 1)
    return (row < col).astype(jnp.float32).astype(jnp.bfloat16)


def ranks_in(mask, blocks):
    chosen = mask.astype(jnp.float32).astype(jnp.bfloat16)
    return jnp.dot(chosen, earlier_matrix(blocks), preferred_element_type=jnp.float32).astype(jnp.int32)


def prep_kernel(ids_ref, probe_ref, sent_ref, tail_ref, sem):
    blocks = probe_ref.shape[0]
    copy = pltpu.make_async_copy(probe_ref.at[pl.ds(blocks - REACH, REACH)], tail_ref, sem)
    copy.start()
    sent_ref[...] = jnp.broadcast_to(ids_ref[3:4, :], sent_ref.shape)
    copy.wait()


def pick_kernel(capacity, ids_ref, probe_ref, out_ref, picks_ref, probe, out, picks_smem, sems):
    groups, blocks = ids_ref.shape
    load = pltpu.make_async_copy(probe_ref, probe, sems.at[0])
    load.start()
    me = lax.axis_index("blk")
    local = ids_ref[...] - me * blocks
    mask = (local >= 0) & (local < blocks)
    rank = ranks_in(mask, blocks)
    lane = lax.broadcasted_iota(jnp.int32, (groups, blocks), 1)
    picks = jnp.zeros((groups, blocks), jnp.int32)
    for r in range(capacity):
        found = jnp.sum(jnp.where(mask & (rank == r), local + 1, 0), axis=1, keepdims=True)
        picks = jnp.where(lane == r, found, picks)
    picks_ref[...] = picks
    copy = pltpu.make_async_copy(picks_ref, picks_smem, sems.at[1])
    copy.start()
    copy.wait()
    load.wait()
    part = groups // STORES

    def store(p):
        rows = pl.ds(p * part * capacity, part * capacity)
        return pltpu.make_async_copy(out.at[rows], out_ref.at[rows], sems.at[2 + p])

    for p in range(STORES):

        @pl.loop(p * part, (p + 1) * part, unroll=8)
        def _(g):
            for r in range(capacity):
                out[g * capacity + r] = probe[jnp.maximum(picks_smem[g, r] - 1, 0)]

        store(p).start()
    for p in range(STORES):
        store(p).wait()


def stacked(mats):
    return mats.reshape(-1, mats.shape[-1])


def apart(left0, left1, mats):
    zero = jnp.zeros_like(left0)
    left = jnp.concatenate(
        [jnp.concatenate([left0, zero], axis=1), jnp.concatenate([zero, left1], axis=1)], axis=0
    )
    out = jnp.dot(left, mats, preferred_element_type=jnp.float32)
    return out.reshape((2,) + (left0.shape[0], mats.shape[1]))


def apart_back(lefts, mats):
    rows, half = lefts.shape[1], mats.shape[0] // 2
    out = lax.dot_general(lefts.reshape(2 * rows, lefts.shape[2]), mats, NT, preferred_element_type=jnp.float32)
    return out[:rows, :half], out[rows:, half:]


def near_place(ids_ref, k, i, first, count):
    place = ids_ref[k, i] - first + REACH
    return jnp.where(place >= count, place - count, place)


def near_forward_kernel(
    groups, capacity, ids_ref, ids_row_ref, halo_ref, probe_ref, coeffs_ref, prec_ref,
    out_ref, slot_ref, first_ref, back_ref, ext, coeffs, prec, back, sems
):
    blocks = probe_ref.shape[0]
    chunks = blocks // CHUNK

    def loads(c):
        own = pl.ds(c * CHUNK, CHUNK)
        return (
            pltpu.make_async_copy(coeffs_ref.at[own], coeffs.at[own], sems.at[0, c]),
            pltpu.make_async_copy(prec_ref.at[own], prec.at[own], sems.at[1, c]),
        )

    def store(c):
        own = pl.ds(c * CHUNK, CHUNK)
        return pltpu.make_async_copy(back.at[own], back_ref.at[own], sems.at[2, c])

    for c in range(chunks):
        for load in loads(c):
            load.start()
    ext[pl.ds(0, REACH)] = halo_ref[...]
    ext[pl.ds(REACH, blocks)] = probe_ref[...]
    owner = ids_row_ref[3:4, :] // blocks
    mask = lax.broadcasted_iota(jnp.int32, (groups, blocks), 0) == owner
    rank = jnp.sum(jnp.where(mask, ranks_in(mask, blocks), 0), axis=0, keepdims=True)
    slot_ref[...] = owner * capacity + rank
    first = lax.axis_index("blk") * blocks

    @pl.loop(0, chunks)
    def _(c):
        for load in loads(c):
            load.wait()
        for b in range(0, CHUNK, 2):
            i = c * CHUNK + b
            rows = []
            for j in range(2):
                tiles = [ext[near_place(ids_ref, k, i + j, first, groups * blocks)] for k in range(3)]
                rows.append(jnp.concatenate(tiles, axis=1))
            mats = [stacked(coeffs[i + j, pl.ds(0, 3)]) for j in range(2)]
            mixed = apart(rows[0], rows[1], jnp.concatenate(mats, axis=0))
            out_ref[pl.ds(i, 2)] = probe_ref[pl.ds(i, 2)].astype(jnp.float32) - mixed
            for j in range(2):
                folded = lax.dot_general(prec[i + j], coeffs[i + j, 3], NT, preferred_element_type=jnp.float32)
                back[i + j] = folded.astype(jnp.bfloat16)
        store(c).start()

    for c in range(chunks):
        store(c).wait()
    first_ref[0] = coeffs[pl.ds(0, CHUNK), 3]
    first_ref[1] = back[pl.ds(0, CHUNK)]


def far_kernel(
    slots_ref, part_ref, far_ref, first_ref, coeffs_ref, back_ref,
    white_ref, parcel_ref, coeffs, back, slot, sems
):
    blocks = part_ref.shape[0]
    chunks = blocks // CHUNK

    def load_coeffs(c):
        own = pl.ds(c * CHUNK, CHUNK)
        return pltpu.make_async_copy(coeffs_ref.at[own, 3], coeffs.at[own], sems.at[0, c])

    def load_back(c):
        own = pl.ds(c * CHUNK, CHUNK)
        return pltpu.make_async_copy(back_ref.at[own], back.at[own], sems.at[1, c])

    slot_copy = pltpu.make_async_copy(slots_ref, slot, sems.at[0, 0])
    slot_copy.start()
    for c in range(1, chunks + 2):
        if c < chunks:
            load_coeffs(c).start()
        if c >= 3:
            load_back(c - 2).start()
    parcel_ref[...] = jnp.zeros_like(parcel_ref)
    slot_copy.wait()

    def mix(c, mats):
        for b in range(0, CHUNK, 2):
            i = c * CHUNK + b
            mixed = apart(far_ref[slot[0, i]], far_ref[slot[0, i + 1]], stacked(mats(c, b)))
            white_ref[pl.ds(i, 2)] = (part_ref[pl.ds(i, 2)] - mixed).astype(jnp.bfloat16)

    def send_back(c, mats):
        for b in range(0, CHUNK, 2):
            i = c * CHUNK + b
            terms = apart(white_ref[i], white_ref[i + 1], stacked(mats(c, b)))
            for j in range(2):
                parcel_ref[slot[0, i + j]] = terms[j].astype(jnp.bfloat16)

    def held(mats):
        return lambda c, b: mats[pl.ds(c * CHUNK + b, 2)]

    mix(0, lambda c, b: first_ref[0, pl.ds(b, 2)])
    load_coeffs(1).wait()
    send_back(0, lambda c, b: first_ref[1, pl.ds(b, 2)])
    mix(1, held(coeffs))
    load_coeffs(2).wait()
    mix(2, held(coeffs))

    @pl.loop(3, chunks)
    def _(c):
        load_coeffs(c).wait()
        load_back(c - 2).wait()
        send_back(c - 2, held(back))
        mix(c, held(coeffs))

    for c in (chunks - 2, chunks - 1):
        load_back(c).wait()
        send_back(c, held(back))


def near_back_kernel(
    groups, ids_ref, white_ref, coeffs_ref, prec_ref, base_ref, halo_ref, total, scaled, coeffs, prec, sems
):
    blocks = white_ref.shape[0]
    points = white_ref.shape[2]
    chunks = blocks // CHUNK

    def load_prec(c):
        own = pl.ds(c * CHUNK, CHUNK)
        return pltpu.make_async_copy(prec_ref.at[own], prec.at[own], sems.at[1, c])

    def load_coeffs(c):
        own = pl.ds(c * CHUNK, CHUNK)
        return pltpu.make_async_copy(coeffs_ref.at[own, pl.ds(0, 3)], coeffs.at[own], sems.at[0, c])

    for c in range(chunks):
        load_prec(c).start()
        load_coeffs(c).start()
    total[pl.ds(0, REACH)] = jnp.zeros((REACH,) + total.shape[1:], jnp.float32)
    first = lax.axis_index("blk") * blocks

    def scale(c):
        load_prec(c).wait()
        for b in range(0, CHUNK, 2):
            i = c * CHUNK + b
            tiles = apart(white_ref[i], white_ref[i + 1], stacked(prec[pl.ds(i, 2)])).astype(jnp.bfloat16)
            scaled[pl.ds(i, 2)] = tiles
            total[pl.ds(REACH + i, 2)] = tiles.astype(jnp.float32)

    def back(c):
        load_coeffs(c).wait()
        terms = []
        for b in range(CHUNK + AHEAD):
            if b < CHUNK and b % 2 == 0:
                i = c * CHUNK + b
                terms.extend(apart_back(scaled[pl.ds(i, 2)], stacked(coeffs[pl.ds(i, 2)])))
            if b >= AHEAD:
                i = c * CHUNK + b - AHEAD
                places = [near_place(ids_ref, k, i, first, groups * blocks) for k in range(3)]
                olds = [total[place] for place in places]
                for k in range(3):
                    total[places[k]] = olds[k] - terms[b - AHEAD][:, k * points : (k + 1) * points]

    scale(0)

    @pl.loop(0, chunks - 1)
    def _(c):
        scale(c + 1)
        back(c)

    back(chunks - 1)
    halo_ref[...] = total[pl.ds(0, REACH)].astype(halo_ref.dtype)
    base_ref[...] = total[pl.ds(REACH, blocks)]


def sum_kernel(capacity, all_picks_ref, base_ref, halo_ref, back_ref, out_ref, total, picks_ref, sems):
    groups = all_picks_ref.shape[0]
    picks_copy = pltpu.make_async_copy(all_picks_ref, picks_ref, sems.at[0])
    picks_copy.start()
    blocks = base_ref.shape[0]
    total[pl.ds(0, blocks)] = base_ref[...]
    last = pl.ds(blocks - REACH, REACH)
    total[last] = total[last] + halo_ref[...].astype(jnp.float32)
    picks_copy.wait()

    @pl.loop(0, groups, unroll=8)
    def _(g):
        picks = [picks_ref[g, r] for r in range(capacity)]
        places = [jnp.where(pick > 0, pick - 1, blocks) for pick in picks]
        olds = [total[place] for place in places]
        for r in range(capacity):
            total[places[r]] = olds[r] - back_ref[g * capacity + r].astype(jnp.float32)

    store = pltpu.make_async_copy(total.at[pl.ds(0, blocks)], out_ref, sems.at[1])
    store.start()
    store.wait()


def per_device(probe_vecs, coeffs, cond_prec, neighbours):
    blocks, probes, points = probe_vecs.shape
    groups = lax.axis_size("blk")
    capacity = max(2, blocks // (groups - 1) + 1)
    slots = groups * capacity
    chunks = blocks // CHUNK
    bf16, f32 = jnp.bfloat16, jnp.float32
    tile = (probes, points)
    flops = 2 * blocks * probes * points * points

    def exchange(x):
        return lax.all_to_all(x, "blk", split_axis=0, concat_axis=0, tiled=True)

    ids = neighbours.T
    sent_ids, tail = pl.pallas_call(
        prep_kernel,
        name="prep",
        out_shape=(
            jax.ShapeDtypeStruct((groups, blocks), jnp.int32),
            jax.ShapeDtypeStruct((REACH,) + tile, bf16),
        ),
        in_specs=[VMEM, HBM],
        out_specs=(VMEM, VMEM),
        scratch_shapes=[pltpu.SemaphoreType.DMA],
        compiler_params=params(8),
    )(in_hbm(ids), in_hbm(probe_vecs))
    halo = passed_along(tail, "blk", 1)
    all_ids = exchange(sent_ids)
    all_ids, halo = lax.optimization_barrier((all_ids, halo))
    outgoing, picks = pl.pallas_call(
        functools.partial(pick_kernel, capacity),
        name="pick_tiles",
        out_shape=(
            jax.ShapeDtypeStruct((slots,) + tile, bf16),
            jax.ShapeDtypeStruct((groups, blocks), jnp.int32),
        ),
        in_specs=[VMEM, HBM],
        out_specs=(HBM, VMEM),
        scratch_shapes=[
            pltpu.VMEM((blocks,) + tile, bf16),
            pltpu.VMEM((slots,) + tile, bf16),
            pltpu.SMEM((groups, blocks), jnp.int32),
            pltpu.SemaphoreType.DMA((2 + STORES,)),
        ],
        compiler_params=params(8),
        cost_estimate=pl.CostEstimate(flops=0, bytes_accessed=2 * slots * 4096, transcendentals=0),
    )(all_ids, in_hbm(probe_vecs))
    arrived = exchange(outgoing.reshape((groups, capacity) + tile)).reshape((slots,) + tile)
    mats = (blocks, points, points)
    part, slot_of, first_mats, back_mats = pl.pallas_call(
        functools.partial(near_forward_kernel, groups, capacity),
        name="near_forward",
        out_shape=(
            jax.ShapeDtypeStruct((blocks,) + tile, f32),
            jax.ShapeDtypeStruct((1, blocks), jnp.int32),
            jax.ShapeDtypeStruct((2, CHUNK, points, points), bf16),
            pltpu.HBM(mats, bf16),
        ),
        in_specs=[SMEM, VMEM, VMEM, VMEM, HBM, HBM],
        out_specs=(VMEM, VMEM, VMEM, HBM),
        scratch_shapes=[
            pltpu.VMEM((REACH + blocks,) + tile, bf16),
            pltpu.VMEM((blocks, 4, points, points), bf16),
            pltpu.VMEM(mats, bf16),
            pltpu.VMEM(mats, bf16),
            pltpu.SemaphoreType.DMA((3, chunks)),
        ],
        compiler_params=params(36),
        cost_estimate=pl.CostEstimate(flops=5 * flops, bytes_accessed=26 * 2**20, transcendentals=0),
    )(ids, ids, halo, probe_vecs, in_hbm(coeffs), in_hbm(cond_prec))
    white, parcel = pl.pallas_call(
        far_kernel,
        name="far_terms",
        out_shape=(
            jax.ShapeDtypeStruct((blocks,) + tile, bf16),
            jax.ShapeDtypeStruct((slots,) + tile, bf16),
        ),
        in_specs=[VMEM, VMEM, VMEM, VMEM, HBM, HBM],
        out_specs=(VMEM, VMEM),
        scratch_shapes=[
            pltpu.VMEM(mats, bf16),
            pltpu.VMEM(mats, bf16),
            pltpu.SMEM((1, blocks), jnp.int32),
            pltpu.SemaphoreType.DMA((2, chunks)),
        ],
        compiler_params=params(24),
        cost_estimate=pl.CostEstimate(flops=2 * flops, bytes_accessed=11 * 2**20, transcendentals=0),
    )(slot_of, part, arrived, first_mats, in_hbm(coeffs), in_hbm(back_mats))
    returned = exchange(parcel.reshape((groups, capacity) + tile)).reshape((slots,) + tile)
    base, halo_back = pl.pallas_call(
        functools.partial(near_back_kernel, groups),
        name="near_back",
        out_shape=(
            jax.ShapeDtypeStruct((blocks,) + tile, f32),
            jax.ShapeDtypeStruct((REACH,) + tile, bf16),
        ),
        in_specs=[SMEM, VMEM, HBM, HBM],
        out_specs=(VMEM, VMEM),
        scratch_shapes=[
            pltpu.VMEM((REACH + blocks,) + tile, f32),
            pltpu.VMEM((blocks,) + tile, bf16),
            pltpu.VMEM((blocks, 3, points, points), bf16),
            pltpu.VMEM(mats, bf16),
            pltpu.SemaphoreType.DMA((2, chunks)),
        ],
        compiler_params=params(28),
        cost_estimate=pl.CostEstimate(flops=4 * flops, bytes_accessed=18 * 2**20, transcendentals=0),
    )(ids, white, in_hbm(coeffs), in_hbm(cond_prec))
    halo_sum = passed_along(halo_back, "blk", -1)
    return pl.pallas_call(
        functools.partial(sum_kernel, capacity),
        name="final_sum",
        out_shape=jax.ShapeDtypeStruct((blocks,) + tile, f32),
        in_specs=[VMEM, VMEM, VMEM, VMEM],
        out_specs=HBM,
        scratch_shapes=[
            pltpu.VMEM((blocks + 1,) + tile, f32),
            pltpu.SMEM((groups, blocks), jnp.int32),
            pltpu.SemaphoreType.DMA((2,)),
        ],
        compiler_params=params(8),
        cost_estimate=pl.CostEstimate(flops=0, bytes_accessed=3 * 2**20, transcendentals=0),
    )(picks, base, halo_sum, returned)


def solution(mesh):
    in_specs = (
        P("blk", None, None),
        P("blk", None, None, None),
        P("blk", None, None),
        P("blk", None),
    )
    return jax.shard_map(
        per_device, mesh=mesh, in_specs=in_specs, out_specs=P("blk", None, None), check_vma=False
    )
```

```python
import functools

import jax
import jax.numpy as jnp
from jax import lax
from jax.experimental import pallas as pl
from jax.experimental.pallas import tpu as pltpu
from jax.sharding import PartitionSpec as P

REACH = 16
CHUNK = 16
AHEAD = 4
HELD = 3
STORES = 4
VMEM = pl.BlockSpec(memory_space=pltpu.VMEM)
SMEM = pl.BlockSpec(memory_space=pltpu.SMEM)
HBM = pl.BlockSpec(memory_space=pl.ANY)
NT = (((1,), (1,)), ((), ()))


def params(mib):
    return pltpu.CompilerParams(vmem_limit_bytes=mib * 2**20)


def in_hbm(x):
    return pltpu.with_memory_space_constraint(x, pltpu.HBM)


def passed_along(block, axis, distance):
    size = lax.axis_size(axis)
    return lax.ppermute(block, axis, [((i - distance) % size, i) for i in range(size)])


def earlier_matrix(blocks):
    row = lax.broadcasted_iota(jnp.int32, (blocks, blocks), 0)
    col = lax.broadcasted_iota(jnp.int32, (blocks, blocks), 1)
    return (row < col).astype(jnp.float32).astype(jnp.bfloat16)


def ranks_in(mask, blocks):
    chosen = mask.astype(jnp.float32).astype(jnp.bfloat16)
    return jnp.dot(chosen, earlier_matrix(blocks), preferred_element_type=jnp.float32).astype(jnp.int32)


def prep_kernel(ids_ref, probe_ref, sent_ref, tail_ref, ids, sems):
    blocks = probe_ref.shape[0]
    ids_copy = pltpu.make_async_copy(ids_ref, ids, sems.at[0])
    tail_copy = pltpu.make_async_copy(probe_ref.at[pl.ds(blocks - REACH, REACH)], tail_ref, sems.at[1])
    ids_copy.start()
    tail_copy.start()
    ids_copy.wait()
    sent_ref[...] = jnp.broadcast_to(ids[3:4, :], sent_ref.shape)
    tail_copy.wait()


def pick_kernel(capacity, ids_ref, probe_ref, out_ref, picks_ref, probe, out, picks_smem, sems):
    groups, blocks = ids_ref.shape
    load = pltpu.make_async_copy(probe_ref, probe, sems.at[0])
    load.start()
    me = lax.axis_index("blk")
    local = ids_ref[...] - me * blocks
    mask = (local >= 0) & (local < blocks)
    rank = ranks_in(mask, blocks)
    lane = lax.broadcasted_iota(jnp.int32, (groups, blocks), 1)
    picks = jnp.zeros((groups, blocks), jnp.int32)
    for r in range(capacity):
        found = jnp.sum(jnp.where(mask & (rank == r), local + 1, 0), axis=1, keepdims=True)
        picks = jnp.where(lane == r, found, picks)
    picks_ref[...] = picks
    copy = pltpu.make_async_copy(picks_ref, picks_smem, sems.at[1])
    copy.start()
    copy.wait()
    load.wait()
    part = groups // STORES

    def store(p):
        rows = pl.ds(p * part * capacity, part * capacity)
        return pltpu.make_async_copy(out.at[rows], out_ref.at[rows], sems.at[2 + p])

    for p in range(STORES):

        @pl.loop(p * part, (p + 1) * part, unroll=8)
        def _(g):
            for r in range(capacity):
                out[g * capacity + r] = probe[jnp.maximum(picks_smem[g, r] - 1, 0)]

        store(p).start()
    for p in range(STORES):
        store(p).wait()


def stacked(mats):
    return mats.reshape(-1, mats.shape[-1])


def apart(left0, left1, mats):
    zero = jnp.zeros_like(left0)
    left = jnp.concatenate(
        [jnp.concatenate([left0, zero], axis=1), jnp.concatenate([zero, left1], axis=1)], axis=0
    )
    out = jnp.dot(left, mats, preferred_element_type=jnp.float32)
    return out.reshape((2,) + (left0.shape[0], mats.shape[1]))


def apart_back(lefts, mats):
    rows, half = lefts.shape[1], mats.shape[0] // 2
    out = lax.dot_general(lefts.reshape(2 * rows, lefts.shape[2]), mats, NT, preferred_element_type=jnp.float32)
    return out[:rows, :half], out[rows:, half:]


def near_place(ids_ref, k, i, first, count):
    place = ids_ref[k, i] - first + REACH
    return jnp.where(place >= count, place - count, place)


def near_forward_kernel(
    groups, capacity, ids_ref, ids_row_ref, halo_ref, probe_ref, coeffs_ref, prec_ref,
    part_ref, own_ref, slot_ref, first_ref, mats_ref, ext, coeffs, prec, part, fold, mats, sems
):
    blocks = probe_ref.shape[0]
    chunks = blocks // CHUNK

    def loads(c):
        own = pl.ds(c * CHUNK, CHUNK)
        return (
            pltpu.make_async_copy(coeffs_ref.at[own], coeffs.at[own], sems.at[0, c]),
            pltpu.make_async_copy(prec_ref.at[own], prec.at[own], sems.at[1, c]),
        )

    def store_part(c):
        own = pl.ds(c * CHUNK, CHUNK)
        return pltpu.make_async_copy(part.at[own], part_ref.at[own], sems.at[2, c])

    def store_mats(c):
        own = pl.ds(c * CHUNK, CHUNK)
        return pltpu.make_async_copy(mats.at[own], mats_ref.at[own], sems.at[3, c])

    own_load = pltpu.make_async_copy(probe_ref, ext.at[pl.ds(REACH, blocks)], sems.at[2, 0])
    own_load.start()
    for c in range(chunks):
        for load in loads(c):
            load.start()
    ext[pl.ds(0, REACH)] = halo_ref[...]
    owner = ids_row_ref[3:4, :] // blocks
    mask = lax.broadcasted_iota(jnp.int32, (groups, blocks), 0) == owner
    rank = jnp.sum(jnp.where(mask, ranks_in(mask, blocks), 0), axis=0, keepdims=True)
    slot_ref[...] = owner * capacity + rank
    first = lax.axis_index("blk") * blocks
    own_load.wait()

    def make(c):
        for b in range(0, CHUNK, 2):
            i = c * CHUNK + b
            rows = []
            for j in range(2):
                tiles = [ext[near_place(ids_ref, k, i + j, first, groups * blocks)] for k in range(3)]
                rows.append(jnp.concatenate(tiles, axis=1))
            near = [stacked(coeffs[i + j, pl.ds(0, 3)]) for j in range(2)]
            mixed = apart(rows[0], rows[1], jnp.concatenate(near, axis=0))
            part[pl.ds(i, 2)] = ext[pl.ds(REACH + i, 2)].astype(jnp.float32) - mixed
            for j in range(2):
                folded = lax.dot_general(prec[i + j], coeffs[i + j, 3], NT, preferred_element_type=jnp.float32)
                fold[i + j] = folded.astype(jnp.bfloat16)
        store_part(c).start()

    def use(c):
        for b in range(0, CHUNK, 2):
            i = c * CHUNK + b
            halves = []
            for j in range(2):
                high = part[i + j].astype(jnp.bfloat16)
                low = (part[i + j] - high.astype(jnp.float32)).astype(jnp.bfloat16)
                halves.append(jnp.concatenate([high, low], axis=0))
            both = apart(halves[0], halves[1], stacked(fold[pl.ds(i, 2)]))
            rows = both.shape[1] // 2
            own_ref[pl.ds(i, 2)] = both[:, :rows] + both[:, rows:]
            for j in range(2):
                mat = jnp.dot(coeffs[i + j, 3], fold[i + j], preferred_element_type=jnp.float32)
                mats[i + j] = mat.astype(jnp.bfloat16)
        store_mats(c).start()

    for load in loads(0):
        load.wait()
    make(0)

    @pl.loop(1, chunks)
    def _(c):
        for load in loads(c):
            load.wait()
        use(c - 1)
        make(c)

    use(chunks - 1)
    first_ref[...] = mats[pl.ds(0, HELD * CHUNK)]
    for c in range(chunks):
        store_part(c).wait()
        store_mats(c).wait()


def far_kernel(slots_ref, own_ref, far_ref, first_ref, mats_ref, parcel_ref, mats, slot, sems):
    blocks = own_ref.shape[0]
    chunks = blocks // CHUNK

    def load(c):
        own = pl.ds(c * CHUNK, CHUNK)
        return pltpu.make_async_copy(mats_ref.at[own], mats.at[own], sems.at[c])

    slot_copy = pltpu.make_async_copy(slots_ref, slot, sems.at[0])
    slot_copy.start()
    for c in range(HELD, chunks):
        load(c).start()
    parcel_ref[...] = jnp.zeros_like(parcel_ref)
    slot_copy.wait()

    def send_back(c, pair):
        for b in range(0, CHUNK, 2):
            i = c * CHUNK + b
            terms = own_ref[pl.ds(i, 2)] - apart(far_ref[slot[0, i]], far_ref[slot[0, i + 1]], stacked(pair[pl.ds(i, 2)]))
            for j in range(2):
                parcel_ref[slot[0, i + j]] = terms[j].astype(jnp.bfloat16)

    for c in range(HELD):
        send_back(c, first_ref)

    @pl.loop(HELD, chunks)
    def _(c):
        load(c).wait()
        send_back(c, mats)


def near_back_kernel(
    groups, ids_ref, slot_ref, far_ref, part_ref, coeffs_ref, prec_ref,
    base_ref, halo_ref, total, white, scaled, part, coeffs, prec, sems
):
    blocks = base_ref.shape[0]
    points = base_ref.shape[2]
    chunks = blocks // CHUNK

    def load(c, which):
        own = pl.ds(c * CHUNK, CHUNK)
        source, target = ((part_ref, part), (coeffs_ref, coeffs), (prec_ref, prec))[which]
        return pltpu.make_async_copy(source.at[own], target.at[own], sems.at[which, c])

    for c in range(chunks):
        for which in range(3):
            load(c, which).start()
    total[pl.ds(0, REACH)] = jnp.zeros((REACH,) + total.shape[1:], jnp.float32)
    first = lax.axis_index("blk") * blocks

    def mix(c):
        load(c, 0).wait()
        load(c, 1).wait()
        for b in range(0, CHUNK, 2):
            i = c * CHUNK + b
            mats = jnp.concatenate([coeffs[i, 3], coeffs[i + 1, 3]], axis=0)
            mixed = apart(far_ref[slot_ref[0, i]], far_ref[slot_ref[0, i + 1]], mats)
            white[pl.ds(i, 2)] = (part[pl.ds(i, 2)] - mixed).astype(jnp.bfloat16)

    def scale(c):
        load(c, 2).wait()
        for b in range(0, CHUNK, 2):
            i = c * CHUNK + b
            tiles = apart(white[i], white[i + 1], stacked(prec[pl.ds(i, 2)])).astype(jnp.bfloat16)
            scaled[pl.ds(i, 2)] = tiles
            total[pl.ds(REACH + i, 2)] = tiles.astype(jnp.float32)

    def back(c):
        terms = []
        for b in range(CHUNK + AHEAD):
            if b < CHUNK and b % 2 == 0:
                i = c * CHUNK + b
                mats = [stacked(coeffs[i + j, pl.ds(0, 3)]) for j in range(2)]
                terms.extend(apart_back(scaled[pl.ds(i, 2)], jnp.concatenate(mats, axis=0)))
            if b >= AHEAD:
                i = c * CHUNK + b - AHEAD
                places = [near_place(ids_ref, k, i, first, groups * blocks) for k in range(3)]
                olds = [total[place] for place in places]
                for k in range(3):
                    total[places[k]] = olds[k] - terms[b - AHEAD][:, k * points : (k + 1) * points]

    mix(0)
    scale(0)
    mix(1)

    @pl.loop(0, chunks - 2)
    def _(c):
        back(c)
        scale(c + 1)
        mix(c + 2)

    back(chunks - 2)
    scale(chunks - 1)
    back(chunks - 1)
    halo_ref[...] = total[pl.ds(0, REACH)].astype(halo_ref.dtype)
    base_ref[...] = total[pl.ds(REACH, blocks)]


def sum_kernel(capacity, all_picks_ref, base_ref, halo_ref, back_ref, out_ref, total, picks_ref, sems):
    groups = all_picks_ref.shape[0]
    picks_copy = pltpu.make_async_copy(all_picks_ref, picks_ref, sems.at[0])
    picks_copy.start()
    blocks = base_ref.shape[0]
    total[pl.ds(0, blocks)] = base_ref[...]
    last = pl.ds(blocks - REACH, REACH)
    total[last] = total[last] + halo_ref[...].astype(jnp.float32)
    picks_copy.wait()

    @pl.loop(0, groups, unroll=8)
    def _(g):
        picks = [picks_ref[g, r] for r in range(capacity)]
        places = [jnp.where(pick > 0, pick - 1, blocks) for pick in picks]
        olds = [total[place] for place in places]
        for r in range(capacity):
            total[places[r]] = olds[r] - back_ref[g * capacity + r].astype(jnp.float32)

    store = pltpu.make_async_copy(total.at[pl.ds(0, blocks)], out_ref, sems.at[1])
    store.start()
    store.wait()


def per_device(probe_vecs, coeffs, cond_prec, neighbours):
    blocks, probes, points = probe_vecs.shape
    groups = lax.axis_size("blk")
    capacity = max(2, blocks // (groups - 1) + 1)
    slots = groups * capacity
    chunks = blocks // CHUNK
    bf16, f32 = jnp.bfloat16, jnp.float32
    tile = (probes, points)
    flops = 2 * blocks * probes * points * points

    def exchange(x):
        return lax.all_to_all(x, "blk", split_axis=0, concat_axis=0, tiled=True)

    ids = neighbours.T
    sent_ids, tail = pl.pallas_call(
        prep_kernel,
        name="prep",
        out_shape=(
            jax.ShapeDtypeStruct((groups, blocks), jnp.int32),
            jax.ShapeDtypeStruct((REACH,) + tile, bf16),
        ),
        in_specs=[HBM, HBM],
        out_specs=(VMEM, VMEM),
        scratch_shapes=[pltpu.VMEM(ids.shape, jnp.int32), pltpu.SemaphoreType.DMA((2,))],
        compiler_params=params(8),
    )(in_hbm(ids), in_hbm(probe_vecs))
    halo = passed_along(tail, "blk", 1)
    all_ids = exchange(sent_ids)
    all_ids, halo = lax.optimization_barrier((all_ids, halo))
    outgoing, picks = pl.pallas_call(
        functools.partial(pick_kernel, capacity),
        name="pick_tiles",
        out_shape=(
            jax.ShapeDtypeStruct((slots,) + tile, bf16),
            jax.ShapeDtypeStruct((groups, blocks), jnp.int32),
        ),
        in_specs=[VMEM, HBM],
        out_specs=(HBM, VMEM),
        scratch_shapes=[
            pltpu.VMEM((blocks,) + tile, bf16),
            pltpu.VMEM((slots,) + tile, bf16),
            pltpu.SMEM((groups, blocks), jnp.int32),
            pltpu.SemaphoreType.DMA((2 + STORES,)),
        ],
        compiler_params=params(8),
        cost_estimate=pl.CostEstimate(flops=0, bytes_accessed=2 * slots * 4096, transcendentals=0),
    )(all_ids, in_hbm(probe_vecs))
    arrived = exchange(outgoing.reshape((groups, capacity) + tile)).reshape((slots,) + tile)
    mats = (blocks, points, points)
    all_mats = pltpu.VMEM((blocks, 4, points, points), bf16)
    tiles_f32 = jax.ShapeDtypeStruct((blocks,) + tile, f32)
    part, own_far, slot_of, first_mats, far_mats = pl.pallas_call(
        functools.partial(near_forward_kernel, groups, capacity),
        name="near_forward",
        out_shape=(
            pltpu.HBM((blocks,) + tile, f32),
            tiles_f32,
            jax.ShapeDtypeStruct((1, blocks), jnp.int32),
            jax.ShapeDtypeStruct((HELD * CHUNK, points, points), bf16),
            pltpu.HBM(mats, bf16),
        ),
        in_specs=[SMEM, VMEM, VMEM, HBM, HBM, HBM],
        out_specs=(HBM, VMEM, VMEM, VMEM, HBM),
        scratch_shapes=[
            pltpu.VMEM((REACH + blocks,) + tile, bf16),
            all_mats,
            pltpu.VMEM(mats, bf16),
            pltpu.VMEM((blocks,) + tile, f32),
            pltpu.VMEM(mats, bf16),
            pltpu.VMEM(mats, bf16),
            pltpu.SemaphoreType.DMA((4, chunks)),
        ],
        compiler_params=params(40),
        cost_estimate=pl.CostEstimate(flops=20 * flops, bytes_accessed=28 * 2**20, transcendentals=0),
    )(ids, ids, halo, in_hbm(probe_vecs), in_hbm(coeffs), in_hbm(cond_prec))
    parcel = pl.pallas_call(
        far_kernel,
        name="far_terms",
        out_shape=jax.ShapeDtypeStruct((slots,) + tile, bf16),
        in_specs=[VMEM, VMEM, VMEM, VMEM, HBM],
        out_specs=VMEM,
        scratch_shapes=[
            pltpu.VMEM(mats, bf16),
            pltpu.SMEM((1, blocks), jnp.int32),
            pltpu.SemaphoreType.DMA((chunks,)),
        ],
        compiler_params=params(16),
        cost_estimate=pl.CostEstimate(flops=flops, bytes_accessed=6 * 2**20, transcendentals=0),
    )(slot_of, own_far, arrived, first_mats, in_hbm(far_mats))
    parcel, arrived = lax.optimization_barrier((parcel, arrived))
    returned = exchange(parcel.reshape((groups, capacity) + tile)).reshape((slots,) + tile)
    base, halo_back = pl.pallas_call(
        functools.partial(near_back_kernel, groups),
        name="near_back",
        out_shape=(tiles_f32, jax.ShapeDtypeStruct((REACH,) + tile, bf16)),
        in_specs=[SMEM, SMEM, VMEM, HBM, HBM, HBM],
        out_specs=(VMEM, VMEM),
        scratch_shapes=[
            pltpu.VMEM((REACH + blocks,) + tile, f32),
            pltpu.VMEM((blocks,) + tile, bf16),
            pltpu.VMEM((blocks,) + tile, bf16),
            pltpu.VMEM((blocks,) + tile, f32),
            all_mats,
            pltpu.VMEM(mats, bf16),
            pltpu.SemaphoreType.DMA((3, chunks)),
        ],
        compiler_params=params(36),
        cost_estimate=pl.CostEstimate(flops=5 * flops, bytes_accessed=23 * 2**20, transcendentals=0),
    )(ids, slot_of, arrived, in_hbm(part), in_hbm(coeffs), in_hbm(cond_prec))
    halo_sum = passed_along(halo_back, "blk", -1)
    return pl.pallas_call(
        functools.partial(sum_kernel, capacity),
        name="final_sum",
        out_shape=jax.ShapeDtypeStruct((blocks,) + tile, f32),
        in_specs=[VMEM, VMEM, VMEM, VMEM],
        out_specs=HBM,
        scratch_shapes=[
            pltpu.VMEM((blocks + 1,) + tile, f32),
            pltpu.SMEM((groups, blocks), jnp.int32),
            pltpu.SemaphoreType.DMA((2,)),
        ],
        compiler_params=params(8),
        cost_estimate=pl.CostEstimate(flops=0, bytes_accessed=3 * 2**20, transcendentals=0),
    )(picks, base, halo_sum, returned)


def solution(mesh):
    in_specs = (
        P("blk", None, None),
        P("blk", None, None, None),
        P("blk", None, None),
        P("blk", None),
    )
    return jax.shard_map(
        per_device, mesh=mesh, in_specs=in_specs, out_specs=P("blk", None, None), check_vma=False
    )
```

```python
import functools

import jax
import jax.numpy as jnp
from jax import lax
from jax.experimental import pallas as pl
from jax.experimental.pallas import tpu as pltpu
from jax.sharding import PartitionSpec as P

REACH = 16
CHUNK = 16
AHEAD = 4
HELD = 3
LEAD = 3
STORES = 4
VMEM = pl.BlockSpec(memory_space=pltpu.VMEM)
SMEM = pl.BlockSpec(memory_space=pltpu.SMEM)
HBM = pl.BlockSpec(memory_space=pl.ANY)
NT = (((1,), (1,)), ((), ()))


def params(mib):
    return pltpu.CompilerParams(vmem_limit_bytes=mib * 2**20)


def in_hbm(x):
    return pltpu.with_memory_space_constraint(x, pltpu.HBM)


def passed_along(block, axis, distance):
    size = lax.axis_size(axis)
    return lax.ppermute(block, axis, [((i - distance) % size, i) for i in range(size)])


def earlier_matrix(blocks):
    row = lax.broadcasted_iota(jnp.int32, (blocks, blocks), 0)
    col = lax.broadcasted_iota(jnp.int32, (blocks, blocks), 1)
    return (row < col).astype(jnp.float32).astype(jnp.bfloat16)


def ranks_in(mask, blocks):
    chosen = mask.astype(jnp.float32).astype(jnp.bfloat16)
    return jnp.dot(chosen, earlier_matrix(blocks), preferred_element_type=jnp.float32).astype(jnp.int32)


def prep_kernel(ids_ref, probe_ref, sent_ref, tail_ref, ids, sems):
    blocks = probe_ref.shape[0]
    ids_copy = pltpu.make_async_copy(ids_ref, ids, sems.at[0])
    tail_copy = pltpu.make_async_copy(probe_ref.at[pl.ds(blocks - REACH, REACH)], tail_ref, sems.at[1])
    ids_copy.start()
    tail_copy.start()
    ids_copy.wait()
    sent_ref[...] = jnp.broadcast_to(ids[3:4, :], sent_ref.shape)
    tail_copy.wait()


def pick_kernel(capacity, ids_ref, probe_ref, out_ref, picks_ref, probe, out, picks_smem, sems):
    groups, blocks = ids_ref.shape
    load = pltpu.make_async_copy(probe_ref, probe, sems.at[0])
    load.start()
    me = lax.axis_index("blk")
    local = ids_ref[...] - me * blocks
    mask = (local >= 0) & (local < blocks)
    rank = ranks_in(mask, blocks)
    row = lax.broadcasted_iota(jnp.int32, (picks_ref.shape[0], groups), 0)
    ones = jnp.ones((picks_ref.shape[0], blocks), jnp.bfloat16)
    picks = jnp.zeros(row.shape, jnp.float32)
    for r in range(capacity):
        chosen = jnp.where(mask & (rank == r), local + 1, 0).astype(jnp.float32).astype(jnp.bfloat16)
        found = lax.dot_general(ones, chosen, NT, preferred_element_type=jnp.float32)
        picks = jnp.where(row == r, found, picks)
    picks_ref[:, pl.ds(0, groups)] = picks.astype(jnp.int32)
    copy = pltpu.make_async_copy(picks_ref, picks_smem, sems.at[1])
    copy.start()
    copy.wait()
    load.wait()
    part = groups // STORES

    def store(p):
        rows = pl.ds(p * part * capacity, part * capacity)
        return pltpu.make_async_copy(out.at[rows], out_ref.at[rows], sems.at[2 + p])

    for p in range(STORES):

        @pl.loop(p * part, (p + 1) * part, unroll=8)
        def _(g):
            for r in range(capacity):
                out[g * capacity + r] = probe[jnp.maximum(picks_smem[r, g] - 1, 0)]

        store(p).start()
    for p in range(STORES):
        store(p).wait()


def stacked(mats):
    return mats.reshape(-1, mats.shape[-1])


def apart(left0, left1, mats):
    zero = jnp.zeros_like(left0)
    left = jnp.concatenate(
        [jnp.concatenate([left0, zero], axis=1), jnp.concatenate([zero, left1], axis=1)], axis=0
    )
    out = jnp.dot(left, mats, preferred_element_type=jnp.float32)
    return out.reshape((2,) + (left0.shape[0], mats.shape[1]))


def apart_back(lefts, mats):
    rows, half = lefts.shape[1], mats.shape[0] // 2
    out = lax.dot_general(lefts.reshape(2 * rows, lefts.shape[2]), mats, NT, preferred_element_type=jnp.float32)
    return out[:rows, :half], out[rows:, half:]


def near_place(ids_ref, k, i, first, count):
    place = ids_ref[k, i] - first + REACH
    return jnp.where(place >= count, place - count, place)


def near_forward_kernel(
    groups, capacity, ids_ref, ids_row_ref, halo_ref, probe_ref, coeffs_ref, prec_ref,
    part_ref, own_ref, slot_ref, first_ref, mats_ref, ext, coeffs, prec, part, fold, mats, sems
):
    blocks = probe_ref.shape[0]
    chunks = blocks // CHUNK

    def loads(c):
        own = pl.ds(c * CHUNK, CHUNK)
        return (
            pltpu.make_async_copy(coeffs_ref.at[own], coeffs.at[own], sems.at[0, c]),
            pltpu.make_async_copy(prec_ref.at[own], prec.at[own], sems.at[1, c]),
        )

    def store_part(c):
        own = pl.ds(c * CHUNK, CHUNK)
        return pltpu.make_async_copy(part.at[own], part_ref.at[own], sems.at[2, c])

    def store_mats(c):
        own = pl.ds(c * CHUNK, CHUNK)
        return pltpu.make_async_copy(mats.at[own], mats_ref.at[own], sems.at[3, c])

    own_load = pltpu.make_async_copy(probe_ref, ext.at[pl.ds(REACH, blocks)], sems.at[2, 0])
    own_load.start()

    def fetch(c):
        for load in loads(c):
            load.start()

    def ready(c):
        for load in loads(c):
            load.wait()

    for c in range(LEAD):
        fetch(c)
    ext[pl.ds(0, REACH)] = halo_ref[...]
    owner = ids_row_ref[3:4, :] // blocks
    mask = lax.broadcasted_iota(jnp.int32, (groups, blocks), 0) == owner
    rank = jnp.sum(jnp.where(mask, ranks_in(mask, blocks), 0), axis=0, keepdims=True)
    slot_ref[...] = owner * capacity + rank
    first = lax.axis_index("blk") * blocks
    own_load.wait()

    def make(c):
        for b in range(0, CHUNK, 2):
            i = c * CHUNK + b
            rows = []
            for j in range(2):
                tiles = [ext[near_place(ids_ref, k, i + j, first, groups * blocks)] for k in range(3)]
                rows.append(jnp.concatenate(tiles, axis=1))
            near = [stacked(coeffs[i + j, pl.ds(0, 3)]) for j in range(2)]
            mixed = apart(rows[0], rows[1], jnp.concatenate(near, axis=0))
            part[pl.ds(i, 2)] = ext[pl.ds(REACH + i, 2)].astype(jnp.float32) - mixed
            for j in range(2):
                folded = lax.dot_general(prec[i + j], coeffs[i + j, 3], NT, preferred_element_type=jnp.float32)
                fold[i + j] = folded.astype(jnp.bfloat16)
        store_part(c).start()

    def use(c):
        for b in range(0, CHUNK, 2):
            i = c * CHUNK + b
            halves = []
            for j in range(2):
                high = part[i + j].astype(jnp.bfloat16)
                low = (part[i + j] - high.astype(jnp.float32)).astype(jnp.bfloat16)
                halves.append(jnp.concatenate([high, low], axis=0))
            both = apart(halves[0], halves[1], stacked(fold[pl.ds(i, 2)]))
            rows = both.shape[1] // 2
            own_ref[pl.ds(i, 2)] = both[:, :rows] + both[:, rows:]
            for j in range(2):
                mat = jnp.dot(coeffs[i + j, 3], fold[i + j], preferred_element_type=jnp.float32)
                mats[i + j] = mat.astype(jnp.bfloat16)
        store_mats(c).start()

    ready(0)
    fetch(LEAD)
    make(0)

    @pl.loop(1, chunks)
    def _(c):
        ready(c)

        @pl.when(c + LEAD < chunks)
        def _():
            fetch(c + LEAD)

        use(c - 1)
        make(c)

    use(chunks - 1)
    first_ref[...] = mats[pl.ds(0, HELD * CHUNK)]
    for c in range(chunks):
        store_part(c).wait()
        store_mats(c).wait()


def far_kernel(slots_ref, own_ref, far_ref, first_ref, mats_ref, parcel_ref, mats, slot, sems):
    blocks = own_ref.shape[0]
    chunks = blocks // CHUNK

    def load(c):
        own = pl.ds(c * CHUNK, CHUNK)
        return pltpu.make_async_copy(mats_ref.at[own], mats.at[own], sems.at[c])

    slot_copy = pltpu.make_async_copy(slots_ref, slot, sems.at[0])
    slot_copy.start()
    for c in range(HELD, chunks):
        load(c).start()
    parcel_ref[...] = jnp.zeros_like(parcel_ref)
    slot_copy.wait()

    def send_back(c, pair):
        for b in range(0, CHUNK, 2):
            i = c * CHUNK + b
            terms = own_ref[pl.ds(i, 2)] - apart(far_ref[slot[0, i]], far_ref[slot[0, i + 1]], stacked(pair[pl.ds(i, 2)]))
            for j in range(2):
                parcel_ref[slot[0, i + j]] = terms[j].astype(jnp.bfloat16)

    for c in range(HELD):
        send_back(c, first_ref)

    @pl.loop(HELD, chunks)
    def _(c):
        load(c).wait()
        send_back(c, mats)


def near_back_kernel(
    groups, ids_ref, slot_ref, far_ref, part_ref, coeffs_ref, prec_ref,
    base_ref, halo_ref, total, white, scaled, part, coeffs, prec, sems
):
    blocks = base_ref.shape[0]
    points = base_ref.shape[2]
    chunks = blocks // CHUNK

    def load(c, which):
        own = pl.ds(c * CHUNK, CHUNK)
        source, target = ((part_ref, part), (coeffs_ref, coeffs), (prec_ref, prec))[which]
        return pltpu.make_async_copy(source.at[own], target.at[own], sems.at[which, c])

    def fetch(c):
        for which in range(3):
            load(c, which).start()

    for c in range(LEAD):
        fetch(c)
    total[pl.ds(0, REACH)] = jnp.zeros((REACH,) + total.shape[1:], jnp.float32)
    first = lax.axis_index("blk") * blocks

    def mix(c):
        load(c, 0).wait()
        load(c, 1).wait()
        for b in range(0, CHUNK, 2):
            i = c * CHUNK + b
            mats = jnp.concatenate([coeffs[i, 3], coeffs[i + 1, 3]], axis=0)
            mixed = apart(far_ref[slot_ref[0, i]], far_ref[slot_ref[0, i + 1]], mats)
            white[pl.ds(i, 2)] = (part[pl.ds(i, 2)] - mixed).astype(jnp.bfloat16)

    def scale(c):
        load(c, 2).wait()
        for b in range(0, CHUNK, 2):
            i = c * CHUNK + b
            tiles = apart(white[i], white[i + 1], stacked(prec[pl.ds(i, 2)])).astype(jnp.bfloat16)
            scaled[pl.ds(i, 2)] = tiles
            total[pl.ds(REACH + i, 2)] = tiles.astype(jnp.float32)

    def back(c):
        terms = []
        for b in range(CHUNK + AHEAD):
            if b < CHUNK and b % 2 == 0:
                i = c * CHUNK + b
                mats = [stacked(coeffs[i + j, pl.ds(0, 3)]) for j in range(2)]
                terms.extend(apart_back(scaled[pl.ds(i, 2)], jnp.concatenate(mats, axis=0)))
            if b >= AHEAD:
                i = c * CHUNK + b - AHEAD
                places = [near_place(ids_ref, k, i, first, groups * blocks) for k in range(3)]
                olds = [total[place] for place in places]
                for k in range(3):
                    total[places[k]] = olds[k] - terms[b - AHEAD][:, k * points : (k + 1) * points]

    mix(0)
    fetch(LEAD)
    scale(0)
    mix(1)
    fetch(LEAD + 1)

    @pl.loop(0, chunks - 2)
    def _(c):
        @pl.when(c + LEAD + 2 < chunks)
        def _():
            fetch(c + LEAD + 2)

        back(c)
        scale(c + 1)
        mix(c + 2)

    back(chunks - 2)
    scale(chunks - 1)
    back(chunks - 1)
    halo_ref[...] = total[pl.ds(0, REACH)].astype(halo_ref.dtype)
    base_ref[...] = total[pl.ds(REACH, blocks)]


def sum_kernel(capacity, all_picks_ref, base_ref, halo_ref, back_ref, out_ref, total, picks_ref, sems):
    groups = back_ref.shape[0] // capacity
    picks_copy = pltpu.make_async_copy(all_picks_ref, picks_ref, sems.at[0])
    picks_copy.start()
    blocks = base_ref.shape[0]
    total[pl.ds(0, blocks)] = base_ref[...]
    last = pl.ds(blocks - REACH, REACH)
    total[last] = total[last] + halo_ref[...].astype(jnp.float32)
    picks_copy.wait()

    @pl.loop(0, groups, unroll=8)
    def _(g):
        picks = [picks_ref[r, g] for r in range(capacity)]
        places = [jnp.where(pick > 0, pick - 1, blocks) for pick in picks]
        olds = [total[place] for place in places]
        for r in range(capacity):
            total[places[r]] = olds[r] - back_ref[g * capacity + r].astype(jnp.float32)

    store = pltpu.make_async_copy(total.at[pl.ds(0, blocks)], out_ref, sems.at[1])
    store.start()
    store.wait()


def per_device(probe_vecs, coeffs, cond_prec, neighbours):
    blocks, probes, points = probe_vecs.shape
    groups = lax.axis_size("blk")
    capacity = max(2, blocks // (groups - 1) + 1)
    slots = groups * capacity
    picks_shape = (-(-capacity // 8) * 8, -(-groups // 128) * 128)
    chunks = blocks // CHUNK
    bf16, f32 = jnp.bfloat16, jnp.float32
    tile = (probes, points)
    flops = 2 * blocks * probes * points * points

    def exchange(x):
        return lax.all_to_all(x, "blk", split_axis=0, concat_axis=0, tiled=True)

    ids = neighbours.T
    sent_ids, tail = pl.pallas_call(
        prep_kernel,
        name="prep",
        out_shape=(
            jax.ShapeDtypeStruct((groups, blocks), jnp.int32),
            jax.ShapeDtypeStruct((REACH,) + tile, bf16),
        ),
        in_specs=[HBM, HBM],
        out_specs=(VMEM, VMEM),
        scratch_shapes=[pltpu.VMEM(ids.shape, jnp.int32), pltpu.SemaphoreType.DMA((2,))],
        compiler_params=params(8),
    )(in_hbm(ids), in_hbm(probe_vecs))
    halo = passed_along(tail, "blk", 1)
    all_ids = exchange(sent_ids)
    all_ids, halo = lax.optimization_barrier((all_ids, halo))
    outgoing, picks = pl.pallas_call(
        functools.partial(pick_kernel, capacity),
        name="pick_tiles",
        out_shape=(
            jax.ShapeDtypeStruct((slots,) + tile, bf16),
            jax.ShapeDtypeStruct(picks_shape, jnp.int32),
        ),
        in_specs=[VMEM, HBM],
        out_specs=(HBM, VMEM),
        scratch_shapes=[
            pltpu.VMEM((blocks,) + tile, bf16),
            pltpu.VMEM((slots,) + tile, bf16),
            pltpu.SMEM(picks_shape, jnp.int32),
            pltpu.SemaphoreType.DMA((2 + STORES,)),
        ],
        compiler_params=params(8),
        cost_estimate=pl.CostEstimate(flops=0, bytes_accessed=2 * slots * 4096, transcendentals=0),
    )(all_ids, in_hbm(probe_vecs))
    arrived = exchange(outgoing.reshape((groups, capacity) + tile)).reshape((slots,) + tile)
    mats = (blocks, points, points)
    all_mats = pltpu.VMEM((blocks, 4, points, points), bf16)
    tiles_f32 = jax.ShapeDtypeStruct((blocks,) + tile, f32)
    part, own_far, slot_of, first_mats, far_mats = pl.pallas_call(
        functools.partial(near_forward_kernel, groups, capacity),
        name="near_forward",
        out_shape=(
            pltpu.HBM((blocks,) + tile, f32),
            tiles_f32,
            jax.ShapeDtypeStruct((1, blocks), jnp.int32),
            jax.ShapeDtypeStruct((HELD * CHUNK, points, points), bf16),
            pltpu.HBM(mats, bf16),
        ),
        in_specs=[SMEM, VMEM, VMEM, HBM, HBM, HBM],
        out_specs=(HBM, VMEM, VMEM, VMEM, HBM),
        scratch_shapes=[
            pltpu.VMEM((REACH + blocks,) + tile, bf16),
            all_mats,
            pltpu.VMEM(mats, bf16),
            pltpu.VMEM((blocks,) + tile, f32),
            pltpu.VMEM(mats, bf16),
            pltpu.VMEM(mats, bf16),
            pltpu.SemaphoreType.DMA((4, chunks)),
        ],
        compiler_params=params(40),
        cost_estimate=pl.CostEstimate(flops=20 * flops, bytes_accessed=28 * 2**20, transcendentals=0),
    )(ids, ids, halo, in_hbm(probe_vecs), in_hbm(coeffs), in_hbm(cond_prec))
    parcel = pl.pallas_call(
        far_kernel,
        name="far_terms",
        out_shape=jax.ShapeDtypeStruct((slots,) + tile, bf16),
        in_specs=[VMEM, VMEM, VMEM, VMEM, HBM],
        out_specs=VMEM,
        scratch_shapes=[
            pltpu.VMEM(mats, bf16),
            pltpu.SMEM((1, blocks), jnp.int32),
            pltpu.SemaphoreType.DMA((chunks,)),
        ],
        compiler_params=params(16),
        cost_estimate=pl.CostEstimate(flops=flops, bytes_accessed=6 * 2**20, transcendentals=0),
    )(slot_of, own_far, arrived, first_mats, in_hbm(far_mats))
    parcel, arrived = lax.optimization_barrier((parcel, arrived))
    returned = exchange(parcel.reshape((groups, capacity) + tile)).reshape((slots,) + tile)
    base, halo_back = pl.pallas_call(
        functools.partial(near_back_kernel, groups),
        name="near_back",
        out_shape=(tiles_f32, jax.ShapeDtypeStruct((REACH,) + tile, bf16)),
        in_specs=[SMEM, SMEM, VMEM, HBM, HBM, HBM],
        out_specs=(VMEM, VMEM),
        scratch_shapes=[
            pltpu.VMEM((REACH + blocks,) + tile, f32),
            pltpu.VMEM((blocks,) + tile, bf16),
            pltpu.VMEM((blocks,) + tile, bf16),
            pltpu.VMEM((blocks,) + tile, f32),
            all_mats,
            pltpu.VMEM(mats, bf16),
            pltpu.SemaphoreType.DMA((3, chunks)),
        ],
        compiler_params=params(36),
        cost_estimate=pl.CostEstimate(flops=5 * flops, bytes_accessed=23 * 2**20, transcendentals=0),
    )(ids, slot_of, arrived, in_hbm(part), in_hbm(coeffs), in_hbm(cond_prec))
    halo_sum = passed_along(halo_back, "blk", -1)
    return pl.pallas_call(
        functools.partial(sum_kernel, capacity),
        name="final_sum",
        out_shape=jax.ShapeDtypeStruct((blocks,) + tile, f32),
        in_specs=[VMEM, VMEM, VMEM, VMEM],
        out_specs=HBM,
        scratch_shapes=[
            pltpu.VMEM((blocks + 1,) + tile, f32),
            pltpu.SMEM(picks_shape, jnp.int32),
            pltpu.SemaphoreType.DMA((2,)),
        ],
        compiler_params=params(8),
        cost_estimate=pl.CostEstimate(flops=0, bytes_accessed=3 * 2**20, transcendentals=0),
    )(picks, base, halo_sum, returned)


def solution(mesh):
    in_specs = (
        P("blk", None, None),
        P("blk", None, None, None),
        P("blk", None, None),
        P("blk", None),
    )
    return jax.shard_map(
        per_device, mesh=mesh, in_specs=in_specs, out_specs=P("blk", None, None), check_vma=False
    )
```

```python
import functools

import jax
import jax.numpy as jnp
from jax import lax
from jax.experimental import pallas as pl
from jax.experimental.pallas import tpu as pltpu
from jax.sharding import PartitionSpec as P

REACH = 16
CHUNK = 16
AHEAD = 4
HELD = 3
LEAD = 3
STORES = 4
VMEM = pl.BlockSpec(memory_space=pltpu.VMEM)
SMEM = pl.BlockSpec(memory_space=pltpu.SMEM)
HBM = pl.BlockSpec(memory_space=pl.ANY)
NT = (((1,), (1,)), ((), ()))


def params(mib):
    return pltpu.CompilerParams(vmem_limit_bytes=mib * 2**20)


def in_hbm(x):
    return pltpu.with_memory_space_constraint(x, pltpu.HBM)


def passed_along(block, axis, distance):
    size = lax.axis_size(axis)
    return lax.ppermute(block, axis, [((i - distance) % size, i) for i in range(size)])


def earlier_matrix(blocks):
    row = lax.broadcasted_iota(jnp.int32, (blocks, blocks), 0)
    col = lax.broadcasted_iota(jnp.int32, (blocks, blocks), 1)
    return (row < col).astype(jnp.float32).astype(jnp.bfloat16)


def ranks_in(mask, blocks):
    chosen = mask.astype(jnp.float32).astype(jnp.bfloat16)
    return jnp.dot(chosen, earlier_matrix(blocks), preferred_element_type=jnp.float32).astype(jnp.int32)


def prep_kernel(ids_ref, probe_ref, sent_ref, tail_ref, ids, sems):
    blocks = probe_ref.shape[0]
    ids_copy = pltpu.make_async_copy(ids_ref, ids, sems.at[0])
    tail_copy = pltpu.make_async_copy(probe_ref.at[pl.ds(blocks - REACH, REACH)], tail_ref, sems.at[1])
    ids_copy.start()
    tail_copy.start()
    ids_copy.wait()
    sent_ref[...] = jnp.broadcast_to(ids[3:4, :], sent_ref.shape)
    tail_copy.wait()


def pick_kernel(capacity, ids_ref, probe_ref, out_ref, picks_ref, probe, out, picks_smem, sems):
    groups, blocks = ids_ref.shape
    load = pltpu.make_async_copy(probe_ref, probe, sems.at[0])
    load.start()
    me = lax.axis_index("blk")
    local = ids_ref[...] - me * blocks
    mask = (local >= 0) & (local < blocks)
    rank = ranks_in(mask, blocks)
    row = lax.broadcasted_iota(jnp.int32, (picks_ref.shape[0], groups), 0)
    ones = jnp.ones((picks_ref.shape[0], blocks), jnp.bfloat16)
    picks = jnp.zeros(row.shape, jnp.float32)
    for r in range(capacity):
        chosen = jnp.where(mask & (rank == r), local + 1, 0).astype(jnp.float32).astype(jnp.bfloat16)
        found = lax.dot_general(ones, chosen, NT, preferred_element_type=jnp.float32)
        picks = jnp.where(row == r, found, picks)
    picks_ref[:, pl.ds(0, groups)] = picks.astype(jnp.int32)
    copy = pltpu.make_async_copy(picks_ref, picks_smem, sems.at[1])
    copy.start()
    copy.wait()
    load.wait()
    part = groups // STORES

    def store(p):
        rows = pl.ds(p * part * capacity, part * capacity)
        return pltpu.make_async_copy(out.at[rows], out_ref.at[rows], sems.at[2 + p])

    for p in range(STORES):

        @pl.loop(p * part, (p + 1) * part, unroll=8)
        def _(g):
            for r in range(capacity):
                out[g * capacity + r] = probe[jnp.maximum(picks_smem[r, g] - 1, 0)]

        store(p).start()
    for p in range(STORES):
        store(p).wait()


def stacked(mats):
    return mats.reshape(-1, mats.shape[-1])


def apart(left0, left1, mats):
    zero = jnp.zeros_like(left0)
    left = jnp.concatenate(
        [jnp.concatenate([left0, zero], axis=1), jnp.concatenate([zero, left1], axis=1)], axis=0
    )
    out = jnp.dot(left, mats, preferred_element_type=jnp.float32)
    return out.reshape((2,) + (left0.shape[0], mats.shape[1]))


def apart4(lefts, mats):
    zero = jnp.zeros_like(lefts[0])
    rows = zero.shape[0]
    left = jnp.concatenate(
        [jnp.concatenate([x, zero] if j % 2 == 0 else [zero, x], axis=1) for j, x in enumerate(lefts)], axis=0
    )
    right = jnp.concatenate(
        [jnp.concatenate([mats[0], mats[1]], axis=0), jnp.concatenate([mats[2], mats[3]], axis=0)], axis=1
    )
    out = jnp.dot(left, right, preferred_element_type=jnp.float32)
    half = right.shape[1] // 2
    return [out[j * rows : (j + 1) * rows, (j // 2) * half : (j // 2 + 1) * half] for j in range(4)]


def apart_back(lefts, mats):
    rows, half = lefts.shape[1], mats.shape[0] // 2
    out = lax.dot_general(lefts.reshape(2 * rows, lefts.shape[2]), mats, NT, preferred_element_type=jnp.float32)
    return out[:rows, :half], out[rows:, half:]


def near_place(ids_ref, k, i, first, count):
    place = ids_ref[k, i] - first + REACH
    return jnp.where(place >= count, place - count, place)


def near_forward_kernel(
    groups, capacity, ids_ref, ids_row_ref, halo_ref, probe_ref, coeffs_ref, prec_ref,
    part_ref, own_ref, slot_ref, first_ref, mats_ref, ext, coeffs, prec, part, fold, mats, sems
):
    blocks = probe_ref.shape[0]
    chunks = blocks // CHUNK

    def loads(c):
        own = pl.ds(c * CHUNK, CHUNK)
        return (
            pltpu.make_async_copy(coeffs_ref.at[own], coeffs.at[own], sems.at[0, c]),
            pltpu.make_async_copy(prec_ref.at[own], prec.at[own], sems.at[1, c]),
        )

    def store_part(c):
        own = pl.ds(c * CHUNK, CHUNK)
        return pltpu.make_async_copy(part.at[own], part_ref.at[own], sems.at[2, c])

    def store_mats(c):
        own = pl.ds(c * CHUNK, CHUNK)
        return pltpu.make_async_copy(mats.at[own], mats_ref.at[own], sems.at[3, c])

    own_load = pltpu.make_async_copy(probe_ref, ext.at[pl.ds(REACH, blocks)], sems.at[2, 0])
    own_load.start()

    def fetch(c):
        for load in loads(c):
            load.start()

    def ready(c):
        for load in loads(c):
            load.wait()

    for c in range(LEAD):
        fetch(c)
    ext[pl.ds(0, REACH)] = halo_ref[...]
    owner = ids_row_ref[3:4, :] // blocks
    mask = lax.broadcasted_iota(jnp.int32, (groups, blocks), 0) == owner
    rank = jnp.sum(jnp.where(mask, ranks_in(mask, blocks), 0), axis=0, keepdims=True)
    slot_ref[...] = owner * capacity + rank
    first = lax.axis_index("blk") * blocks
    own_load.wait()

    def make(c):
        for b in range(0, CHUNK, 2):
            i = c * CHUNK + b
            rows = []
            for j in range(2):
                tiles = [ext[near_place(ids_ref, k, i + j, first, groups * blocks)] for k in range(3)]
                rows.append(jnp.concatenate(tiles, axis=1))
            near = [stacked(coeffs[i + j, pl.ds(0, 3)]) for j in range(2)]
            mixed = apart(rows[0], rows[1], jnp.concatenate(near, axis=0))
            part[pl.ds(i, 2)] = ext[pl.ds(REACH + i, 2)].astype(jnp.float32) - mixed
            for j in range(2):
                folded = lax.dot_general(prec[i + j], coeffs[i + j, 3], NT, preferred_element_type=jnp.float32)
                fold[i + j] = folded.astype(jnp.bfloat16)
        store_part(c).start()

    def use(c):
        for b in range(0, CHUNK, 2):
            i = c * CHUNK + b
            halves = []
            for j in range(2):
                high = part[i + j].astype(jnp.bfloat16)
                low = (part[i + j] - high.astype(jnp.float32)).astype(jnp.bfloat16)
                halves.append(jnp.concatenate([high, low], axis=0))
            both = apart(halves[0], halves[1], stacked(fold[pl.ds(i, 2)]))
            rows = both.shape[1] // 2
            own_ref[pl.ds(i, 2)] = both[:, :rows] + both[:, rows:]
            for j in range(2):
                mat = jnp.dot(coeffs[i + j, 3], fold[i + j], preferred_element_type=jnp.float32)
                mats[i + j] = mat.astype(jnp.bfloat16)
        store_mats(c).start()

    ready(0)
    fetch(LEAD)
    make(0)

    @pl.loop(1, chunks)
    def _(c):
        ready(c)

        @pl.when(c + LEAD < chunks)
        def _():
            fetch(c + LEAD)

        use(c - 1)
        make(c)

    use(chunks - 1)
    first_ref[...] = mats[pl.ds(0, HELD * CHUNK)]
    for c in range(chunks):
        store_part(c).wait()
        store_mats(c).wait()


def far_kernel(slots_ref, own_ref, far_ref, first_ref, mats_ref, parcel_ref, mats, slot, sems):
    blocks = own_ref.shape[0]
    chunks = blocks // CHUNK

    def load(c):
        own = pl.ds(c * CHUNK, CHUNK)
        return pltpu.make_async_copy(mats_ref.at[own], mats.at[own], sems.at[c])

    slot_copy = pltpu.make_async_copy(slots_ref, slot, sems.at[0])
    slot_copy.start()
    for c in range(HELD, chunks):
        load(c).start()
    parcel_ref[...] = jnp.zeros_like(parcel_ref)
    slot_copy.wait()

    def send_back(c, pair):
        for b in range(0, CHUNK, 4):
            i = c * CHUNK + b
            mixed = apart4([far_ref[slot[0, i + j]] for j in range(4)], [pair[i + j] for j in range(4)])
            for j in range(4):
                parcel_ref[slot[0, i + j]] = (own_ref[i + j] - mixed[j]).astype(jnp.bfloat16)

    for c in range(HELD):
        send_back(c, first_ref)

    @pl.loop(HELD, chunks)
    def _(c):
        load(c).wait()
        send_back(c, mats)


def near_back_kernel(
    groups, ids_ref, slot_ref, far_ref, part_ref, coeffs_ref, prec_ref,
    base_ref, halo_ref, total, white, scaled, part, coeffs, prec, sems
):
    blocks = base_ref.shape[0]
    points = base_ref.shape[2]
    chunks = blocks // CHUNK

    def load(c, which):
        own = pl.ds(c * CHUNK, CHUNK)
        source, target = (
            (part_ref.at[own], part.at[own]),
            (coeffs_ref.at[own, 3], coeffs.at[own, 3]),
            (prec_ref.at[own], prec.at[own]),
            (coeffs_ref.at[own, pl.ds(0, 3)], coeffs.at[own, pl.ds(0, 3)]),
        )[which]
        return pltpu.make_async_copy(source, target, sems.at[which, c])

    def fetch(c):
        for which in range(4):
            load(c, which).start()

    for c in range(LEAD):
        fetch(c)
    total[pl.ds(0, REACH)] = jnp.zeros((REACH,) + total.shape[1:], jnp.float32)
    first = lax.axis_index("blk") * blocks

    def mix(c):
        load(c, 0).wait()
        load(c, 1).wait()
        for b in range(0, CHUNK, 4):
            i = c * CHUNK + b
            mixed = apart4([far_ref[slot_ref[0, i + j]] for j in range(4)], [coeffs[i + j, 3] for j in range(4)])
            for j in range(4):
                white[i + j] = (part[i + j] - mixed[j]).astype(jnp.bfloat16)

    def scale(c):
        load(c, 2).wait()
        for b in range(0, CHUNK, 4):
            i = c * CHUNK + b
            tiles = apart4([white[i + j] for j in range(4)], [prec[i + j] for j in range(4)])
            for j in range(4):
                scaled[i + j] = tiles[j].astype(jnp.bfloat16)
                total[REACH + i + j] = scaled[i + j].astype(jnp.float32)

    def back(c):
        load(c, 3).wait()
        terms = []
        for b in range(CHUNK + AHEAD):
            if b < CHUNK and b % 2 == 0:
                i = c * CHUNK + b
                mats = [stacked(coeffs[i + j, pl.ds(0, 3)]) for j in range(2)]
                terms.extend(apart_back(scaled[pl.ds(i, 2)], jnp.concatenate(mats, axis=0)))
            if b >= AHEAD:
                i = c * CHUNK + b - AHEAD
                places = [near_place(ids_ref, k, i, first, groups * blocks) for k in range(3)]
                olds = [total[place] for place in places]
                for k in range(3):
                    total[places[k]] = olds[k] - terms[b - AHEAD][:, k * points : (k + 1) * points]

    mix(0)
    fetch(LEAD)
    scale(0)
    mix(1)
    fetch(LEAD + 1)

    @pl.loop(0, chunks - 2)
    def _(c):
        @pl.when(c + LEAD + 2 < chunks)
        def _():
            fetch(c + LEAD + 2)

        back(c)
        scale(c + 1)
        mix(c + 2)

    back(chunks - 2)
    scale(chunks - 1)
    back(chunks - 1)
    halo_ref[...] = total[pl.ds(0, REACH)].astype(halo_ref.dtype)
    base_ref[...] = total[pl.ds(REACH, blocks)]


def sum_kernel(capacity, all_picks_ref, base_ref, halo_ref, back_ref, out_ref, total, picks_ref, sems):
    groups = back_ref.shape[0] // capacity
    picks_copy = pltpu.make_async_copy(all_picks_ref, picks_ref, sems.at[0])
    picks_copy.start()
    blocks = base_ref.shape[0]
    total[pl.ds(0, blocks)] = base_ref[...]
    last = pl.ds(blocks - REACH, REACH)
    total[last] = total[last] + halo_ref[...].astype(jnp.float32)
    picks_copy.wait()

    @pl.loop(0, groups, unroll=8)
    def _(g):
        picks = [picks_ref[r, g] for r in range(capacity)]
        places = [jnp.where(pick > 0, pick - 1, blocks) for pick in picks]
        olds = [total[place] for place in places]
        for r in range(capacity):
            total[places[r]] = olds[r] - back_ref[g * capacity + r].astype(jnp.float32)

    store = pltpu.make_async_copy(total.at[pl.ds(0, blocks)], out_ref, sems.at[1])
    store.start()
    store.wait()


def per_device(probe_vecs, coeffs, cond_prec, neighbours):
    blocks, probes, points = probe_vecs.shape
    groups = lax.axis_size("blk")
    capacity = max(2, blocks // (groups - 1) + 1)
    slots = groups * capacity
    picks_shape = (-(-capacity // 8) * 8, -(-groups // 128) * 128)
    chunks = blocks // CHUNK
    bf16, f32 = jnp.bfloat16, jnp.float32
    tile = (probes, points)
    flops = 2 * blocks * probes * points * points

    def exchange(x):
        return lax.all_to_all(x, "blk", split_axis=0, concat_axis=0, tiled=True)

    ids = neighbours.T
    sent_ids, tail = pl.pallas_call(
        prep_kernel,
        name="prep",
        out_shape=(
            jax.ShapeDtypeStruct((groups, blocks), jnp.int32),
            jax.ShapeDtypeStruct((REACH,) + tile, bf16),
        ),
        in_specs=[HBM, HBM],
        out_specs=(VMEM, VMEM),
        scratch_shapes=[pltpu.VMEM(ids.shape, jnp.int32), pltpu.SemaphoreType.DMA((2,))],
        compiler_params=params(8),
    )(in_hbm(ids), in_hbm(probe_vecs))
    halo = passed_along(tail, "blk", 1)
    all_ids = exchange(sent_ids)
    all_ids, halo = lax.optimization_barrier((all_ids, halo))
    outgoing, picks = pl.pallas_call(
        functools.partial(pick_kernel, capacity),
        name="pick_tiles",
        out_shape=(
            jax.ShapeDtypeStruct((slots,) + tile, bf16),
            jax.ShapeDtypeStruct(picks_shape, jnp.int32),
        ),
        in_specs=[VMEM, HBM],
        out_specs=(HBM, VMEM),
        scratch_shapes=[
            pltpu.VMEM((blocks,) + tile, bf16),
            pltpu.VMEM((slots,) + tile, bf16),
            pltpu.SMEM(picks_shape, jnp.int32),
            pltpu.SemaphoreType.DMA((2 + STORES,)),
        ],
        compiler_params=params(8),
        cost_estimate=pl.CostEstimate(flops=0, bytes_accessed=2 * slots * 4096, transcendentals=0),
    )(all_ids, in_hbm(probe_vecs))
    arrived = exchange(outgoing.reshape((groups, capacity) + tile)).reshape((slots,) + tile)
    mats = (blocks, points, points)
    all_mats = pltpu.VMEM((blocks, 4, points, points), bf16)
    tiles_f32 = jax.ShapeDtypeStruct((blocks,) + tile, f32)
    part, own_far, slot_of, first_mats, far_mats = pl.pallas_call(
        functools.partial(near_forward_kernel, groups, capacity),
        name="near_forward",
        out_shape=(
            pltpu.HBM((blocks,) + tile, f32),
            tiles_f32,
            jax.ShapeDtypeStruct((1, blocks), jnp.int32),
            jax.ShapeDtypeStruct((HELD * CHUNK, points, points), bf16),
            pltpu.HBM(mats, bf16),
        ),
        in_specs=[SMEM, VMEM, VMEM, HBM, HBM, HBM],
        out_specs=(HBM, VMEM, VMEM, VMEM, HBM),
        scratch_shapes=[
            pltpu.VMEM((REACH + blocks,) + tile, bf16),
            all_mats,
            pltpu.VMEM(mats, bf16),
            pltpu.VMEM((blocks,) + tile, f32),
            pltpu.VMEM(mats, bf16),
            pltpu.VMEM(mats, bf16),
            pltpu.SemaphoreType.DMA((4, chunks)),
        ],
        compiler_params=params(40),
        cost_estimate=pl.CostEstimate(flops=20 * flops, bytes_accessed=28 * 2**20, transcendentals=0),
    )(ids, ids, halo, in_hbm(probe_vecs), in_hbm(coeffs), in_hbm(cond_prec))
    parcel = pl.pallas_call(
        far_kernel,
        name="far_terms",
        out_shape=jax.ShapeDtypeStruct((slots,) + tile, bf16),
        in_specs=[VMEM, VMEM, VMEM, VMEM, HBM],
        out_specs=VMEM,
        scratch_shapes=[
            pltpu.VMEM(mats, bf16),
            pltpu.SMEM((1, blocks), jnp.int32),
            pltpu.SemaphoreType.DMA((chunks,)),
        ],
        compiler_params=params(16),
        cost_estimate=pl.CostEstimate(flops=flops, bytes_accessed=6 * 2**20, transcendentals=0),
    )(slot_of, own_far, arrived, first_mats, in_hbm(far_mats))
    parcel, arrived = lax.optimization_barrier((parcel, arrived))
    returned = exchange(parcel.reshape((groups, capacity) + tile)).reshape((slots,) + tile)
    base, halo_back = pl.pallas_call(
        functools.partial(near_back_kernel, groups),
        name="near_back",
        out_shape=(tiles_f32, jax.ShapeDtypeStruct((REACH,) + tile, bf16)),
        in_specs=[SMEM, SMEM, VMEM, HBM, HBM, HBM],
        out_specs=(VMEM, VMEM),
        scratch_shapes=[
            pltpu.VMEM((REACH + blocks,) + tile, f32),
            pltpu.VMEM((blocks,) + tile, bf16),
            pltpu.VMEM((blocks,) + tile, bf16),
            pltpu.VMEM((blocks,) + tile, f32),
            all_mats,
            pltpu.VMEM(mats, bf16),
            pltpu.SemaphoreType.DMA((4, chunks)),
        ],
        compiler_params=params(36),
        cost_estimate=pl.CostEstimate(flops=5 * flops, bytes_accessed=23 * 2**20, transcendentals=0),
    )(ids, slot_of, arrived, in_hbm(part), in_hbm(coeffs), in_hbm(cond_prec))
    halo_sum = passed_along(halo_back, "blk", -1)
    return pl.pallas_call(
        functools.partial(sum_kernel, capacity),
        name="final_sum",
        out_shape=jax.ShapeDtypeStruct((blocks,) + tile, f32),
        in_specs=[VMEM, VMEM, VMEM, VMEM],
        out_specs=HBM,
        scratch_shapes=[
            pltpu.VMEM((blocks + 1,) + tile, f32),
            pltpu.SMEM(picks_shape, jnp.int32),
            pltpu.SemaphoreType.DMA((2,)),
        ],
        compiler_params=params(8),
        cost_estimate=pl.CostEstimate(flops=0, bytes_accessed=3 * 2**20, transcendentals=0),
    )(picks, base, halo_sum, returned)


def solution(mesh):
    in_specs = (
        P("blk", None, None),
        P("blk", None, None, None),
        P("blk", None, None),
        P("blk", None),
    )
    return jax.shard_map(
        per_device, mesh=mesh, in_specs=in_specs, out_specs=P("blk", None, None), check_vma=False
    )
```

```python
import functools

import jax
import jax.numpy as jnp
from jax import lax
from jax.experimental import pallas as pl
from jax.experimental.pallas import tpu as pltpu
from jax.sharding import PartitionSpec as P

REACH = 16
CHUNK = 16
AHEAD = 8
WIDTH = 8
HELD = 3
LEAD = 3
STORES = 4
VMEM = pl.BlockSpec(memory_space=pltpu.VMEM)
SMEM = pl.BlockSpec(memory_space=pltpu.SMEM)
HBM = pl.BlockSpec(memory_space=pl.ANY)
NT = (((1,), (1,)), ((), ()))


def params(mib):
    return pltpu.CompilerParams(vmem_limit_bytes=mib * 2**20)


def in_hbm(x):
    return pltpu.with_memory_space_constraint(x, pltpu.HBM)


def passed_along(block, axis, distance):
    size = lax.axis_size(axis)
    return lax.ppermute(block, axis, [((i - distance) % size, i) for i in range(size)])


def earlier_matrix(blocks):
    row = lax.broadcasted_iota(jnp.int32, (blocks, blocks), 0)
    col = lax.broadcasted_iota(jnp.int32, (blocks, blocks), 1)
    return (row < col).astype(jnp.float32).astype(jnp.bfloat16)


def ranks_in(mask, blocks):
    chosen = mask.astype(jnp.float32).astype(jnp.bfloat16)
    return jnp.dot(chosen, earlier_matrix(blocks), preferred_element_type=jnp.float32).astype(jnp.int32)


def prep_kernel(ids_ref, probe_ref, sent_ref, tail_ref, ids, sems):
    blocks = probe_ref.shape[0]
    ids_copy = pltpu.make_async_copy(ids_ref, ids, sems.at[0])
    tail_copy = pltpu.make_async_copy(probe_ref.at[pl.ds(blocks - REACH, REACH)], tail_ref, sems.at[1])
    ids_copy.start()
    tail_copy.start()
    ids_copy.wait()
    sent_ref[...] = jnp.broadcast_to(ids[3:4, :], sent_ref.shape)
    tail_copy.wait()


def pick_kernel(capacity, ids_ref, probe_ref, out_ref, picks_ref, probe, out, picks_smem, sems):
    groups, blocks = ids_ref.shape
    load = pltpu.make_async_copy(probe_ref, probe, sems.at[0])
    load.start()
    me = lax.axis_index("blk")
    local = ids_ref[...] - me * blocks
    mask = (local >= 0) & (local < blocks)
    rank = ranks_in(mask, blocks)
    row = lax.broadcasted_iota(jnp.int32, (picks_ref.shape[0], groups), 0)
    ones = jnp.ones((picks_ref.shape[0], blocks), jnp.bfloat16)
    picks = jnp.zeros(row.shape, jnp.float32)
    for r in range(capacity):
        chosen = jnp.where(mask & (rank == r), local + 1, 0).astype(jnp.float32).astype(jnp.bfloat16)
        found = lax.dot_general(ones, chosen, NT, preferred_element_type=jnp.float32)
        picks = jnp.where(row == r, found, picks)
    picks_ref[:, pl.ds(0, groups)] = picks.astype(jnp.int32)
    copy = pltpu.make_async_copy(picks_ref, picks_smem, sems.at[1])
    copy.start()
    copy.wait()
    load.wait()
    part = groups // STORES

    def store(p):
        rows = pl.ds(p * part * capacity, part * capacity)
        return pltpu.make_async_copy(out.at[rows], out_ref.at[rows], sems.at[2 + p])

    for p in range(STORES):

        @pl.loop(p * part, (p + 1) * part, unroll=8)
        def _(g):
            for r in range(capacity):
                out[g * capacity + r] = probe[jnp.maximum(picks_smem[r, g] - 1, 0)]

        store(p).start()
    for p in range(STORES):
        store(p).wait()


def stacked(mats):
    return mats.reshape(-1, mats.shape[-1])


def apart(left0, left1, mats):
    zero = jnp.zeros_like(left0)
    left = jnp.concatenate(
        [jnp.concatenate([left0, zero], axis=1), jnp.concatenate([zero, left1], axis=1)], axis=0
    )
    out = jnp.dot(left, mats, preferred_element_type=jnp.float32)
    return out.reshape((2,) + (left0.shape[0], mats.shape[1]))


def apart4(lefts, mats):
    zero = jnp.zeros_like(lefts[0])
    rows = zero.shape[0]
    left = jnp.concatenate(
        [jnp.concatenate([x, zero] if j % 2 == 0 else [zero, x], axis=1) for j, x in enumerate(lefts)], axis=0
    )
    right = jnp.concatenate(
        [jnp.concatenate([mats[0], mats[1]], axis=0), jnp.concatenate([mats[2], mats[3]], axis=0)], axis=1
    )
    out = jnp.dot(left, right, preferred_element_type=jnp.float32)
    half = right.shape[1] // 2
    return [out[j * rows : (j + 1) * rows, (j // 2) * half : (j // 2 + 1) * half] for j in range(4)]


def streamed(tiles, mats):
    rows = tiles[0].shape[0]
    size = mats.shape[1]
    out = lax.dot_general(stacked(mats), jnp.concatenate(tiles, axis=0), NT, preferred_element_type=jnp.float32)
    owner = lax.broadcasted_iota(jnp.int32, (size, rows * len(tiles)), 1) // rows
    kept = out[:size]
    for j in range(1, len(tiles)):
        kept = jnp.where(owner == j, out[j * size : (j + 1) * size], kept)
    return kept.T.reshape(len(tiles), rows, size)


def apart_back(lefts, mats):
    rows, half = lefts.shape[1], mats.shape[0] // 2
    out = lax.dot_general(lefts.reshape(2 * rows, lefts.shape[2]), mats, NT, preferred_element_type=jnp.float32)
    return out[:rows, :half], out[rows:, half:]


def near_place(ids_ref, k, i, first, count):
    place = ids_ref[k, i] - first + REACH
    return jnp.where(place >= count, place - count, place)


def near_forward_kernel(
    groups, capacity, ids_ref, ids_row_ref, halo_ref, probe_ref, coeffs_ref, prec_ref,
    part_ref, own_ref, slot_ref, first_ref, mats_ref, ext, coeffs, prec, part, fold, mats, sems
):
    blocks = probe_ref.shape[0]
    chunks = blocks // CHUNK

    def loads(c):
        own = pl.ds(c * CHUNK, CHUNK)
        return (
            pltpu.make_async_copy(coeffs_ref.at[own], coeffs.at[own], sems.at[0, c]),
            pltpu.make_async_copy(prec_ref.at[own], prec.at[own], sems.at[1, c]),
        )

    def store_part(c):
        own = pl.ds(c * CHUNK, CHUNK)
        return pltpu.make_async_copy(part.at[own], part_ref.at[own], sems.at[2, c])

    def store_mats(c):
        own = pl.ds(c * CHUNK, CHUNK)
        return pltpu.make_async_copy(mats.at[own], mats_ref.at[own], sems.at[3, c])

    own_load = pltpu.make_async_copy(probe_ref, ext.at[pl.ds(REACH, blocks)], sems.at[2, 0])
    own_load.start()

    def fetch(c):
        for load in loads(c):
            load.start()

    def ready(c):
        for load in loads(c):
            load.wait()

    for c in range(LEAD):
        fetch(c)
    ext[pl.ds(0, REACH)] = halo_ref[...]
    owner = ids_row_ref[3:4, :] // blocks
    mask = lax.broadcasted_iota(jnp.int32, (groups, blocks), 0) == owner
    rank = jnp.sum(jnp.where(mask, ranks_in(mask, blocks), 0), axis=0, keepdims=True)
    slot_ref[...] = owner * capacity + rank
    first = lax.axis_index("blk") * blocks
    own_load.wait()

    def make(c):
        for b in range(0, CHUNK, 2):
            i = c * CHUNK + b
            rows = []
            for j in range(2):
                tiles = [ext[near_place(ids_ref, k, i + j, first, groups * blocks)] for k in range(3)]
                rows.append(jnp.concatenate(tiles, axis=1))
            near = [stacked(coeffs[i + j, pl.ds(0, 3)]) for j in range(2)]
            mixed = apart(rows[0], rows[1], jnp.concatenate(near, axis=0))
            part[pl.ds(i, 2)] = ext[pl.ds(REACH + i, 2)].astype(jnp.float32) - mixed
            for j in range(2):
                folded = lax.dot_general(coeffs[i + j, 3], prec[i + j], NT, preferred_element_type=jnp.float32)
                fold[i + j] = folded.astype(jnp.bfloat16)
        store_part(c).start()

    def use(c):
        for b in range(0, CHUNK, 2):
            i = c * CHUNK + b
            halves = []
            for j in range(2):
                high = part[i + j].astype(jnp.bfloat16)
                low = (part[i + j] - high.astype(jnp.float32)).astype(jnp.bfloat16)
                halves.append(jnp.concatenate([high, low], axis=0)[None])
            both = apart_back(jnp.concatenate(halves, axis=0), stacked(fold[pl.ds(i, 2)]))
            for j in range(2):
                rows = both[j].shape[0] // 2
                own_ref[i + j] = both[j][:rows] + both[j][rows:]
                mat = lax.dot_general(fold[i + j], coeffs[i + j, 3], NT, preferred_element_type=jnp.float32)
                mats[i + j] = mat.astype(jnp.bfloat16)
        store_mats(c).start()

    ready(0)
    fetch(LEAD)
    make(0)

    @pl.loop(1, chunks)
    def _(c):
        ready(c)

        @pl.when(c + LEAD < chunks)
        def _():
            fetch(c + LEAD)

        use(c - 1)
        make(c)

    use(chunks - 1)
    first_ref[...] = mats[pl.ds(0, HELD * CHUNK)]
    for c in range(chunks):
        store_part(c).wait()
        store_mats(c).wait()


def far_kernel(slots_ref, own_ref, far_ref, first_ref, mats_ref, parcel_ref, mats, slot, sems):
    blocks = own_ref.shape[0]
    chunks = blocks // CHUNK

    def load(c):
        own = pl.ds(c * CHUNK, CHUNK)
        return pltpu.make_async_copy(mats_ref.at[own], mats.at[own], sems.at[c])

    slot_copy = pltpu.make_async_copy(slots_ref, slot, sems.at[0])
    slot_copy.start()
    for c in range(HELD, chunks):
        load(c).start()
    parcel_ref[...] = jnp.zeros_like(parcel_ref)
    slot_copy.wait()

    def send_back(c, pair):
        for b in range(0, CHUNK, WIDTH):
            i = c * CHUNK + b
            mixed = streamed([far_ref[slot[0, i + j]] for j in range(WIDTH)], pair[pl.ds(i, WIDTH)])
            for j in range(WIDTH):
                parcel_ref[slot[0, i + j]] = (own_ref[i + j] - mixed[j]).astype(jnp.bfloat16)

    for c in range(HELD):
        send_back(c, first_ref)

    @pl.loop(HELD, chunks)
    def _(c):
        load(c).wait()
        send_back(c, mats)


def near_back_kernel(
    groups, ids_ref, slot_ref, far_ref, part_ref, coeffs_ref, prec_ref,
    base_ref, halo_ref, total, white, scaled, part, coeffs, prec, sems
):
    blocks = base_ref.shape[0]
    chunks = blocks // CHUNK

    def load(c, which):
        own = pl.ds(c * CHUNK, CHUNK)
        source, target = (
            (part_ref.at[own], part.at[own]),
            (coeffs_ref.at[own, 3], coeffs.at[own, 3]),
            (prec_ref.at[own], prec.at[own]),
            (coeffs_ref.at[own, pl.ds(0, 3)], coeffs.at[own, pl.ds(0, 3)]),
        )[which]
        return pltpu.make_async_copy(source, target, sems.at[which, c])

    def fetch(c):
        for which in range(4):
            load(c, which).start()

    for c in range(LEAD):
        fetch(c)
    total[pl.ds(0, REACH)] = jnp.zeros((REACH,) + total.shape[1:], jnp.float32)
    first = lax.axis_index("blk") * blocks

    def mix(c):
        load(c, 0).wait()
        load(c, 1).wait()
        for b in range(0, CHUNK, 4):
            i = c * CHUNK + b
            mixed = apart4([far_ref[slot_ref[0, i + j]] for j in range(4)], [coeffs[i + j, 3] for j in range(4)])
            for j in range(4):
                white[i + j] = (part[i + j] - mixed[j]).astype(jnp.bfloat16)

    def scale(c):
        load(c, 2).wait()
        for b in range(0, CHUNK, 4):
            i = c * CHUNK + b
            tiles = apart4([white[i + j] for j in range(4)], [prec[i + j] for j in range(4)])
            for j in range(4):
                scaled[i + j] = tiles[j].astype(jnp.bfloat16)
                total[REACH + i + j] = scaled[i + j].astype(jnp.float32)

    def back(c):
        load(c, 3).wait()
        terms = []
        for b in range(CHUNK + AHEAD):
            if b < CHUNK and b % WIDTH == 0:
                i = c * CHUNK + b
                tiles = [scaled[i + j] for j in range(WIDTH)]
                terms.append([streamed(tiles, coeffs[pl.ds(i, WIDTH), k]) for k in range(3)])
            if b >= AHEAD:
                i = c * CHUNK + b - AHEAD
                places = [near_place(ids_ref, k, i, first, groups * blocks) for k in range(3)]
                olds = [total[place] for place in places]
                for k in range(3):
                    total[places[k]] = olds[k] - terms[(b - AHEAD) // WIDTH][k][(b - AHEAD) % WIDTH]

    mix(0)
    fetch(LEAD)
    scale(0)
    mix(1)
    fetch(LEAD + 1)

    @pl.loop(0, chunks - 2)
    def _(c):
        @pl.when(c + LEAD + 2 < chunks)
        def _():
            fetch(c + LEAD + 2)

        back(c)
        scale(c + 1)
        mix(c + 2)

    back(chunks - 2)
    scale(chunks - 1)
    back(chunks - 1)
    halo_ref[...] = total[pl.ds(0, REACH)].astype(halo_ref.dtype)
    base_ref[...] = total[pl.ds(REACH, blocks)]


def sum_kernel(capacity, all_picks_ref, base_ref, halo_ref, back_ref, out_ref, total, picks_ref, sems):
    groups = back_ref.shape[0] // capacity
    picks_copy = pltpu.make_async_copy(all_picks_ref, picks_ref, sems.at[0])
    picks_copy.start()
    blocks = base_ref.shape[0]
    total[pl.ds(0, blocks)] = base_ref[...]
    last = pl.ds(blocks - REACH, REACH)
    total[last] = total[last] + halo_ref[...].astype(jnp.float32)
    picks_copy.wait()

    @pl.loop(0, groups, unroll=8)
    def _(g):
        picks = [picks_ref[r, g] for r in range(capacity)]
        places = [jnp.where(pick > 0, pick - 1, blocks) for pick in picks]
        olds = [total[place] for place in places]
        for r in range(capacity):
            total[places[r]] = olds[r] - back_ref[g * capacity + r].astype(jnp.float32)

    store = pltpu.make_async_copy(total.at[pl.ds(0, blocks)], out_ref, sems.at[1])
    store.start()
    store.wait()


def per_device(probe_vecs, coeffs, cond_prec, neighbours):
    blocks, probes, points = probe_vecs.shape
    groups = lax.axis_size("blk")
    capacity = max(2, blocks // (groups - 1) + 1)
    slots = groups * capacity
    picks_shape = (-(-capacity // 8) * 8, -(-groups // 128) * 128)
    chunks = blocks // CHUNK
    bf16, f32 = jnp.bfloat16, jnp.float32
    tile = (probes, points)
    flops = 2 * blocks * probes * points * points

    def exchange(x):
        return lax.all_to_all(x, "blk", split_axis=0, concat_axis=0, tiled=True)

    ids = neighbours.T
    sent_ids, tail = pl.pallas_call(
        prep_kernel,
        name="prep",
        out_shape=(
            jax.ShapeDtypeStruct((groups, blocks), jnp.int32),
            jax.ShapeDtypeStruct((REACH,) + tile, bf16),
        ),
        in_specs=[HBM, HBM],
        out_specs=(VMEM, VMEM),
        scratch_shapes=[pltpu.VMEM(ids.shape, jnp.int32), pltpu.SemaphoreType.DMA((2,))],
        compiler_params=params(8),
    )(in_hbm(ids), in_hbm(probe_vecs))
    halo = passed_along(tail, "blk", 1)
    all_ids = exchange(sent_ids)
    all_ids, halo = lax.optimization_barrier((all_ids, halo))
    outgoing, picks = pl.pallas_call(
        functools.partial(pick_kernel, capacity),
        name="pick_tiles",
        out_shape=(
            jax.ShapeDtypeStruct((slots,) + tile, bf16),
            jax.ShapeDtypeStruct(picks_shape, jnp.int32),
        ),
        in_specs=[VMEM, HBM],
        out_specs=(HBM, VMEM),
        scratch_shapes=[
            pltpu.VMEM((blocks,) + tile, bf16),
            pltpu.VMEM((slots,) + tile, bf16),
            pltpu.SMEM(picks_shape, jnp.int32),
            pltpu.SemaphoreType.DMA((2 + STORES,)),
        ],
        compiler_params=params(8),
        cost_estimate=pl.CostEstimate(flops=0, bytes_accessed=2 * slots * 4096, transcendentals=0),
    )(all_ids, in_hbm(probe_vecs))
    arrived = exchange(outgoing.reshape((groups, capacity) + tile)).reshape((slots,) + tile)
    mats = (blocks, points, points)
    all_mats = pltpu.VMEM((blocks, 4, points, points), bf16)
    tiles_f32 = jax.ShapeDtypeStruct((blocks,) + tile, f32)
    part, own_far, slot_of, first_mats, far_mats = pl.pallas_call(
        functools.partial(near_forward_kernel, groups, capacity),
        name="near_forward",
        out_shape=(
            pltpu.HBM((blocks,) + tile, f32),
            tiles_f32,
            jax.ShapeDtypeStruct((1, blocks), jnp.int32),
            jax.ShapeDtypeStruct((HELD * CHUNK, points, points), bf16),
            pltpu.HBM(mats, bf16),
        ),
        in_specs=[SMEM, VMEM, VMEM, HBM, HBM, HBM],
        out_specs=(HBM, VMEM, VMEM, VMEM, HBM),
        scratch_shapes=[
            pltpu.VMEM((REACH + blocks,) + tile, bf16),
            all_mats,
            pltpu.VMEM(mats, bf16),
            pltpu.VMEM((blocks,) + tile, f32),
            pltpu.VMEM(mats, bf16),
            pltpu.VMEM(mats, bf16),
            pltpu.SemaphoreType.DMA((4, chunks)),
        ],
        compiler_params=params(40),
        cost_estimate=pl.CostEstimate(flops=20 * flops, bytes_accessed=28 * 2**20, transcendentals=0),
    )(ids, ids, halo, in_hbm(probe_vecs), in_hbm(coeffs), in_hbm(cond_prec))
    parcel = pl.pallas_call(
        far_kernel,
        name="far_terms",
        out_shape=jax.ShapeDtypeStruct((slots,) + tile, bf16),
        in_specs=[VMEM, VMEM, VMEM, VMEM, HBM],
        out_specs=VMEM,
        scratch_shapes=[
            pltpu.VMEM(mats, bf16),
            pltpu.SMEM((1, blocks), jnp.int32),
            pltpu.SemaphoreType.DMA((chunks,)),
        ],
        compiler_params=params(16),
        cost_estimate=pl.CostEstimate(flops=flops, bytes_accessed=6 * 2**20, transcendentals=0),
    )(slot_of, own_far, arrived, first_mats, in_hbm(far_mats))
    parcel, arrived = lax.optimization_barrier((parcel, arrived))
    returned = exchange(parcel.reshape((groups, capacity) + tile)).reshape((slots,) + tile)
    base, halo_back = pl.pallas_call(
        functools.partial(near_back_kernel, groups),
        name="near_back",
        out_shape=(tiles_f32, jax.ShapeDtypeStruct((REACH,) + tile, bf16)),
        in_specs=[SMEM, SMEM, VMEM, HBM, HBM, HBM],
        out_specs=(VMEM, VMEM),
        scratch_shapes=[
            pltpu.VMEM((REACH + blocks,) + tile, f32),
            pltpu.VMEM((blocks,) + tile, bf16),
            pltpu.VMEM((blocks,) + tile, bf16),
            pltpu.VMEM((blocks,) + tile, f32),
            all_mats,
            pltpu.VMEM(mats, bf16),
            pltpu.SemaphoreType.DMA((4, chunks)),
        ],
        compiler_params=params(36),
        cost_estimate=pl.CostEstimate(flops=5 * flops, bytes_accessed=23 * 2**20, transcendentals=0),
    )(ids, slot_of, arrived, in_hbm(part), in_hbm(coeffs), in_hbm(cond_prec))
    halo_sum = passed_along(halo_back, "blk", -1)
    return pl.pallas_call(
        functools.partial(sum_kernel, capacity),
        name="final_sum",
        out_shape=jax.ShapeDtypeStruct((blocks,) + tile, f32),
        in_specs=[VMEM, VMEM, VMEM, VMEM],
        out_specs=HBM,
        scratch_shapes=[
            pltpu.VMEM((blocks + 1,) + tile, f32),
            pltpu.SMEM(picks_shape, jnp.int32),
            pltpu.SemaphoreType.DMA((2,)),
        ],
        compiler_params=params(8),
        cost_estimate=pl.CostEstimate(flops=0, bytes_accessed=3 * 2**20, transcendentals=0),
    )(picks, base, halo_sum, returned)


def solution(mesh):
    in_specs = (
        P("blk", None, None),
        P("blk", None, None, None),
        P("blk", None, None),
        P("blk", None),
    )
    return jax.shard_map(
        per_device, mesh=mesh, in_specs=in_specs, out_specs=P("blk", None, None), check_vma=False
    )
```

```python
import functools

import jax
import jax.numpy as jnp
from jax import lax
from jax.experimental import pallas as pl
from jax.experimental.pallas import tpu as pltpu
from jax.sharding import PartitionSpec as P

REACH = 16
CHUNK = 16
AHEAD = 4
HELD = 3
LEAD = 3
STORES = 4
VMEM = pl.BlockSpec(memory_space=pltpu.VMEM)
SMEM = pl.BlockSpec(memory_space=pltpu.SMEM)
HBM = pl.BlockSpec(memory_space=pl.ANY)
NT = (((1,), (1,)), ((), ()))


def params(mib):
    return pltpu.CompilerParams(vmem_limit_bytes=mib * 2**20)


def in_hbm(x):
    return pltpu.with_memory_space_constraint(x, pltpu.HBM)


def passed_along(block, axis, distance):
    size = lax.axis_size(axis)
    return lax.ppermute(block, axis, [((i - distance) % size, i) for i in range(size)])


def earlier_matrix(blocks):
    row = lax.broadcasted_iota(jnp.int32, (blocks, blocks), 0)
    col = lax.broadcasted_iota(jnp.int32, (blocks, blocks), 1)
    return (row < col).astype(jnp.float32).astype(jnp.bfloat16)


def ranks_in(mask, blocks):
    chosen = mask.astype(jnp.float32).astype(jnp.bfloat16)
    return jnp.dot(chosen, earlier_matrix(blocks), preferred_element_type=jnp.float32).astype(jnp.int32)


def prep_kernel(ids_ref, probe_ref, sent_ref, tail_ref, ids, sems):
    blocks = probe_ref.shape[0]
    ids_copy = pltpu.make_async_copy(ids_ref, ids, sems.at[0])
    tail_copy = pltpu.make_async_copy(probe_ref.at[pl.ds(blocks - REACH, REACH)], tail_ref, sems.at[1])
    ids_copy.start()
    tail_copy.start()
    ids_copy.wait()
    sent_ref[...] = jnp.broadcast_to(ids[3:4, :], sent_ref.shape)
    tail_copy.wait()


def pick_kernel(capacity, ids_ref, probe_ref, out_ref, picks_ref, probe, out, picks_smem, sems):
    groups, blocks = ids_ref.shape
    load = pltpu.make_async_copy(probe_ref, probe, sems.at[0])
    load.start()
    me = lax.axis_index("blk")
    local = ids_ref[...] - me * blocks
    mask = (local >= 0) & (local < blocks)
    rank = ranks_in(mask, blocks)
    row = lax.broadcasted_iota(jnp.int32, (picks_ref.shape[0], groups), 0)
    ones = jnp.ones((picks_ref.shape[0], blocks), jnp.bfloat16)
    picks = jnp.zeros(row.shape, jnp.float32)
    for r in range(capacity):
        chosen = jnp.where(mask & (rank == r), local + 1, 0).astype(jnp.float32).astype(jnp.bfloat16)
        found = lax.dot_general(ones, chosen, NT, preferred_element_type=jnp.float32)
        picks = jnp.where(row == r, found, picks)
    picks_ref[:, pl.ds(0, groups)] = picks.astype(jnp.int32)
    copy = pltpu.make_async_copy(picks_ref, picks_smem, sems.at[1])
    copy.start()
    copy.wait()
    load.wait()
    part = groups // STORES

    def store(p):
        rows = pl.ds(p * part * capacity, part * capacity)
        return pltpu.make_async_copy(out.at[rows], out_ref.at[rows], sems.at[2 + p])

    for p in range(STORES):

        @pl.loop(p * part, (p + 1) * part, unroll=8)
        def _(g):
            for r in range(capacity):
                out[g * capacity + r] = probe[jnp.maximum(picks_smem[r, g] - 1, 0)]

        store(p).start()
    for p in range(STORES):
        store(p).wait()


def stacked(mats):
    return mats.reshape(-1, mats.shape[-1])


def apart(left0, left1, mats):
    zero = jnp.zeros_like(left0)
    left = jnp.concatenate(
        [jnp.concatenate([left0, zero], axis=1), jnp.concatenate([zero, left1], axis=1)], axis=0
    )
    out = jnp.dot(left, mats, preferred_element_type=jnp.float32)
    return out.reshape((2,) + (left0.shape[0], mats.shape[1]))


def apart4(lefts, mats):
    zero = jnp.zeros_like(lefts[0])
    rows = zero.shape[0]
    left = jnp.concatenate(
        [jnp.concatenate([x, zero] if j % 2 == 0 else [zero, x], axis=1) for j, x in enumerate(lefts)], axis=0
    )
    right = jnp.concatenate(
        [jnp.concatenate([mats[0], mats[1]], axis=0), jnp.concatenate([mats[2], mats[3]], axis=0)], axis=1
    )
    out = jnp.dot(left, right, preferred_element_type=jnp.float32)
    half = right.shape[1] // 2
    return [out[j * rows : (j + 1) * rows, (j // 2) * half : (j // 2 + 1) * half] for j in range(4)]


def apart_back(lefts, mats):
    rows, half = lefts.shape[1], mats.shape[0] // 2
    out = lax.dot_general(lefts.reshape(2 * rows, lefts.shape[2]), mats, NT, preferred_element_type=jnp.float32)
    return out[:rows, :half], out[rows:, half:]


def near_place(ids_ref, k, i, first, count):
    place = ids_ref[k, i] - first + REACH
    return jnp.where(place >= count, place - count, place)


def near_forward_kernel(
    groups, capacity, ids_ref, ids_row_ref, halo_ref, probe_ref, coeffs_ref, prec_ref,
    part_ref, own_ref, slot_ref, first_ref, mats_ref, ext, coeffs, prec, part, fold, mats, sems
):
    blocks = probe_ref.shape[0]
    chunks = blocks // CHUNK

    def loads(c):
        own = pl.ds(c * CHUNK, CHUNK)
        return (
            pltpu.make_async_copy(coeffs_ref.at[own], coeffs.at[own], sems.at[0, c]),
            pltpu.make_async_copy(prec_ref.at[own], prec.at[own], sems.at[1, c]),
        )

    def store_part(c):
        own = pl.ds(c * CHUNK, CHUNK)
        return pltpu.make_async_copy(part.at[own], part_ref.at[own], sems.at[2, c])

    def store_mats(c):
        own = pl.ds(c * CHUNK, CHUNK)
        return pltpu.make_async_copy(mats.at[own], mats_ref.at[own], sems.at[3, c])

    own_load = pltpu.make_async_copy(probe_ref, ext.at[pl.ds(REACH, blocks)], sems.at[2, 0])
    own_load.start()

    def fetch(c):
        for load in loads(c):
            load.start()

    def ready(c):
        for load in loads(c):
            load.wait()

    for c in range(LEAD):
        fetch(c)
    ext[pl.ds(0, REACH)] = halo_ref[...]
    owner = ids_row_ref[3:4, :] // blocks
    mask = lax.broadcasted_iota(jnp.int32, (groups, blocks), 0) == owner
    rank = jnp.sum(jnp.where(mask, ranks_in(mask, blocks), 0), axis=0, keepdims=True)
    slot_ref[...] = owner * capacity + rank
    first = lax.axis_index("blk") * blocks
    own_load.wait()

    def make(c):
        for b in range(0, CHUNK, 2):
            i = c * CHUNK + b
            rows = []
            for j in range(2):
                tiles = [ext[near_place(ids_ref, k, i + j, first, groups * blocks)] for k in range(3)]
                rows.append(jnp.concatenate(tiles, axis=1))
            near = [stacked(coeffs[i + j, pl.ds(0, 3)]) for j in range(2)]
            mixed = apart(rows[0], rows[1], jnp.concatenate(near, axis=0))
            part[pl.ds(i, 2)] = ext[pl.ds(REACH + i, 2)].astype(jnp.float32) - mixed
            for j in range(2):
                folded = lax.dot_general(prec[i + j], coeffs[i + j, 3], NT, preferred_element_type=jnp.float32)
                fold[i + j] = folded.astype(jnp.bfloat16)
        store_part(c).start()

    def use(c):
        for b in range(0, CHUNK, 2):
            i = c * CHUNK + b
            halves = []
            for j in range(2):
                high = part[i + j].astype(jnp.bfloat16)
                low = (part[i + j] - high.astype(jnp.float32)).astype(jnp.bfloat16)
                halves.append(jnp.concatenate([high, low], axis=0))
            both = apart(halves[0], halves[1], stacked(fold[pl.ds(i, 2)]))
            rows = both.shape[1] // 2
            own_ref[pl.ds(i, 2)] = both[:, :rows] + both[:, rows:]
            for j in range(2):
                mat = jnp.dot(coeffs[i + j, 3], fold[i + j], preferred_element_type=jnp.float32)
                mats[i + j] = mat.astype(jnp.bfloat16)
        store_mats(c).start()

    ready(0)
    fetch(LEAD)
    make(0)

    @pl.loop(1, chunks)
    def _(c):
        ready(c)

        @pl.when(c + LEAD < chunks)
        def _():
            fetch(c + LEAD)

        use(c - 1)
        make(c)

    use(chunks - 1)
    first_ref[...] = mats[pl.ds(0, HELD * CHUNK)]
    for c in range(chunks):
        store_part(c).wait()
        store_mats(c).wait()


def far_kernel(slots_ref, own_ref, far_ref, first_ref, mats_ref, parcel_ref, mats, slot, sems):
    blocks = own_ref.shape[0]
    chunks = blocks // CHUNK

    def load(c):
        own = pl.ds(c * CHUNK, CHUNK)
        return pltpu.make_async_copy(mats_ref.at[own], mats.at[own], sems.at[c])

    slot_copy = pltpu.make_async_copy(slots_ref, slot, sems.at[0])
    slot_copy.start()
    for c in range(HELD, chunks):
        load(c).start()
    parcel_ref[...] = jnp.zeros_like(parcel_ref)
    slot_copy.wait()

    def send_back(c, pair):
        for b in range(0, CHUNK, 4):
            i = c * CHUNK + b
            mixed = apart4([far_ref[slot[0, i + j]] for j in range(4)], [pair[i + j] for j in range(4)])
            for j in range(4):
                parcel_ref[slot[0, i + j]] = (own_ref[i + j] - mixed[j]).astype(jnp.bfloat16)

    for c in range(HELD):
        send_back(c, first_ref)
    middle = (HELD + chunks) // 2
    for part in (range(HELD, middle), range(middle, chunks)):
        for c in part:
            load(c).wait()
        for c in part:
            send_back(c, mats)


def near_back_kernel(
    groups, all_ids_ref, slots_ref, far_ref, part_ref, coeffs_ref, prec_ref,
    total, halo_ref, white, scaled, part, coeffs, prec, ids_ref, slot_ref, sems
):
    blocks, _, points = white.shape
    chunks = blocks // CHUNK

    def load(c, which):
        own = pl.ds(c * CHUNK, CHUNK)
        source, target = (
            (part_ref.at[own], part.at[own]),
            (coeffs_ref.at[own, 3], coeffs.at[own, 3]),
            (prec_ref.at[own], prec.at[own]),
            (coeffs_ref.at[own, pl.ds(0, 3)], coeffs.at[own, pl.ds(0, 3)]),
        )[which]
        return pltpu.make_async_copy(source, target, sems.at[which, c])

    def fetch(c):
        for which in range(4):
            load(c, which).start()

    for which in range(3):
        load(0, which).start()
    ids_copy = pltpu.make_async_copy(all_ids_ref, ids_ref, sems.at[4, 0])
    slot_copy = pltpu.make_async_copy(slots_ref, slot_ref, sems.at[4, 1])
    ids_copy.start()
    slot_copy.start()
    load(0, 3).start()
    for c in range(1, LEAD):
        fetch(c)
    total[pl.ds(0, REACH)] = jnp.zeros((REACH,) + total.shape[1:], jnp.float32)
    first = lax.axis_index("blk") * blocks

    def mix(c):
        load(c, 0).wait()
        load(c, 1).wait()
        for b in range(0, CHUNK, 4):
            i = c * CHUNK + b
            mixed = apart4([far_ref[slot_ref[0, i + j]] for j in range(4)], [coeffs[i + j, 3] for j in range(4)])
            for j in range(4):
                white[i + j] = (part[i + j] - mixed[j]).astype(jnp.bfloat16)

    def scale(c):
        load(c, 2).wait()
        for b in range(0, CHUNK, 4):
            i = c * CHUNK + b
            tiles = apart4([white[i + j] for j in range(4)], [prec[i + j] for j in range(4)])
            for j in range(4):
                scaled[i + j] = tiles[j].astype(jnp.bfloat16)
                total[REACH + i + j] = scaled[i + j].astype(jnp.float32)

    def back(c):
        load(c, 3).wait()
        terms = []
        for b in range(CHUNK + AHEAD):
            if b < CHUNK and b % 2 == 0:
                i = c * CHUNK + b
                mats = [stacked(coeffs[i + j, pl.ds(0, 3)]) for j in range(2)]
                terms.extend(apart_back(scaled[pl.ds(i, 2)], jnp.concatenate(mats, axis=0)))
            if b >= AHEAD:
                i = c * CHUNK + b - AHEAD
                places = [near_place(ids_ref, k, i, first, groups * blocks) for k in range(3)]
                olds = [total[place] for place in places]
                for k in range(3):
                    total[places[k]] = olds[k] - terms[b - AHEAD][:, k * points : (k + 1) * points]

    ids_copy.wait()
    slot_copy.wait()
    mix(0)
    fetch(LEAD)
    scale(0)
    mix(1)
    fetch(LEAD + 1)

    @pl.loop(0, chunks - 2)
    def _(c):
        @pl.when(c + LEAD + 2 < chunks)
        def _():
            fetch(c + LEAD + 2)

        back(c)
        scale(c + 1)
        mix(c + 2)

    back(chunks - 2)
    scale(chunks - 1)
    back(chunks - 1)
    halo_ref[...] = total[pl.ds(0, REACH)].astype(halo_ref.dtype)


def sum_kernel(capacity, all_picks_ref, base_ref, halo_ref, back_ref, out_ref, total, picks_ref, sems):
    groups = back_ref.shape[0] // capacity
    picks_copy = pltpu.make_async_copy(all_picks_ref, picks_ref, sems.at[0])
    picks_copy.start()
    blocks = out_ref.shape[0]
    total[pl.ds(0, blocks)] = base_ref[pl.ds(REACH, blocks)]
    last = pl.ds(blocks - REACH, REACH)
    total[last] = total[last] + halo_ref[...].astype(jnp.float32)
    picks_copy.wait()

    @pl.loop(0, groups, unroll=8)
    def _(g):
        picks = [picks_ref[r, g] for r in range(capacity)]
        places = [jnp.where(pick > 0, pick - 1, blocks) for pick in picks]
        olds = [total[place] for place in places]
        for r in range(capacity):
            total[places[r]] = olds[r] - back_ref[g * capacity + r].astype(jnp.float32)

    store = pltpu.make_async_copy(total.at[pl.ds(0, blocks)], out_ref, sems.at[1])
    store.start()
    store.wait()


def per_device(probe_vecs, coeffs, cond_prec, neighbours):
    blocks, probes, points = probe_vecs.shape
    groups = lax.axis_size("blk")
    capacity = max(2, blocks // (groups - 1) + 1)
    slots = groups * capacity
    picks_shape = (-(-capacity // 8) * 8, -(-groups // 128) * 128)
    chunks = blocks // CHUNK
    bf16, f32 = jnp.bfloat16, jnp.float32
    tile = (probes, points)
    flops = 2 * blocks * probes * points * points

    def exchange(x):
        return lax.all_to_all(x, "blk", split_axis=0, concat_axis=0, tiled=True)

    ids = neighbours.T
    sent_ids, tail = pl.pallas_call(
        prep_kernel,
        name="prep",
        out_shape=(
            jax.ShapeDtypeStruct((groups, blocks), jnp.int32),
            jax.ShapeDtypeStruct((REACH,) + tile, bf16),
        ),
        in_specs=[HBM, HBM],
        out_specs=(VMEM, VMEM),
        scratch_shapes=[pltpu.VMEM(ids.shape, jnp.int32), pltpu.SemaphoreType.DMA((2,))],
        compiler_params=params(8),
    )(in_hbm(ids), in_hbm(probe_vecs))
    halo = passed_along(tail, "blk", 1)
    all_ids = exchange(sent_ids)
    all_ids, halo = lax.optimization_barrier((all_ids, halo))
    outgoing, picks = pl.pallas_call(
        functools.partial(pick_kernel, capacity),
        name="pick_tiles",
        out_shape=(
            jax.ShapeDtypeStruct((slots,) + tile, bf16),
            jax.ShapeDtypeStruct(picks_shape, jnp.int32),
        ),
        in_specs=[VMEM, HBM],
        out_specs=(HBM, VMEM),
        scratch_shapes=[
            pltpu.VMEM((blocks,) + tile, bf16),
            pltpu.VMEM((slots,) + tile, bf16),
            pltpu.SMEM(picks_shape, jnp.int32),
            pltpu.SemaphoreType.DMA((2 + STORES,)),
        ],
        compiler_params=params(8),
        cost_estimate=pl.CostEstimate(flops=0, bytes_accessed=2 * slots * 4096, transcendentals=0),
    )(all_ids, in_hbm(probe_vecs))
    arrived = exchange(outgoing.reshape((groups, capacity) + tile)).reshape((slots,) + tile)
    mats = (blocks, points, points)
    all_mats = pltpu.VMEM((blocks, 4, points, points), bf16)
    tiles_f32 = jax.ShapeDtypeStruct((blocks,) + tile, f32)
    part, own_far, slot_of, first_mats, far_mats = pl.pallas_call(
        functools.partial(near_forward_kernel, groups, capacity),
        name="near_forward",
        out_shape=(
            pltpu.HBM((blocks,) + tile, f32),
            tiles_f32,
            jax.ShapeDtypeStruct((1, blocks), jnp.int32),
            jax.ShapeDtypeStruct((HELD * CHUNK, points, points), bf16),
            pltpu.HBM(mats, bf16),
        ),
        in_specs=[SMEM, VMEM, VMEM, HBM, HBM, HBM],
        out_specs=(HBM, VMEM, VMEM, VMEM, HBM),
        scratch_shapes=[
            pltpu.VMEM((REACH + blocks,) + tile, bf16),
            all_mats,
            pltpu.VMEM(mats, bf16),
            pltpu.VMEM((blocks,) + tile, f32),
            pltpu.VMEM(mats, bf16),
            pltpu.VMEM(mats, bf16),
            pltpu.SemaphoreType.DMA((4, chunks)),
        ],
        compiler_params=params(40),
        cost_estimate=pl.CostEstimate(flops=20 * flops, bytes_accessed=28 * 2**20, transcendentals=0),
    )(ids, ids, halo, in_hbm(probe_vecs), in_hbm(coeffs), in_hbm(cond_prec))
    parcel = pl.pallas_call(
        far_kernel,
        name="far_terms",
        out_shape=jax.ShapeDtypeStruct((slots,) + tile, bf16),
        in_specs=[VMEM, VMEM, VMEM, VMEM, HBM],
        out_specs=VMEM,
        scratch_shapes=[
            pltpu.VMEM(mats, bf16),
            pltpu.SMEM((1, blocks), jnp.int32),
            pltpu.SemaphoreType.DMA((chunks,)),
        ],
        compiler_params=params(16),
        cost_estimate=pl.CostEstimate(flops=flops, bytes_accessed=6 * 2**20, transcendentals=0),
    )(slot_of, own_far, arrived, first_mats, in_hbm(far_mats))
    parcel, arrived = lax.optimization_barrier((parcel, arrived))
    returned = exchange(parcel.reshape((groups, capacity) + tile)).reshape((slots,) + tile)
    base, halo_back = pl.pallas_call(
        functools.partial(near_back_kernel, groups),
        name="near_back",
        out_shape=(
            jax.ShapeDtypeStruct((REACH + blocks,) + tile, f32),
            jax.ShapeDtypeStruct((REACH,) + tile, bf16),
        ),
        in_specs=[VMEM, VMEM, VMEM, HBM, HBM, HBM],
        out_specs=(VMEM, VMEM),
        scratch_shapes=[
            pltpu.VMEM((blocks,) + tile, bf16),
            pltpu.VMEM((blocks,) + tile, bf16),
            pltpu.VMEM((blocks,) + tile, f32),
            all_mats,
            pltpu.VMEM(mats, bf16),
            pltpu.SMEM(ids.shape, jnp.int32),
            pltpu.SMEM((1, blocks), jnp.int32),
            pltpu.SemaphoreType.DMA((5, chunks)),
        ],
        compiler_params=params(36),
        cost_estimate=pl.CostEstimate(flops=5 * flops, bytes_accessed=23 * 2**20, transcendentals=0),
    )(ids, slot_of, arrived, in_hbm(part), in_hbm(coeffs), in_hbm(cond_prec))
    halo_sum = passed_along(halo_back, "blk", -1)
    return pl.pallas_call(
        functools.partial(sum_kernel, capacity),
        name="final_sum",
        out_shape=jax.ShapeDtypeStruct((blocks,) + tile, f32),
        in_specs=[VMEM, VMEM, VMEM, VMEM],
        out_specs=HBM,
        scratch_shapes=[
            pltpu.VMEM((blocks + 1,) + tile, f32),
            pltpu.SMEM(picks_shape, jnp.int32),
            pltpu.SemaphoreType.DMA((2,)),
        ],
        compiler_params=params(8),
        cost_estimate=pl.CostEstimate(flops=0, bytes_accessed=3 * 2**20, transcendentals=0),
    )(picks, base, halo_sum, returned)


def solution(mesh):
    in_specs = (
        P("blk", None, None),
        P("blk", None, None, None),
        P("blk", None, None),
        P("blk", None),
    )
    return jax.shard_map(
        per_device, mesh=mesh, in_specs=in_specs, out_specs=P("blk", None, None), check_vma=False
    )
```

```python
import functools

import jax
import jax.numpy as jnp
from jax import lax
from jax.experimental import pallas as pl
from jax.experimental.pallas import tpu as pltpu
from jax.sharding import PartitionSpec as P

REACH = 16
CHUNK = 16
AHEAD = 4
HELD = 3
LEAD = 3
STORES = 4
VMEM = pl.BlockSpec(memory_space=pltpu.VMEM)
SMEM = pl.BlockSpec(memory_space=pltpu.SMEM)
HBM = pl.BlockSpec(memory_space=pl.ANY)
NT = (((1,), (1,)), ((), ()))


def params(mib):
    return pltpu.CompilerParams(vmem_limit_bytes=mib * 2**20)


def in_hbm(x):
    return pltpu.with_memory_space_constraint(x, pltpu.HBM)


def passed_along(block, axis, distance):
    size = lax.axis_size(axis)
    return lax.ppermute(block, axis, [((i - distance) % size, i) for i in range(size)])


def earlier_matrix(blocks):
    row = lax.broadcasted_iota(jnp.int32, (blocks, blocks), 0)
    col = lax.broadcasted_iota(jnp.int32, (blocks, blocks), 1)
    return (row < col).astype(jnp.float32).astype(jnp.bfloat16)


def ranks_in(mask, blocks):
    chosen = mask.astype(jnp.float32).astype(jnp.bfloat16)
    return jnp.dot(chosen, earlier_matrix(blocks), preferred_element_type=jnp.float32).astype(jnp.int32)


def prep_kernel(ids_ref, probe_ref, sent_ref, tail_ref, scalars_ref, ids, sems):
    blocks = probe_ref.shape[0]
    ids_copy = pltpu.make_async_copy(ids_ref, ids, sems.at[0])
    tail_copy = pltpu.make_async_copy(probe_ref.at[pl.ds(blocks - REACH, REACH)], tail_ref, sems.at[1])
    scalars_copy = pltpu.make_async_copy(ids_ref, scalars_ref, sems.at[2])
    ids_copy.start()
    tail_copy.start()
    scalars_copy.start()
    ids_copy.wait()
    sent_ref[...] = jnp.broadcast_to(ids[3:4, :], sent_ref.shape)
    tail_copy.wait()
    scalars_copy.wait()


def pick_kernel(capacity, ids_ref, probe_ref, out_ref, picks_smem, probe, out, picks_ref, sems):
    groups, blocks = ids_ref.shape
    load = pltpu.make_async_copy(probe_ref, probe, sems.at[0])
    load.start()
    me = lax.axis_index("blk")
    local = ids_ref[...] - me * blocks
    mask = (local >= 0) & (local < blocks)
    rank = ranks_in(mask, blocks)
    row = lax.broadcasted_iota(jnp.int32, (picks_ref.shape[0], groups), 0)
    ones = jnp.ones((picks_ref.shape[0], blocks), jnp.bfloat16)
    picks = jnp.zeros(row.shape, jnp.float32)
    for r in range(capacity):
        chosen = jnp.where(mask & (rank == r), local + 1, 0).astype(jnp.float32).astype(jnp.bfloat16)
        found = lax.dot_general(ones, chosen, NT, preferred_element_type=jnp.float32)
        picks = jnp.where(row == r, found, picks)
    picks_ref[:, pl.ds(0, groups)] = picks.astype(jnp.int32)
    copy = pltpu.make_async_copy(picks_ref, picks_smem, sems.at[1])
    copy.start()
    copy.wait()
    load.wait()
    part = groups // STORES

    def store(p):
        rows = pl.ds(p * part * capacity, part * capacity)
        return pltpu.make_async_copy(out.at[rows], out_ref.at[rows], sems.at[2 + p])

    for p in range(STORES):

        @pl.loop(p * part, (p + 1) * part, unroll=8)
        def _(g):
            for r in range(capacity):
                out[g * capacity + r] = probe[jnp.maximum(picks_smem[r, g] - 1, 0)]

        store(p).start()
    for p in range(STORES):
        store(p).wait()


def stacked(mats):
    return mats.reshape(-1, mats.shape[-1])


def apart(left0, left1, mats):
    zero = jnp.zeros_like(left0)
    left = jnp.concatenate(
        [jnp.concatenate([left0, zero], axis=1), jnp.concatenate([zero, left1], axis=1)], axis=0
    )
    out = jnp.dot(left, mats, preferred_element_type=jnp.float32)
    return out.reshape((2,) + (left0.shape[0], mats.shape[1]))


def apart4(lefts, mats):
    zero = jnp.zeros_like(lefts[0])
    rows = zero.shape[0]
    left = jnp.concatenate(
        [jnp.concatenate([x, zero] if j % 2 == 0 else [zero, x], axis=1) for j, x in enumerate(lefts)], axis=0
    )
    right = jnp.concatenate(
        [jnp.concatenate([mats[0], mats[1]], axis=0), jnp.concatenate([mats[2], mats[3]], axis=0)], axis=1
    )
    out = jnp.dot(left, right, preferred_element_type=jnp.float32)
    half = right.shape[1] // 2
    return [out[j * rows : (j + 1) * rows, (j // 2) * half : (j // 2 + 1) * half] for j in range(4)]


def apart_back(lefts, mats):
    rows, half = lefts.shape[1], mats.shape[0] // 2
    out = lax.dot_general(lefts.reshape(2 * rows, lefts.shape[2]), mats, NT, preferred_element_type=jnp.float32)
    return out[:rows, :half], out[rows:, half:]


def near_place(ids_ref, k, i, first, count):
    place = ids_ref[k, i] - first + REACH
    return jnp.where(place >= count, place - count, place)


def near_forward_kernel(
    groups, capacity, ids_ref, ids_row_ref, halo_ref, probe_ref, coeffs_ref, prec_ref,
    part_ref, own_ref, slot_ref, first_ref, mats_ref, ext, coeffs, prec, part, fold, mats, slots, sems
):
    blocks = probe_ref.shape[0]
    chunks = blocks // CHUNK

    def loads(c):
        own = pl.ds(c * CHUNK, CHUNK)
        return (
            pltpu.make_async_copy(coeffs_ref.at[own], coeffs.at[own], sems.at[0, c]),
            pltpu.make_async_copy(prec_ref.at[own], prec.at[own], sems.at[1, c]),
        )

    def store_part(c):
        own = pl.ds(c * CHUNK, CHUNK)
        return pltpu.make_async_copy(part.at[own], part_ref.at[own], sems.at[2, c])

    def store_mats(c):
        own = pl.ds(c * CHUNK, CHUNK)
        return pltpu.make_async_copy(mats.at[own], mats_ref.at[own], sems.at[3, c])

    own_load = pltpu.make_async_copy(probe_ref, ext.at[pl.ds(REACH, blocks)], sems.at[2, 0])
    own_load.start()

    def fetch(c):
        for load in loads(c):
            load.start()

    def ready(c):
        for load in loads(c):
            load.wait()

    for c in range(LEAD):
        fetch(c)
    ext[pl.ds(0, REACH)] = halo_ref[...]
    owner = ids_row_ref[3:4, :] // blocks
    mask = lax.broadcasted_iota(jnp.int32, (groups, blocks), 0) == owner
    rank = jnp.sum(jnp.where(mask, ranks_in(mask, blocks), 0), axis=0, keepdims=True)
    slots[...] = owner * capacity + rank
    slot_copy = pltpu.make_async_copy(slots, slot_ref, sems.at[2, 1])
    slot_copy.start()
    first = lax.axis_index("blk") * blocks
    slot_copy.wait()
    own_load.wait()

    def make(c):
        for b in range(0, CHUNK, 2):
            i = c * CHUNK + b
            rows = []
            for j in range(2):
                tiles = [ext[near_place(ids_ref, k, i + j, first, groups * blocks)] for k in range(3)]
                rows.append(jnp.concatenate(tiles, axis=1))
            near = [stacked(coeffs[i + j, pl.ds(0, 3)]) for j in range(2)]
            mixed = apart(rows[0], rows[1], jnp.concatenate(near, axis=0))
            part[pl.ds(i, 2)] = ext[pl.ds(REACH + i, 2)].astype(jnp.float32) - mixed
            for j in range(2):
                folded = lax.dot_general(prec[i + j], coeffs[i + j, 3], NT, preferred_element_type=jnp.float32)
                fold[i + j] = folded.astype(jnp.bfloat16)
        store_part(c).start()

    def use(c):
        for b in range(0, CHUNK, 2):
            i = c * CHUNK + b
            halves = []
            for j in range(2):
                high = part[i + j].astype(jnp.bfloat16)
                low = (part[i + j] - high.astype(jnp.float32)).astype(jnp.bfloat16)
                halves.append(jnp.concatenate([high, low], axis=0))
            both = apart(halves[0], halves[1], stacked(fold[pl.ds(i, 2)]))
            rows = both.shape[1] // 2
            own_ref[pl.ds(i, 2)] = both[:, :rows] + both[:, rows:]
            for j in range(2):
                mat = jnp.dot(coeffs[i + j, 3], fold[i + j], preferred_element_type=jnp.float32)
                mats[i + j] = mat.astype(jnp.bfloat16)
        store_mats(c).start()

    ready(0)
    fetch(LEAD)
    make(0)

    @pl.loop(1, chunks)
    def _(c):
        ready(c)

        @pl.when(c + LEAD < chunks)
        def _():
            fetch(c + LEAD)

        use(c - 1)
        make(c)

    use(chunks - 1)
    first_ref[...] = mats[pl.ds(0, HELD * CHUNK)]
    for c in range(chunks):
        store_part(c).wait()
        store_mats(c).wait()


def far_kernel(slot, own_ref, far_ref, first_ref, mats_ref, parcel_ref, mats, sems):
    blocks = own_ref.shape[0]
    chunks = blocks // CHUNK

    def load(c):
        own = pl.ds(c * CHUNK, CHUNK)
        return pltpu.make_async_copy(mats_ref.at[own], mats.at[own], sems.at[c])

    for c in range(HELD, chunks):
        load(c).start()
    parcel_ref[...] = jnp.zeros_like(parcel_ref)

    def send_back(c, pair):
        for b in range(0, CHUNK, 4):
            i = c * CHUNK + b
            mixed = apart4([far_ref[slot[0, i + j]] for j in range(4)], [pair[i + j] for j in range(4)])
            for j in range(4):
                parcel_ref[slot[0, i + j]] = (own_ref[i + j] - mixed[j]).astype(jnp.bfloat16)

    for c in range(HELD):
        send_back(c, first_ref)
    middle = (HELD + chunks) // 2
    for part in (range(HELD, middle), range(middle, chunks)):
        for c in part:
            load(c).wait()
        for c in part:
            send_back(c, mats)


def near_back_kernel(
    groups, ids_ref, slot_ref, far_ref, part_ref, coeffs_ref, prec_ref,
    total, halo_ref, white, scaled, part, coeffs, prec, sems
):
    blocks, _, points = white.shape
    chunks = blocks // CHUNK

    def load(c, which):
        own = pl.ds(c * CHUNK, CHUNK)
        source, target = (
            (part_ref.at[own], part.at[own]),
            (coeffs_ref.at[own, 3], coeffs.at[own, 3]),
            (prec_ref.at[own], prec.at[own]),
            (coeffs_ref.at[own, pl.ds(0, 3)], coeffs.at[own, pl.ds(0, 3)]),
        )[which]
        return pltpu.make_async_copy(source, target, sems.at[which, c])

    def fetch(c):
        for which in range(4):
            load(c, which).start()

    for which in range(3):
        load(0, which).start()
    load(0, 3).start()
    for c in range(1, LEAD):
        fetch(c)
    total[pl.ds(0, REACH)] = jnp.zeros((REACH,) + total.shape[1:], jnp.float32)
    first = lax.axis_index("blk") * blocks

    def mix(c):
        load(c, 0).wait()
        load(c, 1).wait()
        for b in range(0, CHUNK, 4):
            i = c * CHUNK + b
            mixed = apart4([far_ref[slot_ref[0, i + j]] for j in range(4)], [coeffs[i + j, 3] for j in range(4)])
            for j in range(4):
                white[i + j] = (part[i + j] - mixed[j]).astype(jnp.bfloat16)

    def scale(c):
        load(c, 2).wait()
        for b in range(0, CHUNK, 4):
            i = c * CHUNK + b
            tiles = apart4([white[i + j] for j in range(4)], [prec[i + j] for j in range(4)])
            for j in range(4):
                scaled[i + j] = tiles[j].astype(jnp.bfloat16)
                total[REACH + i + j] = scaled[i + j].astype(jnp.float32)

    def back(c):
        load(c, 3).wait()
        terms = []
        for b in range(CHUNK + AHEAD):
            if b < CHUNK and b % 2 == 0:
                i = c * CHUNK + b
                mats = [stacked(coeffs[i + j, pl.ds(0, 3)]) for j in range(2)]
                terms.extend(apart_back(scaled[pl.ds(i, 2)], jnp.concatenate(mats, axis=0)))
            if b >= AHEAD:
                i = c * CHUNK + b - AHEAD
                places = [near_place(ids_ref, k, i, first, groups * blocks) for k in range(3)]
                olds = [total[place] for place in places]
                for k in range(3):
                    total[places[k]] = olds[k] - terms[b - AHEAD][:, k * points : (k + 1) * points]

    mix(0)
    fetch(LEAD)
    scale(0)
    mix(1)
    fetch(LEAD + 1)

    @pl.loop(0, chunks - 2)
    def _(c):
        @pl.when(c + LEAD + 2 < chunks)
        def _():
            fetch(c + LEAD + 2)

        back(c)
        scale(c + 1)
        mix(c + 2)

    back(chunks - 2)
    scale(chunks - 1)
    back(chunks - 1)
    halo_ref[...] = total[pl.ds(0, REACH)].astype(halo_ref.dtype)


def sum_kernel(capacity, picks_ref, base_ref, halo_ref, back_ref, out_ref, total, sem):
    groups = back_ref.shape[0] // capacity
    blocks = out_ref.shape[0]
    total[pl.ds(0, blocks)] = base_ref[pl.ds(REACH, blocks)]
    last = pl.ds(blocks - REACH, REACH)
    total[last] = total[last] + halo_ref[...].astype(jnp.float32)

    @pl.loop(0, groups, unroll=8)
    def _(g):
        picks = [picks_ref[r, g] for r in range(capacity)]
        places = [jnp.where(pick > 0, pick - 1, blocks) for pick in picks]
        olds = [total[place] for place in places]
        for r in range(capacity):
            total[places[r]] = olds[r] - back_ref[g * capacity + r].astype(jnp.float32)

    store = pltpu.make_async_copy(total.at[pl.ds(0, blocks)], out_ref, sem)
    store.start()
    store.wait()


def per_device(probe_vecs, coeffs, cond_prec, neighbours):
    blocks, probes, points = probe_vecs.shape
    groups = lax.axis_size("blk")
    capacity = max(2, blocks // (groups - 1) + 1)
    slots = groups * capacity
    picks_shape = (-(-capacity // 8) * 8, -(-groups // 128) * 128)
    chunks = blocks // CHUNK
    bf16, f32 = jnp.bfloat16, jnp.float32
    tile = (probes, points)
    flops = 2 * blocks * probes * points * points

    def exchange(x):
        return lax.all_to_all(x, "blk", split_axis=0, concat_axis=0, tiled=True)

    ids = neighbours.T
    sent_ids, tail, scalar_ids = pl.pallas_call(
        prep_kernel,
        name="prep",
        out_shape=(
            jax.ShapeDtypeStruct((groups, blocks), jnp.int32),
            jax.ShapeDtypeStruct((REACH,) + tile, bf16),
            pltpu.SMEM(ids.shape, jnp.int32),
        ),
        in_specs=[HBM, HBM],
        out_specs=(VMEM, VMEM, SMEM),
        scratch_shapes=[pltpu.VMEM(ids.shape, jnp.int32), pltpu.SemaphoreType.DMA((3,))],
        compiler_params=params(8),
    )(in_hbm(ids), in_hbm(probe_vecs))
    halo = passed_along(tail, "blk", 1)
    all_ids = exchange(sent_ids)
    all_ids, halo = lax.optimization_barrier((all_ids, halo))
    outgoing, picks = pl.pallas_call(
        functools.partial(pick_kernel, capacity),
        name="pick_tiles",
        out_shape=(
            jax.ShapeDtypeStruct((slots,) + tile, bf16),
            pltpu.SMEM(picks_shape, jnp.int32),
        ),
        in_specs=[VMEM, HBM],
        out_specs=(HBM, SMEM),
        scratch_shapes=[
            pltpu.VMEM((blocks,) + tile, bf16),
            pltpu.VMEM((slots,) + tile, bf16),
            pltpu.VMEM(picks_shape, jnp.int32),
            pltpu.SemaphoreType.DMA((2 + STORES,)),
        ],
        compiler_params=params(8),
        cost_estimate=pl.CostEstimate(flops=0, bytes_accessed=2 * slots * 4096, transcendentals=0),
    )(all_ids, in_hbm(probe_vecs))
    arrived = exchange(outgoing.reshape((groups, capacity) + tile)).reshape((slots,) + tile)
    mats = (blocks, points, points)
    all_mats = pltpu.VMEM((blocks, 4, points, points), bf16)
    tiles_f32 = jax.ShapeDtypeStruct((blocks,) + tile, f32)
    part, own_far, slot_of, first_mats, far_mats = pl.pallas_call(
        functools.partial(near_forward_kernel, groups, capacity),
        name="near_forward",
        out_shape=(
            pltpu.HBM((blocks,) + tile, f32),
            tiles_f32,
            pltpu.SMEM((1, blocks), jnp.int32),
            jax.ShapeDtypeStruct((HELD * CHUNK, points, points), bf16),
            pltpu.HBM(mats, bf16),
        ),
        in_specs=[SMEM, VMEM, VMEM, HBM, HBM, HBM],
        out_specs=(HBM, VMEM, SMEM, VMEM, HBM),
        scratch_shapes=[
            pltpu.VMEM((REACH + blocks,) + tile, bf16),
            all_mats,
            pltpu.VMEM(mats, bf16),
            pltpu.VMEM((blocks,) + tile, f32),
            pltpu.VMEM(mats, bf16),
            pltpu.VMEM(mats, bf16),
            pltpu.VMEM((1, blocks), jnp.int32),
            pltpu.SemaphoreType.DMA((4, chunks)),
        ],
        compiler_params=params(40),
        cost_estimate=pl.CostEstimate(flops=20 * flops, bytes_accessed=28 * 2**20, transcendentals=0),
    )(scalar_ids, ids, halo, in_hbm(probe_vecs), in_hbm(coeffs), in_hbm(cond_prec))
    parcel = pl.pallas_call(
        far_kernel,
        name="far_terms",
        out_shape=jax.ShapeDtypeStruct((slots,) + tile, bf16),
        in_specs=[SMEM, VMEM, VMEM, VMEM, HBM],
        out_specs=VMEM,
        scratch_shapes=[
            pltpu.VMEM(mats, bf16),
            pltpu.SemaphoreType.DMA((chunks,)),
        ],
        compiler_params=params(16),
        cost_estimate=pl.CostEstimate(flops=flops, bytes_accessed=6 * 2**20, transcendentals=0),
    )(slot_of, own_far, arrived, first_mats, in_hbm(far_mats))
    parcel, arrived = lax.optimization_barrier((parcel, arrived))
    returned = exchange(parcel.reshape((groups, capacity) + tile)).reshape((slots,) + tile)
    base, halo_back = pl.pallas_call(
        functools.partial(near_back_kernel, groups),
        name="near_back",
        out_shape=(
            jax.ShapeDtypeStruct((REACH + blocks,) + tile, f32),
            jax.ShapeDtypeStruct((REACH,) + tile, bf16),
        ),
        in_specs=[SMEM, SMEM, VMEM, HBM, HBM, HBM],
        out_specs=(VMEM, VMEM),
        scratch_shapes=[
            pltpu.VMEM((blocks,) + tile, bf16),
            pltpu.VMEM((blocks,) + tile, bf16),
            pltpu.VMEM((blocks,) + tile, f32),
            all_mats,
            pltpu.VMEM(mats, bf16),
            pltpu.SemaphoreType.DMA((4, chunks)),
        ],
        compiler_params=params(36),
        cost_estimate=pl.CostEstimate(flops=5 * flops, bytes_accessed=23 * 2**20, transcendentals=0),
    )(scalar_ids, slot_of, arrived, in_hbm(part), in_hbm(coeffs), in_hbm(cond_prec))
    halo_sum = passed_along(halo_back, "blk", -1)
    return pl.pallas_call(
        functools.partial(sum_kernel, capacity),
        name="final_sum",
        out_shape=jax.ShapeDtypeStruct((blocks,) + tile, f32),
        in_specs=[SMEM, VMEM, VMEM, VMEM],
        out_specs=HBM,
        scratch_shapes=[
            pltpu.VMEM((blocks + 1,) + tile, f32),
            pltpu.SemaphoreType.DMA,
        ],
        compiler_params=params(8),
        cost_estimate=pl.CostEstimate(flops=0, bytes_accessed=3 * 2**20, transcendentals=0),
    )(picks, base, halo_sum, returned)


def solution(mesh):
    in_specs = (
        P("blk", None, None),
        P("blk", None, None, None),
        P("blk", None, None),
        P("blk", None),
    )
    return jax.shard_map(
        per_device, mesh=mesh, in_specs=in_specs, out_specs=P("blk", None, None), check_vma=False
    )
```

```python
import functools

import jax
import jax.numpy as jnp
from jax import lax
from jax.experimental import pallas as pl
from jax.experimental.pallas import tpu as pltpu
from jax.sharding import PartitionSpec as P

REACH = 16
CHUNK = 16
AHEAD = 4
HELD = 3
LEAD = 3
STORES = 4
VMEM = pl.BlockSpec(memory_space=pltpu.VMEM)
SMEM = pl.BlockSpec(memory_space=pltpu.SMEM)
HBM = pl.BlockSpec(memory_space=pl.ANY)
NT = (((1,), (1,)), ((), ()))


def params(mib):
    return pltpu.CompilerParams(vmem_limit_bytes=mib * 2**20)


def in_hbm(x):
    return pltpu.with_memory_space_constraint(x, pltpu.HBM)


def passed_along(block, axis, distance):
    size = lax.axis_size(axis)
    return lax.ppermute(block, axis, [((i - distance) % size, i) for i in range(size)])


def earlier_matrix(blocks):
    row = lax.broadcasted_iota(jnp.int32, (blocks, blocks), 0)
    col = lax.broadcasted_iota(jnp.int32, (blocks, blocks), 1)
    return (row < col).astype(jnp.float32).astype(jnp.bfloat16)


def ranks_in(mask, blocks):
    chosen = mask.astype(jnp.float32).astype(jnp.bfloat16)
    return jnp.dot(chosen, earlier_matrix(blocks), preferred_element_type=jnp.float32).astype(jnp.int32)


def prep_kernel(ids_ref, probe_ref, sent_ref, tail_ref, scalars_ref, ids, sems):
    blocks = probe_ref.shape[0]
    ids_copy = pltpu.make_async_copy(ids_ref, ids, sems.at[0])
    tail_copy = pltpu.make_async_copy(probe_ref.at[pl.ds(blocks - REACH, REACH)], tail_ref, sems.at[1])
    scalars_copy = pltpu.make_async_copy(ids_ref, scalars_ref, sems.at[2])
    ids_copy.start()
    tail_copy.start()
    scalars_copy.start()
    ids_copy.wait()
    sent_ref[...] = jnp.broadcast_to(ids[3:4, :], sent_ref.shape)
    tail_copy.wait()
    scalars_copy.wait()


def pick_kernel(capacity, ids_ref, probe_ref, out_ref, picks_smem, probe, out, picks_ref, sems):
    groups, blocks = ids_ref.shape
    load = pltpu.make_async_copy(probe_ref, probe, sems.at[0])
    load.start()
    me = lax.axis_index("blk")
    local = ids_ref[...] - me * blocks
    mask = (local >= 0) & (local < blocks)
    rank = ranks_in(mask, blocks)
    row = lax.broadcasted_iota(jnp.int32, (picks_ref.shape[0], groups), 0)
    ones = jnp.ones((picks_ref.shape[0], blocks), jnp.bfloat16)
    picks = jnp.zeros(row.shape, jnp.float32)
    for r in range(capacity):
        chosen = jnp.where(mask & (rank == r), local + 1, 0).astype(jnp.float32).astype(jnp.bfloat16)
        found = lax.dot_general(ones, chosen, NT, preferred_element_type=jnp.float32)
        picks = jnp.where(row == r, found, picks)
    picks_ref[:, pl.ds(0, groups)] = picks.astype(jnp.int32)
    copy = pltpu.make_async_copy(picks_ref, picks_smem, sems.at[1])
    copy.start()
    copy.wait()
    load.wait()
    part = groups // STORES

    def store(p):
        rows = pl.ds(p * part * capacity, part * capacity)
        return pltpu.make_async_copy(out.at[rows], out_ref.at[rows], sems.at[2 + p])

    for p in range(STORES):

        @pl.loop(p * part, (p + 1) * part, unroll=8)
        def _(g):
            for r in range(capacity):
                out[g * capacity + r] = probe[jnp.maximum(picks_smem[r, g] - 1, 0)]

        store(p).start()
    for p in range(STORES):
        store(p).wait()


def stacked(mats):
    return mats.reshape(-1, mats.shape[-1])


def apart(left0, left1, mats):
    zero = jnp.zeros_like(left0)
    left = jnp.concatenate(
        [jnp.concatenate([left0, zero], axis=1), jnp.concatenate([zero, left1], axis=1)], axis=0
    )
    out = jnp.dot(left, mats, preferred_element_type=jnp.float32)
    return out.reshape((2,) + (left0.shape[0], mats.shape[1]))


def apart4(lefts, mats):
    zero = jnp.zeros_like(lefts[0])
    rows = zero.shape[0]
    left = jnp.concatenate(
        [jnp.concatenate([x, zero] if j % 2 == 0 else [zero, x], axis=1) for j, x in enumerate(lefts)], axis=0
    )
    right = jnp.concatenate(
        [jnp.concatenate([mats[0], mats[1]], axis=0), jnp.concatenate([mats[2], mats[3]], axis=0)], axis=1
    )
    out = jnp.dot(left, right, preferred_element_type=jnp.float32)
    half = right.shape[1] // 2
    return [out[j * rows : (j + 1) * rows, (j // 2) * half : (j // 2 + 1) * half] for j in range(4)]


def apart_back(lefts, mats):
    rows, half = lefts.shape[1], mats.shape[0] // 2
    out = lax.dot_general(lefts.reshape(2 * rows, lefts.shape[2]), mats, NT, preferred_element_type=jnp.float32)
    return out[:rows, :half], out[rows:, half:]


def near_place(ids_ref, k, i, first, count):
    place = ids_ref[k, i] - first + REACH
    return jnp.where(place >= count, place - count, place)


def near_forward_kernel(
    groups, capacity, ids_ref, ids_row_ref, halo_ref, probe_ref, coeffs_ref, prec_ref,
    part_ref, own_ref, slot_ref, first_ref, mats_ref, ext, coeffs, prec, part, fold, mats, slots, sems
):
    blocks = probe_ref.shape[0]
    chunks = blocks // CHUNK

    def loads(c):
        own = pl.ds(c * CHUNK, CHUNK)
        return (
            pltpu.make_async_copy(coeffs_ref.at[own], coeffs.at[own], sems.at[0, c]),
            pltpu.make_async_copy(prec_ref.at[own], prec.at[own], sems.at[1, c]),
        )

    def store_part(c):
        own = pl.ds(c * CHUNK, CHUNK)
        return pltpu.make_async_copy(part.at[own], part_ref.at[own], sems.at[2, c])

    def store_mats(c):
        own = pl.ds(c * CHUNK, CHUNK)
        return pltpu.make_async_copy(mats.at[own], mats_ref.at[own], sems.at[3, c])

    own_load = pltpu.make_async_copy(probe_ref, ext.at[pl.ds(REACH, blocks)], sems.at[2, 0])
    own_load.start()

    def fetch(c):
        for load in loads(c):
            load.start()

    def ready(c):
        for load in loads(c):
            load.wait()

    for c in range(LEAD):
        fetch(c)
    ext[pl.ds(0, REACH)] = halo_ref[...]
    owner = ids_row_ref[3:4, :] // blocks
    mask = lax.broadcasted_iota(jnp.int32, (groups, blocks), 0) == owner
    rank = jnp.sum(jnp.where(mask, ranks_in(mask, blocks), 0), axis=0, keepdims=True)
    slots[...] = owner * capacity + rank
    slot_copy = pltpu.make_async_copy(slots, slot_ref, sems.at[2, 1])
    slot_copy.start()
    first = lax.axis_index("blk") * blocks
    slot_copy.wait()
    own_load.wait()

    def make(c):
        for b in range(0, CHUNK, 2):
            i = c * CHUNK + b
            rows = []
            for j in range(2):
                tiles = [ext[near_place(ids_ref, k, i + j, first, groups * blocks)] for k in range(3)]
                rows.append(jnp.concatenate(tiles, axis=1))
            near = [stacked(coeffs[i + j, pl.ds(0, 3)]) for j in range(2)]
            mixed = apart(rows[0], rows[1], jnp.concatenate(near, axis=0))
            part[pl.ds(i, 2)] = ext[pl.ds(REACH + i, 2)].astype(jnp.float32) - mixed
            for j in range(2):
                folded = lax.dot_general(prec[i + j], coeffs[i + j, 3], NT, preferred_element_type=jnp.float32)
                fold[i + j] = folded.astype(jnp.bfloat16)
        store_part(c).start()

    def use(c):
        for b in range(0, CHUNK, 2):
            i = c * CHUNK + b
            halves = []
            for j in range(2):
                high = part[i + j].astype(jnp.bfloat16)
                low = (part[i + j] - high.astype(jnp.float32)).astype(jnp.bfloat16)
                halves.append(jnp.concatenate([high, low], axis=0))
            both = apart(halves[0], halves[1], stacked(fold[pl.ds(i, 2)]))
            rows = both.shape[1] // 2
            own_ref[pl.ds(i, 2)] = both[:, :rows] + both[:, rows:]
            for j in range(2):
                mat = jnp.dot(coeffs[i + j, 3], fold[i + j], preferred_element_type=jnp.float32)
                mats[i + j] = mat.astype(jnp.bfloat16)
        store_mats(c).start()

    ready(0)
    fetch(LEAD)
    make(0)

    @pl.loop(1, chunks)
    def _(c):
        ready(c)

        @pl.when(c + LEAD < chunks)
        def _():
            fetch(c + LEAD)

        use(c - 1)
        make(c)

    use(chunks - 1)
    first_ref[...] = mats[pl.ds(0, HELD * CHUNK)]
    for c in range(chunks):
        store_part(c).wait()
        store_mats(c).wait()


def far_kernel(slot, own_ref, far_ref, first_ref, mats_ref, parcel_ref, mats, sems):
    blocks = own_ref.shape[0]
    chunks = blocks // CHUNK

    def load(c):
        own = pl.ds(c * CHUNK, CHUNK)
        return pltpu.make_async_copy(mats_ref.at[own], mats.at[own], sems.at[c])

    for c in range(HELD, chunks):
        load(c).start()
    parcel_ref[...] = jnp.zeros_like(parcel_ref)

    def send_back(c, pair):
        for b in range(0, CHUNK, 4):
            i = c * CHUNK + b
            mixed = apart4([far_ref[slot[0, i + j]] for j in range(4)], [pair[i + j] for j in range(4)])
            for j in range(4):
                parcel_ref[slot[0, i + j]] = (own_ref[i + j] - mixed[j]).astype(jnp.bfloat16)

    for c in range(HELD):
        send_back(c, first_ref)
    for c in range(HELD, chunks, 2):
        piece = range(c, min(c + 2, chunks))
        for c in piece:
            load(c).wait()
        for c in piece:
            send_back(c, mats)


def near_back_kernel(
    groups, ids_ref, slot_ref, far_ref, part_ref, coeffs_ref, prec_ref,
    total, halo_ref, white, scaled, part, coeffs, prec, sems
):
    blocks, _, points = white.shape
    chunks = blocks // CHUNK

    def load(c, which):
        own = pl.ds(c * CHUNK, CHUNK)
        source, target = (
            (part_ref.at[own], part.at[own]),
            (coeffs_ref.at[own, 3], coeffs.at[own, 3]),
            (prec_ref.at[own], prec.at[own]),
            (coeffs_ref.at[own, pl.ds(0, 3)], coeffs.at[own, pl.ds(0, 3)]),
        )[which]
        return pltpu.make_async_copy(source, target, sems.at[which, c])

    def fetch(c):
        for which in range(4):
            load(c, which).start()

    for which in range(3):
        load(0, which).start()
    load(0, 3).start()
    for c in range(1, LEAD):
        fetch(c)
    total[pl.ds(0, REACH)] = jnp.zeros((REACH,) + total.shape[1:], jnp.float32)
    first = lax.axis_index("blk") * blocks

    def mix(c):
        load(c, 0).wait()
        load(c, 1).wait()
        for b in range(0, CHUNK, 4):
            i = c * CHUNK + b
            mixed = apart4([far_ref[slot_ref[0, i + j]] for j in range(4)], [coeffs[i + j, 3] for j in range(4)])
            for j in range(4):
                white[i + j] = (part[i + j] - mixed[j]).astype(jnp.bfloat16)

    def scale(c):
        load(c, 2).wait()
        for b in range(0, CHUNK, 4):
            i = c * CHUNK + b
            tiles = apart4([white[i + j] for j in range(4)], [prec[i + j] for j in range(4)])
            for j in range(4):
                scaled[i + j] = tiles[j].astype(jnp.bfloat16)
                total[REACH + i + j] = scaled[i + j].astype(jnp.float32)

    def back(c):
        load(c, 3).wait()
        terms = []
        for b in range(CHUNK + AHEAD):
            if b < CHUNK and b % 2 == 0:
                i = c * CHUNK + b
                mats = [stacked(coeffs[i + j, pl.ds(0, 3)]) for j in range(2)]
                terms.extend(apart_back(scaled[pl.ds(i, 2)], jnp.concatenate(mats, axis=0)))
            if b >= AHEAD:
                i = c * CHUNK + b - AHEAD
                places = [near_place(ids_ref, k, i, first, groups * blocks) for k in range(3)]
                olds = [total[place] for place in places]
                for k in range(3):
                    total[places[k]] = olds[k] - terms[b - AHEAD][:, k * points : (k + 1) * points]

    mix(0)
    fetch(LEAD)
    scale(0)
    mix(1)
    fetch(LEAD + 1)

    @pl.loop(0, chunks - 2)
    def _(c):
        @pl.when(c + LEAD + 2 < chunks)
        def _():
            fetch(c + LEAD + 2)

        back(c)
        scale(c + 1)
        mix(c + 2)

    back(chunks - 2)
    scale(chunks - 1)
    back(chunks - 1)
    halo_ref[...] = total[pl.ds(0, REACH)].astype(halo_ref.dtype)


def sum_kernel(capacity, picks_ref, base_ref, halo_ref, back_ref, out_ref, total, sem):
    groups = back_ref.shape[0] // capacity
    blocks = out_ref.shape[0]
    total[pl.ds(0, blocks)] = base_ref[pl.ds(REACH, blocks)]
    last = pl.ds(blocks - REACH, REACH)
    total[last] = total[last] + halo_ref[...].astype(jnp.float32)

    @pl.loop(0, groups, unroll=8)
    def _(g):
        picks = [picks_ref[r, g] for r in range(capacity)]
        places = [jnp.where(pick > 0, pick - 1, blocks) for pick in picks]
        olds = [total[place] for place in places]
        for r in range(capacity):
            total[places[r]] = olds[r] - back_ref[g * capacity + r].astype(jnp.float32)

    store = pltpu.make_async_copy(total.at[pl.ds(0, blocks)], out_ref, sem)
    store.start()
    store.wait()


def per_device(probe_vecs, coeffs, cond_prec, neighbours):
    blocks, probes, points = probe_vecs.shape
    groups = lax.axis_size("blk")
    capacity = max(2, blocks // (groups - 1) + 1)
    slots = groups * capacity
    picks_shape = (-(-capacity // 8) * 8, -(-groups // 128) * 128)
    chunks = blocks // CHUNK
    bf16, f32 = jnp.bfloat16, jnp.float32
    tile = (probes, points)
    flops = 2 * blocks * probes * points * points

    def exchange(x):
        return lax.all_to_all(x, "blk", split_axis=0, concat_axis=0, tiled=True)

    ids = neighbours.T
    sent_ids, tail, scalar_ids = pl.pallas_call(
        prep_kernel,
        name="prep",
        out_shape=(
            jax.ShapeDtypeStruct((groups, blocks), jnp.int32),
            jax.ShapeDtypeStruct((REACH,) + tile, bf16),
            pltpu.SMEM(ids.shape, jnp.int32),
        ),
        in_specs=[HBM, HBM],
        out_specs=(VMEM, VMEM, SMEM),
        scratch_shapes=[pltpu.VMEM(ids.shape, jnp.int32), pltpu.SemaphoreType.DMA((3,))],
        compiler_params=params(8),
    )(in_hbm(ids), in_hbm(probe_vecs))
    halo = passed_along(tail, "blk", 1)
    all_ids = exchange(sent_ids)
    all_ids, halo = lax.optimization_barrier((all_ids, halo))
    outgoing, picks = pl.pallas_call(
        functools.partial(pick_kernel, capacity),
        name="pick_tiles",
        out_shape=(
            jax.ShapeDtypeStruct((slots,) + tile, bf16),
            pltpu.SMEM(picks_shape, jnp.int32),
        ),
        in_specs=[VMEM, HBM],
        out_specs=(HBM, SMEM),
        scratch_shapes=[
            pltpu.VMEM((blocks,) + tile, bf16),
            pltpu.VMEM((slots,) + tile, bf16),
            pltpu.VMEM(picks_shape, jnp.int32),
            pltpu.SemaphoreType.DMA((2 + STORES,)),
        ],
        compiler_params=params(8),
        cost_estimate=pl.CostEstimate(flops=0, bytes_accessed=2 * slots * 4096, transcendentals=0),
    )(all_ids, in_hbm(probe_vecs))
    arrived = exchange(outgoing.reshape((groups, capacity) + tile)).reshape((slots,) + tile)
    mats = (blocks, points, points)
    all_mats = pltpu.VMEM((blocks, 4, points, points), bf16)
    tiles_f32 = jax.ShapeDtypeStruct((blocks,) + tile, f32)
    part, own_far, slot_of, first_mats, far_mats = pl.pallas_call(
        functools.partial(near_forward_kernel, groups, capacity),
        name="near_forward",
        out_shape=(
            pltpu.HBM((blocks,) + tile, f32),
            tiles_f32,
            pltpu.SMEM((1, blocks), jnp.int32),
            jax.ShapeDtypeStruct((HELD * CHUNK, points, points), bf16),
            pltpu.HBM(mats, bf16),
        ),
        in_specs=[SMEM, VMEM, VMEM, HBM, HBM, HBM],
        out_specs=(HBM, VMEM, SMEM, VMEM, HBM),
        scratch_shapes=[
            pltpu.VMEM((REACH + blocks,) + tile, bf16),
            all_mats,
            pltpu.VMEM(mats, bf16),
            pltpu.VMEM((blocks,) + tile, f32),
            pltpu.VMEM(mats, bf16),
            pltpu.VMEM(mats, bf16),
            pltpu.VMEM((1, blocks), jnp.int32),
            pltpu.SemaphoreType.DMA((4, chunks)),
        ],
        compiler_params=params(40),
        cost_estimate=pl.CostEstimate(flops=20 * flops, bytes_accessed=28 * 2**20, transcendentals=0),
    )(scalar_ids, ids, halo, in_hbm(probe_vecs), in_hbm(coeffs), in_hbm(cond_prec))
    parcel = pl.pallas_call(
        far_kernel,
        name="far_terms",
        out_shape=jax.ShapeDtypeStruct((slots,) + tile, bf16),
        in_specs=[SMEM, VMEM, VMEM, VMEM, HBM],
        out_specs=VMEM,
        scratch_shapes=[
            pltpu.VMEM(mats, bf16),
            pltpu.SemaphoreType.DMA((chunks,)),
        ],
        compiler_params=params(16),
        cost_estimate=pl.CostEstimate(flops=flops, bytes_accessed=6 * 2**20, transcendentals=0),
    )(slot_of, own_far, arrived, first_mats, in_hbm(far_mats))
    parcel, arrived = lax.optimization_barrier((parcel, arrived))
    returned = exchange(parcel.reshape((groups, capacity) + tile)).reshape((slots,) + tile)
    base, halo_back = pl.pallas_call(
        functools.partial(near_back_kernel, groups),
        name="near_back",
        out_shape=(
            jax.ShapeDtypeStruct((REACH + blocks,) + tile, f32),
            jax.ShapeDtypeStruct((REACH,) + tile, bf16),
        ),
        in_specs=[SMEM, SMEM, VMEM, HBM, HBM, HBM],
        out_specs=(VMEM, VMEM),
        scratch_shapes=[
            pltpu.VMEM((blocks,) + tile, bf16),
            pltpu.VMEM((blocks,) + tile, bf16),
            pltpu.VMEM((blocks,) + tile, f32),
            all_mats,
            pltpu.VMEM(mats, bf16),
            pltpu.SemaphoreType.DMA((4, chunks)),
        ],
        compiler_params=params(36),
        cost_estimate=pl.CostEstimate(flops=5 * flops, bytes_accessed=23 * 2**20, transcendentals=0),
    )(scalar_ids, slot_of, arrived, in_hbm(part), in_hbm(coeffs), in_hbm(cond_prec))
    halo_sum = passed_along(halo_back, "blk", -1)
    return pl.pallas_call(
        functools.partial(sum_kernel, capacity),
        name="final_sum",
        out_shape=jax.ShapeDtypeStruct((blocks,) + tile, f32),
        in_specs=[SMEM, VMEM, VMEM, VMEM],
        out_specs=HBM,
        scratch_shapes=[
            pltpu.VMEM((blocks + 1,) + tile, f32),
            pltpu.SemaphoreType.DMA,
        ],
        compiler_params=params(8),
        cost_estimate=pl.CostEstimate(flops=0, bytes_accessed=3 * 2**20, transcendentals=0),
    )(picks, base, halo_sum, returned)


def solution(mesh):
    in_specs = (
        P("blk", None, None),
        P("blk", None, None, None),
        P("blk", None, None),
        P("blk", None),
    )
    return jax.shard_map(
        per_device, mesh=mesh, in_specs=in_specs, out_specs=P("blk", None, None), check_vma=False
    )
```

```python
import functools

import jax
import jax.numpy as jnp
from jax import lax
from jax.experimental import pallas as pl
from jax.experimental.pallas import tpu as pltpu
from jax.sharding import PartitionSpec as P

REACH = 16
CHUNK = 16
AHEAD = 4
HELD = 3
LEAD = 3
STORES = 4
VMEM = pl.BlockSpec(memory_space=pltpu.VMEM)
SMEM = pl.BlockSpec(memory_space=pltpu.SMEM)
HBM = pl.BlockSpec(memory_space=pl.ANY)
NT = (((1,), (1,)), ((), ()))


def params(mib):
    return pltpu.CompilerParams(vmem_limit_bytes=mib * 2**20)


def in_hbm(x):
    return pltpu.with_memory_space_constraint(x, pltpu.HBM)


def passed_along(block, axis, distance):
    size = lax.axis_size(axis)
    return lax.ppermute(block, axis, [((i - distance) % size, i) for i in range(size)])


def earlier_matrix(blocks):
    row = lax.broadcasted_iota(jnp.int32, (blocks, blocks), 0)
    col = lax.broadcasted_iota(jnp.int32, (blocks, blocks), 1)
    return (row < col).astype(jnp.float32).astype(jnp.bfloat16)


def ranks_in(mask, blocks):
    chosen = mask.astype(jnp.float32).astype(jnp.bfloat16)
    return jnp.dot(chosen, earlier_matrix(blocks), preferred_element_type=jnp.float32).astype(jnp.int32)


def prep_kernel(ids_ref, probe_ref, sent_ref, tail_ref, scalars_ref, ids, sems):
    blocks = probe_ref.shape[0]
    ids_copy = pltpu.make_async_copy(ids_ref, ids, sems.at[0])
    tail_copy = pltpu.make_async_copy(probe_ref.at[pl.ds(blocks - REACH, REACH)], tail_ref, sems.at[1])
    scalars_copy = pltpu.make_async_copy(ids_ref, scalars_ref, sems.at[2])
    ids_copy.start()
    tail_copy.start()
    scalars_copy.start()
    ids_copy.wait()
    sent_ref[...] = jnp.broadcast_to(ids[3:4, :], sent_ref.shape)
    tail_copy.wait()
    scalars_copy.wait()


def pick_kernel(capacity, ids_ref, probe_ref, out_ref, picks_smem, probe, out, picks_ref, sems):
    groups, blocks = ids_ref.shape
    load = pltpu.make_async_copy(probe_ref, probe, sems.at[0])
    load.start()
    me = lax.axis_index("blk")
    local = ids_ref[...] - me * blocks
    mask = (local >= 0) & (local < blocks)
    rank = ranks_in(mask, blocks)
    row = lax.broadcasted_iota(jnp.int32, (picks_ref.shape[0], groups), 0)
    ones = jnp.ones((picks_ref.shape[0], blocks), jnp.bfloat16)
    picks = jnp.zeros(row.shape, jnp.float32)
    for r in range(capacity):
        chosen = jnp.where(mask & (rank == r), local + 1, 0).astype(jnp.float32).astype(jnp.bfloat16)
        found = lax.dot_general(ones, chosen, NT, preferred_element_type=jnp.float32)
        picks = jnp.where(row == r, found, picks)
    picks_ref[:, pl.ds(0, groups)] = picks.astype(jnp.int32)
    copy = pltpu.make_async_copy(picks_ref, picks_smem, sems.at[1])
    copy.start()
    copy.wait()
    load.wait()
    part = groups // STORES

    def store(p):
        rows = pl.ds(p * part * capacity, part * capacity)
        return pltpu.make_async_copy(out.at[rows], out_ref.at[rows], sems.at[2 + p])

    @pl.loop(0, STORES)
    def _(p):
        @pl.loop(p * part, (p + 1) * part, step=4)
        def _(first):
            for j in range(4):
                for r in range(capacity):
                    out[(first + j) * capacity + r] = probe[jnp.maximum(picks_smem[r, first + j] - 1, 0)]

        store(p).start()

    for p in range(STORES):
        store(p).wait()


def stacked(mats):
    return mats.reshape(-1, mats.shape[-1])


def apart(left0, left1, mats):
    zero = jnp.zeros_like(left0)
    left = jnp.concatenate(
        [jnp.concatenate([left0, zero], axis=1), jnp.concatenate([zero, left1], axis=1)], axis=0
    )
    out = jnp.dot(left, mats, preferred_element_type=jnp.float32)
    return out.reshape((2,) + (left0.shape[0], mats.shape[1]))


def apart4(lefts, mats):
    zero = jnp.zeros_like(lefts[0])
    rows = zero.shape[0]
    left = jnp.concatenate(
        [jnp.concatenate([x, zero] if j % 2 == 0 else [zero, x], axis=1) for j, x in enumerate(lefts)], axis=0
    )
    right = jnp.concatenate(
        [jnp.concatenate([mats[0], mats[1]], axis=0), jnp.concatenate([mats[2], mats[3]], axis=0)], axis=1
    )
    out = jnp.dot(left, right, preferred_element_type=jnp.float32)
    half = right.shape[1] // 2
    return [out[j * rows : (j + 1) * rows, (j // 2) * half : (j // 2 + 1) * half] for j in range(4)]


def apart_back(lefts, mats):
    rows, half = lefts.shape[1], mats.shape[0] // 2
    out = lax.dot_general(lefts.reshape(2 * rows, lefts.shape[2]), mats, NT, preferred_element_type=jnp.float32)
    return out[:rows, :half], out[rows:, half:]


def near_place(ids_ref, k, i, first, count):
    place = ids_ref[k, i] - first + REACH
    return jnp.where(place >= count, place - count, place)


def near_forward_kernel(
    groups, capacity, ids_ref, ids_row_ref, halo_ref, probe_ref, coeffs_ref, prec_ref,
    part_ref, own_ref, slot_ref, first_ref, mats_ref, ext, coeffs, prec, part, fold, mats, slots, sems
):
    blocks = probe_ref.shape[0]
    chunks = blocks // CHUNK

    def loads(c):
        own = pl.ds(c * CHUNK, CHUNK)
        return (
            pltpu.make_async_copy(coeffs_ref.at[own], coeffs.at[own], sems.at[0, c]),
            pltpu.make_async_copy(prec_ref.at[own], prec.at[own], sems.at[1, c]),
        )

    def store_part(c):
        own = pl.ds(c * CHUNK, CHUNK)
        return pltpu.make_async_copy(part.at[own], part_ref.at[own], sems.at[2, c])

    def store_mats(c):
        own = pl.ds(c * CHUNK, CHUNK)
        return pltpu.make_async_copy(mats.at[own], mats_ref.at[own], sems.at[3, c])

    own_load = pltpu.make_async_copy(probe_ref, ext.at[pl.ds(REACH, blocks)], sems.at[2, 0])
    own_load.start()

    def fetch(c):
        for load in loads(c):
            load.start()

    def ready(c):
        for load in loads(c):
            load.wait()

    for c in range(LEAD):
        fetch(c)
    ext[pl.ds(0, REACH)] = halo_ref[...]
    owner = ids_row_ref[3:4, :] // blocks
    mask = lax.broadcasted_iota(jnp.int32, (groups, blocks), 0) == owner
    rank = jnp.sum(jnp.where(mask, ranks_in(mask, blocks), 0), axis=0, keepdims=True)
    slots[...] = owner * capacity + rank
    slot_copy = pltpu.make_async_copy(slots, slot_ref, sems.at[2, 1])
    slot_copy.start()
    first = lax.axis_index("blk") * blocks
    slot_copy.wait()
    own_load.wait()

    def make(c):
        for b in range(0, CHUNK, 2):
            i = c * CHUNK + b
            rows = []
            for j in range(2):
                tiles = [ext[near_place(ids_ref, k, i + j, first, groups * blocks)] for k in range(3)]
                rows.append(jnp.concatenate(tiles, axis=1))
            near = [stacked(coeffs[i + j, pl.ds(0, 3)]) for j in range(2)]
            mixed = apart(rows[0], rows[1], jnp.concatenate(near, axis=0))
            part[pl.ds(i, 2)] = ext[pl.ds(REACH + i, 2)].astype(jnp.float32) - mixed
            for j in range(2):
                folded = lax.dot_general(prec[i + j], coeffs[i + j, 3], NT, preferred_element_type=jnp.float32)
                fold[i + j] = folded.astype(jnp.bfloat16)
        store_part(c).start()

    def use(c):
        for b in range(0, CHUNK, 2):
            i = c * CHUNK + b
            halves = []
            for j in range(2):
                high = part[i + j].astype(jnp.bfloat16)
                low = (part[i + j] - high.astype(jnp.float32)).astype(jnp.bfloat16)
                halves.append(jnp.concatenate([high, low], axis=0))
            both = apart(halves[0], halves[1], stacked(fold[pl.ds(i, 2)]))
            rows = both.shape[1] // 2
            own_ref[pl.ds(i, 2)] = both[:, :rows] + both[:, rows:]
            for j in range(2):
                mat = jnp.dot(coeffs[i + j, 3], fold[i + j], preferred_element_type=jnp.float32)
                mats[i + j] = mat.astype(jnp.bfloat16)
        store_mats(c).start()

    ready(0)
    fetch(LEAD)
    make(0)

    @pl.loop(1, chunks)
    def _(c):
        ready(c)

        @pl.when(c + LEAD < chunks)
        def _():
            fetch(c + LEAD)

        use(c - 1)
        make(c)

    use(chunks - 1)
    first_ref[...] = mats[pl.ds(0, HELD * CHUNK)]
    for c in range(chunks):
        store_part(c).wait()
        store_mats(c).wait()


def far_kernel(slot, own_ref, far_ref, first_ref, mats_ref, parcel_ref, mats, sems):
    blocks = own_ref.shape[0]
    chunks = blocks // CHUNK

    def load(c):
        own = pl.ds(c * CHUNK, CHUNK)
        return pltpu.make_async_copy(mats_ref.at[own], mats.at[own], sems.at[c])

    for c in range(HELD, chunks):
        load(c).start()

    def send_back(c, pair):
        for b in range(0, CHUNK, 4):
            i = c * CHUNK + b
            mixed = apart4([far_ref[slot[0, i + j]] for j in range(4)], [pair[i + j] for j in range(4)])
            for j in range(4):
                parcel_ref[slot[0, i + j]] = (own_ref[i + j] - mixed[j]).astype(jnp.bfloat16)

    @pl.loop(0, HELD)
    def _(c):
        send_back(c, first_ref)

    @pl.loop(HELD, chunks)
    def _(c):
        load(c).wait()
        send_back(c, mats)


def near_back_kernel(
    groups, ids_ref, slot_ref, far_ref, part_ref, coeffs_ref, prec_ref,
    total, halo_ref, white, scaled, part, coeffs, prec, sems
):
    blocks, _, points = white.shape
    chunks = blocks // CHUNK

    def load(c, which):
        own = pl.ds(c * CHUNK, CHUNK)
        source, target = (
            (part_ref.at[own], part.at[own]),
            (coeffs_ref.at[own, 3], coeffs.at[own, 3]),
            (prec_ref.at[own], prec.at[own]),
            (coeffs_ref.at[own, pl.ds(0, 3)], coeffs.at[own, pl.ds(0, 3)]),
        )[which]
        return pltpu.make_async_copy(source, target, sems.at[which, c])

    def fetch(c):
        for which in range(4):
            load(c, which).start()

    for which in range(3):
        load(0, which).start()
    load(0, 3).start()
    for c in range(1, LEAD):
        fetch(c)
    total[pl.ds(0, REACH)] = jnp.zeros((REACH,) + total.shape[1:], jnp.float32)
    first = lax.axis_index("blk") * blocks

    def mix(c):
        load(c, 0).wait()
        load(c, 1).wait()
        for b in range(0, CHUNK, 4):
            i = c * CHUNK + b
            mixed = apart4([far_ref[slot_ref[0, i + j]] for j in range(4)], [coeffs[i + j, 3] for j in range(4)])
            for j in range(4):
                white[i + j] = (part[i + j] - mixed[j]).astype(jnp.bfloat16)

    def scale(c):
        load(c, 2).wait()
        for b in range(0, CHUNK, 4):
            i = c * CHUNK + b
            tiles = apart4([white[i + j] for j in range(4)], [prec[i + j] for j in range(4)])
            for j in range(4):
                scaled[i + j] = tiles[j].astype(jnp.bfloat16)
                total[REACH + i + j] = scaled[i + j].astype(jnp.float32)

    def back(c):
        load(c, 3).wait()
        terms = []
        for b in range(CHUNK + AHEAD):
            if b < CHUNK and b % 2 == 0:
                i = c * CHUNK + b
                mats = [stacked(coeffs[i + j, pl.ds(0, 3)]) for j in range(2)]
                terms.extend(apart_back(scaled[pl.ds(i, 2)], jnp.concatenate(mats, axis=0)))
            if b >= AHEAD:
                i = c * CHUNK + b - AHEAD
                places = [near_place(ids_ref, k, i, first, groups * blocks) for k in range(3)]
                olds = [total[place] for place in places]
                for k in range(3):
                    total[places[k]] = olds[k] - terms[b - AHEAD][:, k * points : (k + 1) * points]

    mix(0)
    fetch(LEAD)
    scale(0)
    mix(1)
    fetch(LEAD + 1)

    @pl.loop(0, chunks - 2)
    def _(c):
        @pl.when(c + LEAD + 2 < chunks)
        def _():
            fetch(c + LEAD + 2)

        back(c)
        scale(c + 1)
        mix(c + 2)

    back(chunks - 2)
    scale(chunks - 1)
    back(chunks - 1)
    halo_ref[...] = total[pl.ds(0, REACH)].astype(halo_ref.dtype)


def sum_kernel(capacity, picks_ref, base_ref, halo_ref, back_ref, out_ref, total, sem):
    groups = back_ref.shape[0] // capacity
    blocks = out_ref.shape[0]

    @pl.loop(0, blocks, unroll=8)
    def _(i):
        total[i] = base_ref[REACH + i]

    last = pl.ds(blocks - REACH, REACH)
    total[last] = total[last] + halo_ref[...].astype(jnp.float32)

    @pl.loop(0, groups, unroll=4)
    def _(g):
        picks = [picks_ref[r, g] for r in range(capacity)]
        places = [jnp.where(pick > 0, pick - 1, blocks) for pick in picks]
        olds = [total[place] for place in places]
        for r in range(capacity):
            total[places[r]] = olds[r] - back_ref[g * capacity + r].astype(jnp.float32)

    store = pltpu.make_async_copy(total.at[pl.ds(0, blocks)], out_ref, sem)
    store.start()
    store.wait()


def per_device(probe_vecs, coeffs, cond_prec, neighbours):
    blocks, probes, points = probe_vecs.shape
    groups = lax.axis_size("blk")
    capacity = max(2, blocks // (groups - 1) + 1)
    slots = groups * capacity
    picks_shape = (-(-capacity // 8) * 8, -(-groups // 128) * 128)
    chunks = blocks // CHUNK
    bf16, f32 = jnp.bfloat16, jnp.float32
    tile = (probes, points)
    flops = 2 * blocks * probes * points * points

    def exchange(x):
        return lax.all_to_all(x, "blk", split_axis=0, concat_axis=0, tiled=True)

    ids = neighbours.T
    sent_ids, tail, scalar_ids = pl.pallas_call(
        prep_kernel,
        name="prep",
        out_shape=(
            jax.ShapeDtypeStruct((groups, blocks), jnp.int32),
            jax.ShapeDtypeStruct((REACH,) + tile, bf16),
            pltpu.SMEM(ids.shape, jnp.int32),
        ),
        in_specs=[HBM, HBM],
        out_specs=(VMEM, VMEM, SMEM),
        scratch_shapes=[pltpu.VMEM(ids.shape, jnp.int32), pltpu.SemaphoreType.DMA((3,))],
        compiler_params=params(8),
    )(in_hbm(ids), in_hbm(probe_vecs))
    halo = passed_along(tail, "blk", 1)
    all_ids = exchange(sent_ids)
    all_ids, halo = lax.optimization_barrier((all_ids, halo))
    outgoing, picks = pl.pallas_call(
        functools.partial(pick_kernel, capacity),
        name="pick_tiles",
        out_shape=(
            jax.ShapeDtypeStruct((slots,) + tile, bf16),
            pltpu.SMEM(picks_shape, jnp.int32),
        ),
        in_specs=[VMEM, HBM],
        out_specs=(HBM, SMEM),
        scratch_shapes=[
            pltpu.VMEM((blocks,) + tile, bf16),
            pltpu.VMEM((slots,) + tile, bf16),
            pltpu.VMEM(picks_shape, jnp.int32),
            pltpu.SemaphoreType.DMA((2 + STORES,)),
        ],
        compiler_params=params(8),
        cost_estimate=pl.CostEstimate(flops=0, bytes_accessed=2 * slots * 4096, transcendentals=0),
    )(all_ids, in_hbm(probe_vecs))
    arrived = exchange(outgoing.reshape((groups, capacity) + tile)).reshape((slots,) + tile)
    mats = (blocks, points, points)
    all_mats = pltpu.VMEM((blocks, 4, points, points), bf16)
    tiles_f32 = jax.ShapeDtypeStruct((blocks,) + tile, f32)
    part, own_far, slot_of, first_mats, far_mats = pl.pallas_call(
        functools.partial(near_forward_kernel, groups, capacity),
        name="near_forward",
        out_shape=(
            pltpu.HBM((blocks,) + tile, f32),
            tiles_f32,
            pltpu.SMEM((1, blocks), jnp.int32),
            jax.ShapeDtypeStruct((HELD * CHUNK, points, points), bf16),
            pltpu.HBM(mats, bf16),
        ),
        in_specs=[SMEM, VMEM, VMEM, HBM, HBM, HBM],
        out_specs=(HBM, VMEM, SMEM, VMEM, HBM),
        scratch_shapes=[
            pltpu.VMEM((REACH + blocks,) + tile, bf16),
            all_mats,
            pltpu.VMEM(mats, bf16),
            pltpu.VMEM((blocks,) + tile, f32),
            pltpu.VMEM(mats, bf16),
            pltpu.VMEM(mats, bf16),
            pltpu.VMEM((1, blocks), jnp.int32),
            pltpu.SemaphoreType.DMA((4, chunks)),
        ],
        compiler_params=params(40),
        cost_estimate=pl.CostEstimate(flops=20 * flops, bytes_accessed=28 * 2**20, transcendentals=0),
    )(scalar_ids, ids, halo, in_hbm(probe_vecs), in_hbm(coeffs), in_hbm(cond_prec))
    parcel = pl.pallas_call(
        far_kernel,
        name="far_terms",
        out_shape=jax.ShapeDtypeStruct((slots,) + tile, bf16),
        in_specs=[SMEM, VMEM, VMEM, VMEM, HBM],
        out_specs=VMEM,
        scratch_shapes=[
            pltpu.VMEM(mats, bf16),
            pltpu.SemaphoreType.DMA((chunks,)),
        ],
        compiler_params=params(16),
        cost_estimate=pl.CostEstimate(flops=flops, bytes_accessed=6 * 2**20, transcendentals=0),
    )(slot_of, own_far, arrived, first_mats, in_hbm(far_mats))
    parcel, arrived = lax.optimization_barrier((parcel, arrived))
    returned = exchange(parcel.reshape((groups, capacity) + tile)).reshape((slots,) + tile)
    base, halo_back = pl.pallas_call(
        functools.partial(near_back_kernel, groups),
        name="near_back",
        out_shape=(
            jax.ShapeDtypeStruct((REACH + blocks,) + tile, f32),
            jax.ShapeDtypeStruct((REACH,) + tile, bf16),
        ),
        in_specs=[SMEM, SMEM, VMEM, HBM, HBM, HBM],
        out_specs=(VMEM, VMEM),
        scratch_shapes=[
            pltpu.VMEM((blocks,) + tile, bf16),
            pltpu.VMEM((blocks,) + tile, bf16),
            pltpu.VMEM((blocks,) + tile, f32),
            all_mats,
            pltpu.VMEM(mats, bf16),
            pltpu.SemaphoreType.DMA((4, chunks)),
        ],
        compiler_params=params(36),
        cost_estimate=pl.CostEstimate(flops=5 * flops, bytes_accessed=23 * 2**20, transcendentals=0),
    )(scalar_ids, slot_of, arrived, in_hbm(part), in_hbm(coeffs), in_hbm(cond_prec))
    halo_sum = passed_along(halo_back, "blk", -1)
    return pl.pallas_call(
        functools.partial(sum_kernel, capacity),
        name="final_sum",
        out_shape=jax.ShapeDtypeStruct((blocks,) + tile, f32),
        in_specs=[SMEM, VMEM, VMEM, VMEM],
        out_specs=HBM,
        scratch_shapes=[
            pltpu.VMEM((blocks + 1,) + tile, f32),
            pltpu.SemaphoreType.DMA,
        ],
        compiler_params=params(8),
        cost_estimate=pl.CostEstimate(flops=0, bytes_accessed=3 * 2**20, transcendentals=0),
    )(picks, base, halo_sum, returned)


def solution(mesh):
    in_specs = (
        P("blk", None, None),
        P("blk", None, None, None),
        P("blk", None, None),
        P("blk", None),
    )
    return jax.shard_map(
        per_device, mesh=mesh, in_specs=in_specs, out_specs=P("blk", None, None), check_vma=False
    )
```

```python
import functools

import jax
import jax.numpy as jnp
from jax import lax
from jax.experimental import pallas as pl
from jax.experimental.pallas import tpu as pltpu
from jax.sharding import PartitionSpec as P

REACH = 16
CHUNK = 16
AHEAD = 4
HELD = 3
LEAD = 3
STORES = 4
VMEM = pl.BlockSpec(memory_space=pltpu.VMEM)
SMEM = pl.BlockSpec(memory_space=pltpu.SMEM)
HBM = pl.BlockSpec(memory_space=pl.ANY)
NT = (((1,), (1,)), ((), ()))


def params(mib):
    return pltpu.CompilerParams(vmem_limit_bytes=mib * 2**20)


def in_hbm(x):
    return pltpu.with_memory_space_constraint(x, pltpu.HBM)


def passed_along(block, axis, distance):
    size = lax.axis_size(axis)
    return lax.ppermute(block, axis, [((i - distance) % size, i) for i in range(size)])


def earlier_matrix(blocks):
    row = lax.broadcasted_iota(jnp.int32, (blocks, blocks), 0)
    col = lax.broadcasted_iota(jnp.int32, (blocks, blocks), 1)
    return (row < col).astype(jnp.float32).astype(jnp.bfloat16)


def ranks_in(mask, blocks):
    chosen = mask.astype(jnp.float32).astype(jnp.bfloat16)
    return jnp.dot(chosen, earlier_matrix(blocks), preferred_element_type=jnp.float32).astype(jnp.int32)


def prep_kernel(ids_ref, probe_ref, sent_ref, tail_ref, scalars_ref, ids, sems):
    blocks = probe_ref.shape[0]
    ids_copy = pltpu.make_async_copy(ids_ref, ids, sems.at[0])
    tail_copy = pltpu.make_async_copy(probe_ref.at[pl.ds(blocks - REACH, REACH)], tail_ref, sems.at[1])
    scalars_copy = pltpu.make_async_copy(ids_ref, scalars_ref, sems.at[2])
    ids_copy.start()
    tail_copy.start()
    scalars_copy.start()
    ids_copy.wait()
    sent_ref[...] = jnp.broadcast_to(ids[3:4, :], sent_ref.shape)
    tail_copy.wait()
    scalars_copy.wait()


def pick_kernel(capacity, ids_ref, probe_ref, out_ref, picks_smem, probe, out, picks_ref, sems):
    groups, blocks = ids_ref.shape
    load = pltpu.make_async_copy(probe_ref, probe, sems.at[0])
    load.start()
    me = lax.axis_index("blk")
    local = ids_ref[...] - me * blocks
    mask = (local >= 0) & (local < blocks)
    rank = ranks_in(mask, blocks)
    row = lax.broadcasted_iota(jnp.int32, (picks_ref.shape[0], groups), 0)
    ones = jnp.ones((picks_ref.shape[0], blocks), jnp.bfloat16)
    picks = jnp.zeros(row.shape, jnp.float32)
    for r in range(capacity):
        chosen = jnp.where(mask & (rank == r), local + 1, 0).astype(jnp.float32).astype(jnp.bfloat16)
        found = lax.dot_general(ones, chosen, NT, preferred_element_type=jnp.float32)
        picks = jnp.where(row == r, found, picks)
    picks_ref[:, pl.ds(0, groups)] = picks.astype(jnp.int32)
    copy = pltpu.make_async_copy(picks_ref, picks_smem, sems.at[1])
    copy.start()
    copy.wait()
    load.wait()
    part = groups // STORES

    def store(p):
        rows = pl.ds(p * part * capacity, part * capacity)
        return pltpu.make_async_copy(out.at[rows], out_ref.at[rows], sems.at[2 + p])

    for p in range(STORES):

        @pl.loop(p * part, (p + 1) * part, unroll=8)
        def _(g):
            for r in range(capacity):
                out[g * capacity + r] = probe[jnp.maximum(picks_smem[r, g] - 1, 0)]

        store(p).start()
    for p in range(STORES):
        store(p).wait()


def stacked(mats):
    return mats.reshape(-1, mats.shape[-1])


def apart(left0, left1, mats):
    zero = jnp.zeros_like(left0)
    left = jnp.concatenate(
        [jnp.concatenate([left0, zero], axis=1), jnp.concatenate([zero, left1], axis=1)], axis=0
    )
    out = jnp.dot(left, mats, preferred_element_type=jnp.float32)
    return out.reshape((2,) + (left0.shape[0], mats.shape[1]))


def apart4(lefts, mats):
    zero = jnp.zeros_like(lefts[0])
    rows = zero.shape[0]
    left = jnp.concatenate(
        [jnp.concatenate([x, zero] if j % 2 == 0 else [zero, x], axis=1) for j, x in enumerate(lefts)], axis=0
    )
    right = jnp.concatenate(
        [jnp.concatenate([mats[0], mats[1]], axis=0), jnp.concatenate([mats[2], mats[3]], axis=0)], axis=1
    )
    out = jnp.dot(left, right, preferred_element_type=jnp.float32)
    half = right.shape[1] // 2
    return [out[j * rows : (j + 1) * rows, (j // 2) * half : (j // 2 + 1) * half] for j in range(4)]


def apart_back(lefts, mats):
    rows, half = lefts.shape[1], mats.shape[0] // 2
    out = lax.dot_general(lefts.reshape(2 * rows, lefts.shape[2]), mats, NT, preferred_element_type=jnp.float32)
    return out[:rows, :half], out[rows:, half:]


def near_place(ids_ref, k, i, first, count):
    place = ids_ref[k, i] - first + REACH
    return jnp.where(place >= count, place - count, place)


def near_forward_kernel(
    groups, capacity, ids_ref, ids_row_ref, halo_ref, probe_ref, coeffs_ref, prec_ref,
    part_ref, own_ref, slot_ref, first_ref, mats_ref, ext, coeffs, prec, part, fold, mats, slots, sems
):
    blocks = probe_ref.shape[0]
    chunks = blocks // CHUNK

    def loads(c):
        own = pl.ds(c * CHUNK, CHUNK)
        return (
            pltpu.make_async_copy(coeffs_ref.at[own], coeffs.at[own], sems.at[0, c]),
            pltpu.make_async_copy(prec_ref.at[own], prec.at[own], sems.at[1, c]),
        )

    def store_part(c):
        own = pl.ds(c * CHUNK, CHUNK)
        return pltpu.make_async_copy(part.at[own], part_ref.at[own], sems.at[2, c])

    def store_mats(c):
        own = pl.ds(c * CHUNK, CHUNK)
        return pltpu.make_async_copy(mats.at[own], mats_ref.at[own], sems.at[3, c])

    own_load = pltpu.make_async_copy(probe_ref, ext.at[pl.ds(REACH, blocks)], sems.at[2, 0])
    own_load.start()

    def fetch(c):
        for load in loads(c):
            load.start()

    def ready(c):
        for load in loads(c):
            load.wait()

    for c in range(LEAD):
        fetch(c)
    ext[pl.ds(0, REACH)] = halo_ref[...]
    owner = ids_row_ref[3:4, :] // blocks
    mask = lax.broadcasted_iota(jnp.int32, (groups, blocks), 0) == owner
    rank = jnp.sum(jnp.where(mask, ranks_in(mask, blocks), 0), axis=0, keepdims=True)
    slots[...] = owner * capacity + rank
    slot_copy = pltpu.make_async_copy(slots, slot_ref, sems.at[2, 1])
    slot_copy.start()
    first = lax.axis_index("blk") * blocks
    slot_copy.wait()
    own_load.wait()

    def make(c):
        for b in range(0, CHUNK, 2):
            i = c * CHUNK + b
            rows = []
            for j in range(2):
                tiles = [ext[near_place(ids_ref, k, i + j, first, groups * blocks)] for k in range(3)]
                rows.append(jnp.concatenate(tiles, axis=1))
            near = [stacked(coeffs[i + j, pl.ds(0, 3)]) for j in range(2)]
            mixed = apart(rows[0], rows[1], jnp.concatenate(near, axis=0))
            part[pl.ds(i, 2)] = ext[pl.ds(REACH + i, 2)].astype(jnp.float32) - mixed
            for j in range(2):
                folded = lax.dot_general(prec[i + j], coeffs[i + j, 3], NT, preferred_element_type=jnp.float32)
                fold[i + j] = folded.astype(jnp.bfloat16)
        store_part(c).start()

    def use(c):
        for b in range(0, CHUNK, 2):
            i = c * CHUNK + b
            halves = []
            for j in range(2):
                high = part[i + j].astype(jnp.bfloat16)
                low = (part[i + j] - high.astype(jnp.float32)).astype(jnp.bfloat16)
                halves.append(jnp.concatenate([high, low], axis=0))
            both = apart(halves[0], halves[1], stacked(fold[pl.ds(i, 2)]))
            rows = both.shape[1] // 2
            own_ref[pl.ds(i, 2)] = both[:, :rows] + both[:, rows:]
            for j in range(2):
                mat = jnp.dot(coeffs[i + j, 3], fold[i + j], preferred_element_type=jnp.float32)
                mats[i + j] = mat.astype(jnp.bfloat16)
        store_mats(c).start()

    ready(0)
    fetch(LEAD)
    make(0)

    @pl.loop(1, chunks)
    def _(c):
        ready(c)

        @pl.when(c + LEAD < chunks)
        def _():
            fetch(c + LEAD)

        use(c - 1)
        make(c)

    use(chunks - 1)
    first_ref[...] = mats[pl.ds(0, HELD * CHUNK)]
    for c in range(chunks):
        store_part(c).wait()
        store_mats(c).wait()


def far_kernel(slot, own_ref, far_ref, first_ref, mats_ref, parcel_ref, mats, sems):
    blocks = own_ref.shape[0]
    chunks = blocks // CHUNK

    def load(c):
        own = pl.ds(c * CHUNK, CHUNK)
        return pltpu.make_async_copy(mats_ref.at[own], mats.at[own], sems.at[c])

    for c in range(HELD, chunks):
        load(c).start()

    def send_back(c, pair):
        for b in range(0, CHUNK, 4):
            i = c * CHUNK + b
            mixed = apart4([far_ref[slot[0, i + j]] for j in range(4)], [pair[i + j] for j in range(4)])
            for j in range(4):
                parcel_ref[slot[0, i + j]] = (own_ref[i + j] - mixed[j]).astype(jnp.bfloat16)

    @pl.loop(0, HELD)
    def _(c):
        send_back(c, first_ref)

    @pl.loop(HELD, chunks)
    def _(c):
        load(c).wait()
        send_back(c, mats)


def near_back_kernel(
    groups, ids_ref, slot_ref, far_ref, part_ref, coeffs_ref, prec_ref,
    total, halo_ref, white, scaled, part, coeffs, prec, sems
):
    blocks, _, points = white.shape
    chunks = blocks // CHUNK

    def load(c, which):
        own = pl.ds(c * CHUNK, CHUNK)
        source, target = (
            (part_ref.at[own], part.at[own]),
            (coeffs_ref.at[own, 3], coeffs.at[own, 3]),
            (prec_ref.at[own], prec.at[own]),
            (coeffs_ref.at[own, pl.ds(0, 3)], coeffs.at[own, pl.ds(0, 3)]),
        )[which]
        return pltpu.make_async_copy(source, target, sems.at[which, c])

    def fetch(c):
        for which in range(4):
            load(c, which).start()

    for which in range(3):
        load(0, which).start()
    load(0, 3).start()
    for c in range(1, LEAD):
        fetch(c)
    total[pl.ds(0, REACH)] = jnp.zeros((REACH,) + total.shape[1:], jnp.float32)
    first = lax.axis_index("blk") * blocks

    def mix(c):
        load(c, 0).wait()
        load(c, 1).wait()
        for b in range(0, CHUNK, 4):
            i = c * CHUNK + b
            mixed = apart4([far_ref[slot_ref[0, i + j]] for j in range(4)], [coeffs[i + j, 3] for j in range(4)])
            for j in range(4):
                white[i + j] = (part[i + j] - mixed[j]).astype(jnp.bfloat16)

    def scale(c):
        load(c, 2).wait()
        for b in range(0, CHUNK, 4):
            i = c * CHUNK + b
            tiles = apart4([white[i + j] for j in range(4)], [prec[i + j] for j in range(4)])
            for j in range(4):
                scaled[i + j] = tiles[j].astype(jnp.bfloat16)
                total[REACH + i + j] = scaled[i + j].astype(jnp.float32)

    def back(c):
        load(c, 3).wait()
        terms = []
        for b in range(CHUNK + AHEAD):
            if b < CHUNK and b % 2 == 0:
                i = c * CHUNK + b
                mats = [stacked(coeffs[i + j, pl.ds(0, 3)]) for j in range(2)]
                terms.extend(apart_back(scaled[pl.ds(i, 2)], jnp.concatenate(mats, axis=0)))
            if b >= AHEAD:
                i = c * CHUNK + b - AHEAD
                places = [near_place(ids_ref, k, i, first, groups * blocks) for k in range(3)]
                olds = [total[place] for place in places]
                for k in range(3):
                    total[places[k]] = olds[k] - terms[b - AHEAD][:, k * points : (k + 1) * points]

    mix(0)
    fetch(LEAD)
    scale(0)
    mix(1)
    fetch(LEAD + 1)

    @pl.loop(0, chunks - 2)
    def _(c):
        @pl.when(c + LEAD + 2 < chunks)
        def _():
            fetch(c + LEAD + 2)

        back(c)
        scale(c + 1)
        mix(c + 2)

    back(chunks - 2)
    scale(chunks - 1)
    back(chunks - 1)
    halo_ref[...] = total[pl.ds(0, REACH)].astype(halo_ref.dtype)


def sum_kernel(capacity, picks_ref, base_ref, halo_ref, back_ref, out_ref, total, sem):
    groups = back_ref.shape[0] // capacity
    blocks = out_ref.shape[0]
    last = pl.ds(blocks, REACH)
    total[last] = base_ref[last] + halo_ref[...].astype(jnp.float32)

    @pl.loop(0, groups, unroll=8)
    def _(g):
        picks = [picks_ref[r, g] for r in range(capacity)]
        places = [jnp.where(pick > 0, pick + (REACH - 1), 0) for pick in picks]
        olds = [total[place] for place in places]
        for r in range(capacity):
            total[places[r]] = olds[r] - back_ref[g * capacity + r].astype(jnp.float32)

    store = pltpu.make_async_copy(total.at[pl.ds(REACH, blocks)], out_ref, sem)
    store.start()
    store.wait()


def per_device(probe_vecs, coeffs, cond_prec, neighbours):
    blocks, probes, points = probe_vecs.shape
    groups = lax.axis_size("blk")
    capacity = max(2, blocks // (groups - 1) + 1)
    slots = groups * capacity
    picks_shape = (-(-capacity // 8) * 8, -(-groups // 128) * 128)
    chunks = blocks // CHUNK
    bf16, f32 = jnp.bfloat16, jnp.float32
    tile = (probes, points)
    flops = 2 * blocks * probes * points * points

    def exchange(x):
        return lax.all_to_all(x, "blk", split_axis=0, concat_axis=0, tiled=True)

    ids = neighbours.T
    sent_ids, tail, scalar_ids = pl.pallas_call(
        prep_kernel,
        name="prep",
        out_shape=(
            jax.ShapeDtypeStruct((groups, blocks), jnp.int32),
            jax.ShapeDtypeStruct((REACH,) + tile, bf16),
            pltpu.SMEM(ids.shape, jnp.int32),
        ),
        in_specs=[HBM, HBM],
        out_specs=(VMEM, VMEM, SMEM),
        scratch_shapes=[pltpu.VMEM(ids.shape, jnp.int32), pltpu.SemaphoreType.DMA((3,))],
        compiler_params=params(8),
    )(in_hbm(ids), in_hbm(probe_vecs))
    halo = passed_along(tail, "blk", 1)
    all_ids = exchange(sent_ids)
    all_ids, halo = lax.optimization_barrier((all_ids, halo))
    outgoing, picks = pl.pallas_call(
        functools.partial(pick_kernel, capacity),
        name="pick_tiles",
        out_shape=(
            jax.ShapeDtypeStruct((slots,) + tile, bf16),
            pltpu.SMEM(picks_shape, jnp.int32),
        ),
        in_specs=[VMEM, HBM],
        out_specs=(HBM, SMEM),
        scratch_shapes=[
            pltpu.VMEM((blocks,) + tile, bf16),
            pltpu.VMEM((slots,) + tile, bf16),
            pltpu.VMEM(picks_shape, jnp.int32),
            pltpu.SemaphoreType.DMA((2 + STORES,)),
        ],
        compiler_params=params(8),
        cost_estimate=pl.CostEstimate(flops=0, bytes_accessed=2 * slots * 4096, transcendentals=0),
    )(all_ids, in_hbm(probe_vecs))
    arrived = exchange(outgoing.reshape((groups, capacity) + tile)).reshape((slots,) + tile)
    mats = (blocks, points, points)
    all_mats = pltpu.VMEM((blocks, 4, points, points), bf16)
    tiles_f32 = jax.ShapeDtypeStruct((blocks,) + tile, f32)
    part, own_far, slot_of, first_mats, far_mats = pl.pallas_call(
        functools.partial(near_forward_kernel, groups, capacity),
        name="near_forward",
        out_shape=(
            pltpu.HBM((blocks,) + tile, f32),
            tiles_f32,
            pltpu.SMEM((1, blocks), jnp.int32),
            jax.ShapeDtypeStruct((HELD * CHUNK, points, points), bf16),
            pltpu.HBM(mats, bf16),
        ),
        in_specs=[SMEM, VMEM, VMEM, HBM, HBM, HBM],
        out_specs=(HBM, VMEM, SMEM, VMEM, HBM),
        scratch_shapes=[
            pltpu.VMEM((REACH + blocks,) + tile, bf16),
            all_mats,
            pltpu.VMEM(mats, bf16),
            pltpu.VMEM((blocks,) + tile, f32),
            pltpu.VMEM(mats, bf16),
            pltpu.VMEM(mats, bf16),
            pltpu.VMEM((1, blocks), jnp.int32),
            pltpu.SemaphoreType.DMA((4, chunks)),
        ],
        compiler_params=params(40),
        cost_estimate=pl.CostEstimate(flops=20 * flops, bytes_accessed=28 * 2**20, transcendentals=0),
    )(scalar_ids, ids, halo, in_hbm(probe_vecs), in_hbm(coeffs), in_hbm(cond_prec))
    parcel = pl.pallas_call(
        far_kernel,
        name="far_terms",
        out_shape=jax.ShapeDtypeStruct((slots,) + tile, bf16),
        in_specs=[SMEM, VMEM, VMEM, VMEM, HBM],
        out_specs=VMEM,
        scratch_shapes=[
            pltpu.VMEM(mats, bf16),
            pltpu.SemaphoreType.DMA((chunks,)),
        ],
        compiler_params=params(16),
        cost_estimate=pl.CostEstimate(flops=flops, bytes_accessed=6 * 2**20, transcendentals=0),
    )(slot_of, own_far, arrived, first_mats, in_hbm(far_mats))
    parcel, arrived = lax.optimization_barrier((parcel, arrived))
    returned = exchange(parcel.reshape((groups, capacity) + tile)).reshape((slots,) + tile)
    base, halo_back = pl.pallas_call(
        functools.partial(near_back_kernel, groups),
        name="near_back",
        out_shape=(
            jax.ShapeDtypeStruct((REACH + blocks,) + tile, f32),
            jax.ShapeDtypeStruct((REACH,) + tile, bf16),
        ),
        in_specs=[SMEM, SMEM, VMEM, HBM, HBM, HBM],
        out_specs=(VMEM, VMEM),
        scratch_shapes=[
            pltpu.VMEM((blocks,) + tile, bf16),
            pltpu.VMEM((blocks,) + tile, bf16),
            pltpu.VMEM((blocks,) + tile, f32),
            all_mats,
            pltpu.VMEM(mats, bf16),
            pltpu.SemaphoreType.DMA((4, chunks)),
        ],
        compiler_params=params(36),
        cost_estimate=pl.CostEstimate(flops=5 * flops, bytes_accessed=23 * 2**20, transcendentals=0),
    )(scalar_ids, slot_of, arrived, in_hbm(part), in_hbm(coeffs), in_hbm(cond_prec))
    halo_sum = passed_along(halo_back, "blk", -1)
    result, _ = pl.pallas_call(
        functools.partial(sum_kernel, capacity),
        name="final_sum",
        out_shape=(
            jax.ShapeDtypeStruct((blocks,) + tile, f32),
            jax.ShapeDtypeStruct((REACH + blocks,) + tile, f32),
        ),
        in_specs=[SMEM, VMEM, VMEM, VMEM],
        out_specs=(HBM, VMEM),
        scratch_shapes=[pltpu.SemaphoreType.DMA],
        input_output_aliases={1: 1},
        compiler_params=params(8),
        cost_estimate=pl.CostEstimate(flops=0, bytes_accessed=3 * 2**20, transcendentals=0),
    )(picks, base, halo_sum, returned)
    return result


def solution(mesh):
    in_specs = (
        P("blk", None, None),
        P("blk", None, None, None),
        P("blk", None, None),
        P("blk", None),
    )
    return jax.shard_map(
        per_device, mesh=mesh, in_specs=in_specs, out_specs=P("blk", None, None), check_vma=False
    )
```

```python
import functools

import jax
import jax.numpy as jnp
from jax import lax
from jax.experimental import pallas as pl
from jax.experimental.pallas import tpu as pltpu
from jax.sharding import PartitionSpec as P

REACH = 16
CHUNK = 16
AHEAD = 4
HELD = 3
LEAD = 3
STORES = 4
VMEM = pl.BlockSpec(memory_space=pltpu.VMEM)
SMEM = pl.BlockSpec(memory_space=pltpu.SMEM)
HBM = pl.BlockSpec(memory_space=pl.ANY)
NT = (((1,), (1,)), ((), ()))


def params(mib):
    return pltpu.CompilerParams(vmem_limit_bytes=mib * 2**20)


def in_hbm(x):
    return pltpu.with_memory_space_constraint(x, pltpu.HBM)


def passed_along(block, axis, distance):
    size = lax.axis_size(axis)
    return lax.ppermute(block, axis, [((i - distance) % size, i) for i in range(size)])


def earlier_matrix(blocks):
    row = lax.broadcasted_iota(jnp.int32, (blocks, blocks), 0)
    col = lax.broadcasted_iota(jnp.int32, (blocks, blocks), 1)
    return (row < col).astype(jnp.float32).astype(jnp.bfloat16)


def ranks_in(mask, blocks):
    chosen = mask.astype(jnp.float32).astype(jnp.bfloat16)
    return jnp.dot(chosen, earlier_matrix(blocks), preferred_element_type=jnp.float32).astype(jnp.int32)


def prep_kernel(ids_ref, probe_ref, sent_ref, tail_ref, scalars_ref, ids, sems):
    blocks = probe_ref.shape[0]
    ids_copy = pltpu.make_async_copy(ids_ref, ids, sems.at[0])
    tail_copy = pltpu.make_async_copy(probe_ref.at[pl.ds(blocks - REACH, REACH)], tail_ref, sems.at[1])
    scalars_copy = pltpu.make_async_copy(ids_ref, scalars_ref, sems.at[2])
    ids_copy.start()
    tail_copy.start()
    scalars_copy.start()
    ids_copy.wait()
    sent_ref[...] = jnp.broadcast_to(ids[3:4, :], sent_ref.shape)
    tail_copy.wait()
    scalars_copy.wait()


def pick_kernel(capacity, ids_ref, probe_ref, out_ref, picks_smem, probe, out, picks_ref, sems):
    groups, blocks = ids_ref.shape
    load = pltpu.make_async_copy(probe_ref, probe, sems.at[0])
    load.start()
    me = lax.axis_index("blk")
    local = ids_ref[...] - me * blocks
    mask = (local >= 0) & (local < blocks)
    rank = ranks_in(mask, blocks)
    row = lax.broadcasted_iota(jnp.int32, (picks_ref.shape[0], groups), 0)
    ones = jnp.ones((picks_ref.shape[0], blocks), jnp.bfloat16)
    picks = jnp.zeros(row.shape, jnp.float32)
    for r in range(capacity):
        chosen = jnp.where(mask & (rank == r), local + 1, 0).astype(jnp.float32).astype(jnp.bfloat16)
        found = lax.dot_general(ones, chosen, NT, preferred_element_type=jnp.float32)
        picks = jnp.where(row == r, found, picks)
    picks_ref[:, pl.ds(0, groups)] = picks.astype(jnp.int32)
    copy = pltpu.make_async_copy(picks_ref, picks_smem, sems.at[1])
    copy.start()
    copy.wait()
    load.wait()
    part = groups // STORES

    def store(p):
        rows = pl.ds(p * part * capacity, part * capacity)
        return pltpu.make_async_copy(out.at[rows], out_ref.at[rows], sems.at[2 + p])

    for p in range(STORES):

        @pl.loop(p * part, (p + 1) * part, unroll=8)
        def _(g):
            for r in range(capacity):
                out[g * capacity + r] = probe[jnp.maximum(picks_smem[r, g] - 1, 0)]

        store(p).start()
    for p in range(STORES):
        store(p).wait()


def stacked(mats):
    return mats.reshape(-1, mats.shape[-1])


def apart(left0, left1, mats):
    zero = jnp.zeros_like(left0)
    left = jnp.concatenate(
        [jnp.concatenate([left0, zero], axis=1), jnp.concatenate([zero, left1], axis=1)], axis=0
    )
    out = jnp.dot(left, mats, preferred_element_type=jnp.float32)
    return out.reshape((2,) + (left0.shape[0], mats.shape[1]))


def apart4(lefts, mats):
    zero = jnp.zeros_like(lefts[0])
    rows = zero.shape[0]
    left = jnp.concatenate(
        [jnp.concatenate([x, zero] if j % 2 == 0 else [zero, x], axis=1) for j, x in enumerate(lefts)], axis=0
    )
    right = jnp.concatenate(
        [jnp.concatenate([mats[0], mats[1]], axis=0), jnp.concatenate([mats[2], mats[3]], axis=0)], axis=1
    )
    out = jnp.dot(left, right, preferred_element_type=jnp.float32)
    half = right.shape[1] // 2
    return [out[j * rows : (j + 1) * rows, (j // 2) * half : (j // 2 + 1) * half] for j in range(4)]


def apart_back(lefts, mats):
    rows, half = lefts.shape[1], mats.shape[0] // 2
    out = lax.dot_general(lefts.reshape(2 * rows, lefts.shape[2]), mats, NT, preferred_element_type=jnp.float32)
    return out[:rows, :half], out[rows:, half:]


def near_place(ids_ref, k, i, first, count):
    place = ids_ref[k, i] - first + REACH
    return jnp.where(place >= count, place - count, place)


def near_forward_kernel(
    groups, capacity, ids_ref, ids_row_ref, halo_ref, probe_ref, coeffs_ref, prec_ref,
    part_ref, own_ref, slot_ref, first_ref, mats_ref, ext, coeffs, prec, part, fold, mats, slots, sems
):
    blocks = probe_ref.shape[0]
    chunks = blocks // CHUNK

    def loads(c):
        own = pl.ds(c * CHUNK, CHUNK)
        return (
            pltpu.make_async_copy(coeffs_ref.at[own], coeffs.at[own], sems.at[0, c]),
            pltpu.make_async_copy(prec_ref.at[own], prec.at[own], sems.at[1, c]),
        )

    def store_part(c):
        own = pl.ds(c * CHUNK, CHUNK)
        return pltpu.make_async_copy(part.at[own], part_ref.at[own], sems.at[2, c])

    def store_mats(c):
        own = pl.ds(c * CHUNK, CHUNK)
        return pltpu.make_async_copy(mats.at[own], mats_ref.at[own], sems.at[3, c])

    own_load = pltpu.make_async_copy(probe_ref, ext.at[pl.ds(REACH, blocks)], sems.at[2, 0])
    own_load.start()

    def fetch(c):
        for load in loads(c):
            load.start()

    def ready(c):
        for load in loads(c):
            load.wait()

    for c in range(LEAD):
        fetch(c)
    ext[pl.ds(0, REACH)] = halo_ref[...]
    owner = ids_row_ref[3:4, :] // blocks
    mask = lax.broadcasted_iota(jnp.int32, (groups, blocks), 0) == owner
    rank = jnp.sum(jnp.where(mask, ranks_in(mask, blocks), 0), axis=0, keepdims=True)
    slots[...] = owner * capacity + rank
    slot_copy = pltpu.make_async_copy(slots, slot_ref, sems.at[2, 1])
    slot_copy.start()
    first = lax.axis_index("blk") * blocks
    slot_copy.wait()
    own_load.wait()

    def make(c):
        for b in range(0, CHUNK, 2):
            i = c * CHUNK + b
            rows = []
            for j in range(2):
                tiles = [ext[near_place(ids_ref, k, i + j, first, groups * blocks)] for k in range(3)]
                rows.append(jnp.concatenate(tiles, axis=1))
            near = [stacked(coeffs[i + j, pl.ds(0, 3)]) for j in range(2)]
            mixed = apart(rows[0], rows[1], jnp.concatenate(near, axis=0))
            part[pl.ds(i, 2)] = ext[pl.ds(REACH + i, 2)].astype(jnp.float32) - mixed
            for j in range(2):
                folded = lax.dot_general(prec[i + j], coeffs[i + j, 3], NT, preferred_element_type=jnp.float32)
                fold[i + j] = folded.astype(jnp.bfloat16)
        store_part(c).start()

    def use(c):
        for b in range(0, CHUNK, 2):
            i = c * CHUNK + b
            halves = []
            for j in range(2):
                high = part[i + j].astype(jnp.bfloat16)
                low = (part[i + j] - high.astype(jnp.float32)).astype(jnp.bfloat16)
                halves.append(jnp.concatenate([high, low], axis=0))
            both = apart(halves[0], halves[1], stacked(fold[pl.ds(i, 2)]))
            rows = both.shape[1] // 2
            own_ref[pl.ds(i, 2)] = both[:, :rows] + both[:, rows:]
            for j in range(2):
                mat = jnp.dot(coeffs[i + j, 3], fold[i + j], preferred_element_type=jnp.float32)
                mats[i + j] = mat.astype(jnp.bfloat16)
        store_mats(c).start()

    ready(0)
    fetch(LEAD)
    make(0)

    @pl.loop(1, chunks)
    def _(c):
        ready(c)

        @pl.when(c + LEAD < chunks)
        def _():
            fetch(c + LEAD)

        use(c - 1)
        make(c)

    use(chunks - 1)
    first_ref[...] = mats[pl.ds(0, HELD * CHUNK)]
    for c in range(chunks):
        store_part(c).wait()
        store_mats(c).wait()


def far_kernel(slot, own_ref, far_ref, first_ref, mats_ref, parcel_ref, mats, sems):
    blocks = own_ref.shape[0]
    chunks = blocks // CHUNK

    def load(c):
        own = pl.ds(c * CHUNK, CHUNK)
        return pltpu.make_async_copy(mats_ref.at[own], mats.at[own], sems.at[c])

    for c in range(HELD, chunks):
        load(c).start()

    def send_back(c, pair):
        for b in range(0, CHUNK, 4):
            i = c * CHUNK + b
            mixed = apart4([far_ref[slot[0, i + j]] for j in range(4)], [pair[i + j] for j in range(4)])
            for j in range(4):
                parcel_ref[slot[0, i + j]] = (own_ref[i + j] - mixed[j]).astype(jnp.bfloat16)

    @pl.loop(0, HELD)
    def _(c):
        send_back(c, first_ref)

    @pl.loop(HELD, chunks)
    def _(c):
        load(c).wait()
        send_back(c, mats)


def near_back_kernel(
    groups, ids_ref, slot_ref, far_ref, part_ref, coeffs_ref, prec_ref,
    total, halo_ref, white, scaled, part, coeffs, prec, sems
):
    blocks, _, points = white.shape
    chunks = blocks // CHUNK

    def load(c, which):
        own = pl.ds(c * CHUNK, CHUNK)
        source, target = (
            (part_ref.at[own], part.at[own]),
            (coeffs_ref.at[own, 3], coeffs.at[own, 3]),
            (prec_ref.at[own], prec.at[own]),
            (coeffs_ref.at[own, pl.ds(0, 3)], coeffs.at[own, pl.ds(0, 3)]),
        )[which]
        return pltpu.make_async_copy(source, target, sems.at[which, c])

    def fetch(c):
        for which in range(4):
            load(c, which).start()

    for which in range(3):
        load(0, which).start()
    load(0, 3).start()
    for c in range(1, LEAD):
        fetch(c)
    total[pl.ds(0, REACH)] = jnp.zeros((REACH,) + total.shape[1:], jnp.float32)
    first = lax.axis_index("blk") * blocks

    def mix(c):
        load(c, 0).wait()
        load(c, 1).wait()
        for b in range(0, CHUNK, 4):
            i = c * CHUNK + b
            mixed = apart4([far_ref[slot_ref[0, i + j]] for j in range(4)], [coeffs[i + j, 3] for j in range(4)])
            for j in range(4):
                white[i + j] = (part[i + j] - mixed[j]).astype(jnp.bfloat16)

    def scale(c):
        load(c, 2).wait()
        for b in range(0, CHUNK, 4):
            i = c * CHUNK + b
            tiles = apart4([white[i + j] for j in range(4)], [prec[i + j] for j in range(4)])
            for j in range(4):
                scaled[i + j] = tiles[j].astype(jnp.bfloat16)
                total[REACH + i + j] = scaled[i + j].astype(jnp.float32)

    def back(c):
        load(c, 3).wait()
        terms = []
        for b in range(CHUNK + AHEAD):
            if b < CHUNK and b % 2 == 0:
                i = c * CHUNK + b
                mats = [stacked(coeffs[i + j, pl.ds(0, 3)]) for j in range(2)]
                terms.extend(apart_back(scaled[pl.ds(i, 2)], jnp.concatenate(mats, axis=0)))
            if b >= AHEAD:
                i = c * CHUNK + b - AHEAD
                places = [near_place(ids_ref, k, i, first, groups * blocks) for k in range(3)]
                olds = [total[place] for place in places]
                for k in range(3):
                    total[places[k]] = olds[k] - terms[b - AHEAD][:, k * points : (k + 1) * points]

    mix(0)
    fetch(LEAD)
    scale(0)
    mix(1)
    fetch(LEAD + 1)

    @pl.loop(0, chunks - 2)
    def _(c):
        @pl.when(c + LEAD + 2 < chunks)
        def _():
            fetch(c + LEAD + 2)

        back(c)
        scale(c + 1)
        mix(c + 2)

    back(chunks - 2)
    scale(chunks - 1)
    back(chunks - 1)
    halo_ref[...] = total[pl.ds(0, REACH)].astype(halo_ref.dtype)


def sum_kernel(capacity, picks_ref, base_ref, halo_ref, back_ref, out_ref, total, sem):
    groups = back_ref.shape[0] // capacity
    blocks = out_ref.shape[0]
    last = pl.ds(blocks, REACH)
    total[last] = base_ref[last] + halo_ref[...].astype(jnp.float32)

    @pl.loop(0, groups, unroll=8)
    def _(g):
        picks = [picks_ref[r, g] for r in range(capacity)]
        places = [jnp.where(pick > 0, pick + (REACH - 1), 0) for pick in picks]
        olds = [total[place] for place in places]
        for r in range(capacity):
            total[places[r]] = olds[r] - back_ref[g * capacity + r].astype(jnp.float32)

    store = pltpu.make_async_copy(total.at[pl.ds(REACH, blocks)], out_ref, sem)
    store.start()
    store.wait()


def per_device(probe_vecs, coeffs, cond_prec, neighbours):
    blocks, probes, points = probe_vecs.shape
    groups = lax.axis_size("blk")
    capacity = max(2, blocks // (groups - 1) + 1)
    slots = groups * capacity
    picks_shape = (-(-capacity // 8) * 8, -(-groups // 128) * 128)
    chunks = blocks // CHUNK
    bf16, f32 = jnp.bfloat16, jnp.float32
    tile = (probes, points)
    flops = 2 * blocks * probes * points * points

    def exchange(x):
        return lax.all_to_all(x, "blk", split_axis=0, concat_axis=0, tiled=True)

    ids = neighbours.T
    sent_ids, tail, scalar_ids = pl.pallas_call(
        prep_kernel,
        name="prep",
        out_shape=(
            jax.ShapeDtypeStruct((groups, blocks), jnp.int32),
            jax.ShapeDtypeStruct((REACH,) + tile, bf16),
            pltpu.SMEM(ids.shape, jnp.int32),
        ),
        in_specs=[HBM, HBM],
        out_specs=(VMEM, VMEM, SMEM),
        scratch_shapes=[pltpu.VMEM(ids.shape, jnp.int32), pltpu.SemaphoreType.DMA((3,))],
        compiler_params=params(8),
    )(in_hbm(ids), in_hbm(probe_vecs))
    halo = passed_along(tail, "blk", 1)
    all_ids = exchange(sent_ids)
    all_ids, halo = lax.optimization_barrier((all_ids, halo))
    outgoing, picks = pl.pallas_call(
        functools.partial(pick_kernel, capacity),
        name="pick_tiles",
        out_shape=(
            jax.ShapeDtypeStruct((slots,) + tile, bf16),
            pltpu.SMEM(picks_shape, jnp.int32),
        ),
        in_specs=[VMEM, HBM],
        out_specs=(HBM, SMEM),
        scratch_shapes=[
            pltpu.VMEM((blocks,) + tile, bf16),
            pltpu.VMEM((slots,) + tile, bf16),
            pltpu.VMEM(picks_shape, jnp.int32),
            pltpu.SemaphoreType.DMA((2 + STORES,)),
        ],
        compiler_params=params(8),
        cost_estimate=pl.CostEstimate(flops=0, bytes_accessed=2 * slots * 4096, transcendentals=0),
    )(all_ids, in_hbm(probe_vecs))
    arrived = exchange(outgoing.reshape(groups, capacity * probes, points)).reshape((slots,) + tile)
    mats = (blocks, points, points)
    all_mats = pltpu.VMEM((blocks, 4, points, points), bf16)
    tiles_f32 = jax.ShapeDtypeStruct((blocks,) + tile, f32)
    part, own_far, slot_of, first_mats, far_mats = pl.pallas_call(
        functools.partial(near_forward_kernel, groups, capacity),
        name="near_forward",
        out_shape=(
            pltpu.HBM((blocks,) + tile, f32),
            tiles_f32,
            pltpu.SMEM((1, blocks), jnp.int32),
            jax.ShapeDtypeStruct((HELD * CHUNK, points, points), bf16),
            pltpu.HBM(mats, bf16),
        ),
        in_specs=[SMEM, VMEM, VMEM, HBM, HBM, HBM],
        out_specs=(HBM, VMEM, SMEM, VMEM, HBM),
        scratch_shapes=[
            pltpu.VMEM((REACH + blocks,) + tile, bf16),
            all_mats,
            pltpu.VMEM(mats, bf16),
            pltpu.VMEM((blocks,) + tile, f32),
            pltpu.VMEM(mats, bf16),
            pltpu.VMEM(mats, bf16),
            pltpu.VMEM((1, blocks), jnp.int32),
            pltpu.SemaphoreType.DMA((4, chunks)),
        ],
        compiler_params=params(40),
        cost_estimate=pl.CostEstimate(flops=20 * flops, bytes_accessed=28 * 2**20, transcendentals=0),
    )(scalar_ids, ids, halo, in_hbm(probe_vecs), in_hbm(coeffs), in_hbm(cond_prec))
    parcel = pl.pallas_call(
        far_kernel,
        name="far_terms",
        out_shape=jax.ShapeDtypeStruct((slots,) + tile, bf16),
        in_specs=[SMEM, VMEM, VMEM, VMEM, HBM],
        out_specs=VMEM,
        scratch_shapes=[
            pltpu.VMEM(mats, bf16),
            pltpu.SemaphoreType.DMA((chunks,)),
        ],
        compiler_params=params(16),
        cost_estimate=pl.CostEstimate(flops=flops, bytes_accessed=6 * 2**20, transcendentals=0),
    )(slot_of, own_far, arrived, first_mats, in_hbm(far_mats))
    parcel, arrived = lax.optimization_barrier((parcel, arrived))
    returned = exchange(parcel.reshape(groups, capacity * probes, points)).reshape((slots,) + tile)
    base, halo_back = pl.pallas_call(
        functools.partial(near_back_kernel, groups),
        name="near_back",
        out_shape=(
            jax.ShapeDtypeStruct((REACH + blocks,) + tile, f32),
            jax.ShapeDtypeStruct((REACH,) + tile, bf16),
        ),
        in_specs=[SMEM, SMEM, VMEM, HBM, HBM, HBM],
        out_specs=(VMEM, VMEM),
        scratch_shapes=[
            pltpu.VMEM((blocks,) + tile, bf16),
            pltpu.VMEM((blocks,) + tile, bf16),
            pltpu.VMEM((blocks,) + tile, f32),
            all_mats,
            pltpu.VMEM(mats, bf16),
            pltpu.SemaphoreType.DMA((4, chunks)),
        ],
        compiler_params=params(36),
        cost_estimate=pl.CostEstimate(flops=5 * flops, bytes_accessed=23 * 2**20, transcendentals=0),
    )(scalar_ids, slot_of, arrived, in_hbm(part), in_hbm(coeffs), in_hbm(cond_prec))
    halo_sum = passed_along(halo_back, "blk", -1)
    result, _ = pl.pallas_call(
        functools.partial(sum_kernel, capacity),
        name="final_sum",
        out_shape=(
            jax.ShapeDtypeStruct((blocks,) + tile, f32),
            jax.ShapeDtypeStruct((REACH + blocks,) + tile, f32),
        ),
        in_specs=[SMEM, VMEM, VMEM, VMEM],
        out_specs=(HBM, VMEM),
        scratch_shapes=[pltpu.SemaphoreType.DMA],
        input_output_aliases={1: 1},
        compiler_params=params(8),
        cost_estimate=pl.CostEstimate(flops=0, bytes_accessed=3 * 2**20, transcendentals=0),
    )(picks, base, halo_sum, returned)
    return result


def solution(mesh):
    in_specs = (
        P("blk", None, None),
        P("blk", None, None, None),
        P("blk", None, None),
        P("blk", None),
    )
    return jax.shard_map(
        per_device, mesh=mesh, in_specs=in_specs, out_specs=P("blk", None, None), check_vma=False
    )
```

```python
import functools

import jax
import jax.numpy as jnp
from jax import lax
from jax.experimental import pallas as pl
from jax.experimental.pallas import tpu as pltpu
from jax.sharding import PartitionSpec as P

REACH = 16
CHUNK = 16
AHEAD = 4
HELD = 3
LEAD = 3
STORES = 4
VMEM = pl.BlockSpec(memory_space=pltpu.VMEM)
SMEM = pl.BlockSpec(memory_space=pltpu.SMEM)
HBM = pl.BlockSpec(memory_space=pl.ANY)
NT = (((1,), (1,)), ((), ()))


def params(mib):
    return pltpu.CompilerParams(vmem_limit_bytes=mib * 2**20)


def in_hbm(x):
    return pltpu.with_memory_space_constraint(x, pltpu.HBM)


def passed_along(block, axis, distance):
    size = lax.axis_size(axis)
    return lax.ppermute(block, axis, [((i - distance) % size, i) for i in range(size)])


def earlier_matrix(blocks):
    row = lax.broadcasted_iota(jnp.int32, (blocks, blocks), 0)
    col = lax.broadcasted_iota(jnp.int32, (blocks, blocks), 1)
    return (row < col).astype(jnp.float32).astype(jnp.bfloat16)


def ranks_in(mask, blocks):
    chosen = mask.astype(jnp.float32).astype(jnp.bfloat16)
    return jnp.dot(chosen, earlier_matrix(blocks), preferred_element_type=jnp.float32).astype(jnp.int32)


def prep_kernel(ids_ref, probe_ref, sent_ref, tail_ref, scalars_ref, ids, sems):
    blocks = probe_ref.shape[0]
    ids_copy = pltpu.make_async_copy(ids_ref, ids, sems.at[0])
    tail_copy = pltpu.make_async_copy(probe_ref.at[pl.ds(blocks - REACH, REACH)], tail_ref, sems.at[1])
    scalars_copy = pltpu.make_async_copy(ids_ref, scalars_ref, sems.at[2])
    ids_copy.start()
    tail_copy.start()
    scalars_copy.start()
    ids_copy.wait()
    sent_ref[...] = jnp.broadcast_to(ids[3:4, :], sent_ref.shape)
    tail_copy.wait()
    scalars_copy.wait()


def pick_kernel(capacity, ids_ref, probe_ref, out_ref, picks_smem, probe, out, picks_ref, sems):
    groups, blocks = ids_ref.shape
    load = pltpu.make_async_copy(probe_ref, probe, sems.at[0])
    load.start()
    me = lax.axis_index("blk")
    local = ids_ref[...] - me * blocks
    mask = (local >= 0) & (local < blocks)
    rank = ranks_in(mask, blocks)
    chosen = [jnp.where(mask & (rank == r), local + 1, 0).astype(jnp.float32) for r in range(capacity)]
    chosen = jnp.concatenate(chosen, axis=0).astype(jnp.bfloat16)
    ones = jnp.ones((8, blocks), jnp.bfloat16)
    found = lax.dot_general(ones, chosen, NT, preferred_element_type=jnp.float32)
    picks_ref[:, pl.ds(0, groups * capacity)] = found[:1].astype(jnp.int32)
    copy = pltpu.make_async_copy(picks_ref, picks_smem, sems.at[1])
    copy.start()
    copy.wait()
    load.wait()
    part = groups // STORES

    def store(p):
        rows = pl.ds(p * part * capacity, part * capacity)
        return pltpu.make_async_copy(out.at[rows], out_ref.at[rows], sems.at[2 + p])

    for p in range(STORES):

        @pl.loop(p * part, (p + 1) * part, unroll=8)
        def _(g):
            for r in range(capacity):
                out[g * capacity + r] = probe[jnp.maximum(picks_smem[0, r * groups + g] - 1, 0)]

        store(p).start()
    for p in range(STORES):
        store(p).wait()


def stacked(mats):
    return mats.reshape(-1, mats.shape[-1])


def apart(left0, left1, mats):
    zero = jnp.zeros_like(left0)
    left = jnp.concatenate(
        [jnp.concatenate([left0, zero], axis=1), jnp.concatenate([zero, left1], axis=1)], axis=0
    )
    out = jnp.dot(left, mats, preferred_element_type=jnp.float32)
    return out.reshape((2,) + (left0.shape[0], mats.shape[1]))


def apart4(lefts, mats):
    zero = jnp.zeros_like(lefts[0])
    rows = zero.shape[0]
    left = jnp.concatenate(
        [jnp.concatenate([x, zero] if j % 2 == 0 else [zero, x], axis=1) for j, x in enumerate(lefts)], axis=0
    )
    right = jnp.concatenate(
        [jnp.concatenate([mats[0], mats[1]], axis=0), jnp.concatenate([mats[2], mats[3]], axis=0)], axis=1
    )
    out = jnp.dot(left, right, preferred_element_type=jnp.float32)
    half = right.shape[1] // 2
    return [out[j * rows : (j + 1) * rows, (j // 2) * half : (j // 2 + 1) * half] for j in range(4)]


def apart_back(lefts, mats):
    rows, half = lefts.shape[1], mats.shape[0] // 2
    out = lax.dot_general(lefts.reshape(2 * rows, lefts.shape[2]), mats, NT, preferred_element_type=jnp.float32)
    return out[:rows, :half], out[rows:, half:]


def near_place(ids_ref, k, i, first, count):
    place = ids_ref[k, i] - first + REACH
    return jnp.where(place >= count, place - count, place)


def near_forward_kernel(
    groups, capacity, ids_ref, ids_row_ref, halo_ref, probe_ref, coeffs_ref, prec_ref,
    part_ref, own_ref, slot_ref, first_ref, mats_ref, ext, coeffs, prec, part, fold, mats, slots, sems
):
    blocks = probe_ref.shape[0]
    chunks = blocks // CHUNK

    def loads(c):
        own = pl.ds(c * CHUNK, CHUNK)
        return (
            pltpu.make_async_copy(coeffs_ref.at[own], coeffs.at[own], sems.at[0, c]),
            pltpu.make_async_copy(prec_ref.at[own], prec.at[own], sems.at[1, c]),
        )

    def store_part(c):
        own = pl.ds(c * CHUNK, CHUNK)
        return pltpu.make_async_copy(part.at[own], part_ref.at[own], sems.at[2, c])

    def store_mats(c):
        own = pl.ds(c * CHUNK, CHUNK)
        return pltpu.make_async_copy(mats.at[own], mats_ref.at[own], sems.at[3, c])

    own_load = pltpu.make_async_copy(probe_ref, ext.at[pl.ds(REACH, blocks)], sems.at[2, 0])
    own_load.start()

    def fetch(c):
        for load in loads(c):
            load.start()

    def ready(c):
        for load in loads(c):
            load.wait()

    for c in range(LEAD):
        fetch(c)
    ext[pl.ds(0, REACH)] = halo_ref[...]
    owner = ids_row_ref[3:4, :] // blocks
    mask = lax.broadcasted_iota(jnp.int32, (groups, blocks), 0) == owner
    rank = jnp.sum(jnp.where(mask, ranks_in(mask, blocks), 0), axis=0, keepdims=True)
    slots[...] = owner * capacity + rank
    slot_copy = pltpu.make_async_copy(slots, slot_ref, sems.at[2, 1])
    slot_copy.start()
    first = lax.axis_index("blk") * blocks
    slot_copy.wait()
    own_load.wait()

    def make(c):
        for b in range(0, CHUNK, 2):
            i = c * CHUNK + b
            rows = []
            for j in range(2):
                tiles = [ext[near_place(ids_ref, k, i + j, first, groups * blocks)] for k in range(3)]
                rows.append(jnp.concatenate(tiles, axis=1))
            near = [stacked(coeffs[i + j, pl.ds(0, 3)]) for j in range(2)]
            mixed = apart(rows[0], rows[1], jnp.concatenate(near, axis=0))
            part[pl.ds(i, 2)] = ext[pl.ds(REACH + i, 2)].astype(jnp.float32) - mixed
            for j in range(2):
                folded = lax.dot_general(prec[i + j], coeffs[i + j, 3], NT, preferred_element_type=jnp.float32)
                fold[i + j] = folded.astype(jnp.bfloat16)
        store_part(c).start()

    def use(c):
        for b in range(0, CHUNK, 2):
            i = c * CHUNK + b
            halves = []
            for j in range(2):
                high = part[i + j].astype(jnp.bfloat16)
                low = (part[i + j] - high.astype(jnp.float32)).astype(jnp.bfloat16)
                halves.append(jnp.concatenate([high, low], axis=0))
            both = apart(halves[0], halves[1], stacked(fold[pl.ds(i, 2)]))
            rows = both.shape[1] // 2
            own_ref[pl.ds(i, 2)] = both[:, :rows] + both[:, rows:]
            for j in range(2):
                mat = jnp.dot(coeffs[i + j, 3], fold[i + j], preferred_element_type=jnp.float32)
                mats[i + j] = mat.astype(jnp.bfloat16)
        store_mats(c).start()

    ready(0)
    fetch(LEAD)
    make(0)

    @pl.loop(1, chunks)
    def _(c):
        ready(c)

        @pl.when(c + LEAD < chunks)
        def _():
            fetch(c + LEAD)

        use(c - 1)
        make(c)

    use(chunks - 1)
    first_ref[...] = mats[pl.ds(0, HELD * CHUNK)]
    for c in range(chunks):
        store_part(c).wait()
        store_mats(c).wait()


def far_kernel(slot, own_ref, far_ref, first_ref, mats_ref, parcel_ref, mats, sems):
    blocks = own_ref.shape[0]
    chunks = blocks // CHUNK

    def load(c):
        own = pl.ds(c * CHUNK, CHUNK)
        return pltpu.make_async_copy(mats_ref.at[own], mats.at[own], sems.at[c])

    for c in range(HELD, chunks):
        load(c).start()

    def send_back(c, pair):
        for b in range(0, CHUNK, 4):
            i = c * CHUNK + b
            mixed = apart4([far_ref[slot[0, i + j]] for j in range(4)], [pair[i + j] for j in range(4)])
            for j in range(4):
                parcel_ref[slot[0, i + j]] = (own_ref[i + j] - mixed[j]).astype(jnp.bfloat16)

    @pl.loop(0, HELD)
    def _(c):
        send_back(c, first_ref)

    @pl.loop(HELD, chunks)
    def _(c):
        load(c).wait()
        send_back(c, mats)


def near_back_kernel(
    groups, ids_ref, slot_ref, far_ref, part_ref, coeffs_ref, prec_ref,
    total, halo_ref, white, scaled, part, coeffs, prec, sems
):
    blocks, _, points = white.shape
    chunks = blocks // CHUNK

    def load(c, which):
        own = pl.ds(c * CHUNK, CHUNK)
        source, target = (
            (part_ref.at[own], part.at[own]),
            (coeffs_ref.at[own, 3], coeffs.at[own, 3]),
            (prec_ref.at[own], prec.at[own]),
            (coeffs_ref.at[own, pl.ds(0, 3)], coeffs.at[own, pl.ds(0, 3)]),
        )[which]
        return pltpu.make_async_copy(source, target, sems.at[which, c])

    def fetch(c):
        for which in range(4):
            load(c, which).start()

    for which in range(3):
        load(0, which).start()
    load(0, 3).start()
    for c in range(1, LEAD):
        fetch(c)
    total[pl.ds(0, REACH)] = jnp.zeros((REACH,) + total.shape[1:], jnp.float32)
    first = lax.axis_index("blk") * blocks

    def mix(c):
        load(c, 0).wait()
        load(c, 1).wait()
        for b in range(0, CHUNK, 4):
            i = c * CHUNK + b
            mixed = apart4([far_ref[slot_ref[0, i + j]] for j in range(4)], [coeffs[i + j, 3] for j in range(4)])
            for j in range(4):
                white[i + j] = (part[i + j] - mixed[j]).astype(jnp.bfloat16)

    def scale(c):
        load(c, 2).wait()
        for b in range(0, CHUNK, 4):
            i = c * CHUNK + b
            tiles = apart4([white[i + j] for j in range(4)], [prec[i + j] for j in range(4)])
            for j in range(4):
                scaled[i + j] = tiles[j].astype(jnp.bfloat16)
                total[REACH + i + j] = scaled[i + j].astype(jnp.float32)

    def back(c):
        load(c, 3).wait()
        terms = []
        for b in range(CHUNK + AHEAD):
            if b < CHUNK and b % 2 == 0:
                i = c * CHUNK + b
                mats = [stacked(coeffs[i + j, pl.ds(0, 3)]) for j in range(2)]
                terms.extend(apart_back(scaled[pl.ds(i, 2)], jnp.concatenate(mats, axis=0)))
            if b >= AHEAD:
                i = c * CHUNK + b - AHEAD
                places = [near_place(ids_ref, k, i, first, groups * blocks) for k in range(3)]
                olds = [total[place] for place in places]
                for k in range(3):
                    total[places[k]] = olds[k] - terms[b - AHEAD][:, k * points : (k + 1) * points]

    mix(0)
    fetch(LEAD)
    scale(0)
    mix(1)
    fetch(LEAD + 1)

    @pl.loop(0, chunks - 2)
    def _(c):
        @pl.when(c + LEAD + 2 < chunks)
        def _():
            fetch(c + LEAD + 2)

        back(c)
        scale(c + 1)
        mix(c + 2)

    back(chunks - 2)
    scale(chunks - 1)
    back(chunks - 1)
    halo_ref[...] = total[pl.ds(0, REACH)].astype(halo_ref.dtype)


def sum_kernel(capacity, picks_ref, base_ref, halo_ref, back_ref, out_ref, total, sem):
    groups = back_ref.shape[0] // capacity
    blocks = out_ref.shape[0]
    last = pl.ds(blocks, REACH)
    total[last] = base_ref[last] + halo_ref[...].astype(jnp.float32)

    @pl.loop(0, groups, unroll=8)
    def _(g):
        picks = [picks_ref[0, r * groups + g] for r in range(capacity)]
        places = [jnp.where(pick > 0, pick + (REACH - 1), 0) for pick in picks]
        olds = [total[place] for place in places]
        for r in range(capacity):
            total[places[r]] = olds[r] - back_ref[g * capacity + r].astype(jnp.float32)

    store = pltpu.make_async_copy(total.at[pl.ds(REACH, blocks)], out_ref, sem)
    store.start()
    store.wait()


def per_device(probe_vecs, coeffs, cond_prec, neighbours):
    blocks, probes, points = probe_vecs.shape
    groups = lax.axis_size("blk")
    capacity = max(2, blocks // (groups - 1) + 1)
    slots = groups * capacity
    picks_shape = (1, -(-slots // 128) * 128)
    chunks = blocks // CHUNK
    bf16, f32 = jnp.bfloat16, jnp.float32
    tile = (probes, points)
    flops = 2 * blocks * probes * points * points

    def exchange(x):
        return lax.all_to_all(x, "blk", split_axis=0, concat_axis=0, tiled=True)

    ids = neighbours.T
    sent_ids, tail, scalar_ids = pl.pallas_call(
        prep_kernel,
        name="prep",
        out_shape=(
            jax.ShapeDtypeStruct((groups, blocks), jnp.int32),
            jax.ShapeDtypeStruct((REACH,) + tile, bf16),
            pltpu.SMEM(ids.shape, jnp.int32),
        ),
        in_specs=[HBM, HBM],
        out_specs=(VMEM, VMEM, SMEM),
        scratch_shapes=[pltpu.VMEM(ids.shape, jnp.int32), pltpu.SemaphoreType.DMA((3,))],
        compiler_params=params(8),
    )(in_hbm(ids), in_hbm(probe_vecs))
    halo = passed_along(tail, "blk", 1)
    all_ids = exchange(sent_ids)
    all_ids, halo = lax.optimization_barrier((all_ids, halo))
    outgoing, picks = pl.pallas_call(
        functools.partial(pick_kernel, capacity),
        name="pick_tiles",
        out_shape=(
            jax.ShapeDtypeStruct((slots,) + tile, bf16),
            pltpu.SMEM(picks_shape, jnp.int32),
        ),
        in_specs=[VMEM, HBM],
        out_specs=(HBM, SMEM),
        scratch_shapes=[
            pltpu.VMEM((blocks,) + tile, bf16),
            pltpu.VMEM((slots,) + tile, bf16),
            pltpu.VMEM(picks_shape, jnp.int32),
            pltpu.SemaphoreType.DMA((2 + STORES,)),
        ],
        compiler_params=params(8),
        cost_estimate=pl.CostEstimate(flops=0, bytes_accessed=2 * slots * 4096, transcendentals=0),
    )(all_ids, in_hbm(probe_vecs))
    arrived = exchange(outgoing.reshape(groups, capacity * probes, points)).reshape((slots,) + tile)
    mats = (blocks, points, points)
    all_mats = pltpu.VMEM((blocks, 4, points, points), bf16)
    tiles_f32 = jax.ShapeDtypeStruct((blocks,) + tile, f32)
    part, own_far, slot_of, first_mats, far_mats = pl.pallas_call(
        functools.partial(near_forward_kernel, groups, capacity),
        name="near_forward",
        out_shape=(
            pltpu.HBM((blocks,) + tile, f32),
            tiles_f32,
            pltpu.SMEM((1, blocks), jnp.int32),
            jax.ShapeDtypeStruct((HELD * CHUNK, points, points), bf16),
            pltpu.HBM(mats, bf16),
        ),
        in_specs=[SMEM, VMEM, VMEM, HBM, HBM, HBM],
        out_specs=(HBM, VMEM, SMEM, VMEM, HBM),
        scratch_shapes=[
            pltpu.VMEM((REACH + blocks,) + tile, bf16),
            all_mats,
            pltpu.VMEM(mats, bf16),
            pltpu.VMEM((blocks,) + tile, f32),
            pltpu.VMEM(mats, bf16),
            pltpu.VMEM(mats, bf16),
            pltpu.VMEM((1, blocks), jnp.int32),
            pltpu.SemaphoreType.DMA((4, chunks)),
        ],
        compiler_params=params(40),
        cost_estimate=pl.CostEstimate(flops=20 * flops, bytes_accessed=28 * 2**20, transcendentals=0),
    )(scalar_ids, ids, halo, in_hbm(probe_vecs), in_hbm(coeffs), in_hbm(cond_prec))
    parcel = pl.pallas_call(
        far_kernel,
        name="far_terms",
        out_shape=jax.ShapeDtypeStruct((slots,) + tile, bf16),
        in_specs=[SMEM, VMEM, VMEM, VMEM, HBM],
        out_specs=VMEM,
        scratch_shapes=[
            pltpu.VMEM(mats, bf16),
            pltpu.SemaphoreType.DMA((chunks,)),
        ],
        compiler_params=params(16),
        cost_estimate=pl.CostEstimate(flops=flops, bytes_accessed=6 * 2**20, transcendentals=0),
    )(slot_of, own_far, arrived, first_mats, in_hbm(far_mats))
    parcel, arrived = lax.optimization_barrier((parcel, arrived))
    returned = exchange(parcel.reshape(groups, capacity * probes, points)).reshape((slots,) + tile)
    base, halo_back = pl.pallas_call(
        functools.partial(near_back_kernel, groups),
        name="near_back",
        out_shape=(
            jax.ShapeDtypeStruct((REACH + blocks,) + tile, f32),
            jax.ShapeDtypeStruct((REACH,) + tile, bf16),
        ),
        in_specs=[SMEM, SMEM, VMEM, HBM, HBM, HBM],
        out_specs=(VMEM, VMEM),
        scratch_shapes=[
            pltpu.VMEM((blocks,) + tile, bf16),
            pltpu.VMEM((blocks,) + tile, bf16),
            pltpu.VMEM((blocks,) + tile, f32),
            all_mats,
            pltpu.VMEM(mats, bf16),
            pltpu.SemaphoreType.DMA((4, chunks)),
        ],
        compiler_params=params(36),
        cost_estimate=pl.CostEstimate(flops=5 * flops, bytes_accessed=23 * 2**20, transcendentals=0),
    )(scalar_ids, slot_of, arrived, in_hbm(part), in_hbm(coeffs), in_hbm(cond_prec))
    halo_sum = passed_along(halo_back, "blk", -1)
    result, _ = pl.pallas_call(
        functools.partial(sum_kernel, capacity),
        name="final_sum",
        out_shape=(
            jax.ShapeDtypeStruct((blocks,) + tile, f32),
            jax.ShapeDtypeStruct((REACH + blocks,) + tile, f32),
        ),
        in_specs=[SMEM, VMEM, VMEM, VMEM],
        out_specs=(HBM, VMEM),
        scratch_shapes=[pltpu.SemaphoreType.DMA],
        input_output_aliases={1: 1},
        compiler_params=params(8),
        cost_estimate=pl.CostEstimate(flops=0, bytes_accessed=3 * 2**20, transcendentals=0),
    )(picks, base, halo_sum, returned)
    return result


def solution(mesh):
    in_specs = (
        P("blk", None, None),
        P("blk", None, None, None),
        P("blk", None, None),
        P("blk", None),
    )
    return jax.shard_map(
        per_device, mesh=mesh, in_specs=in_specs, out_specs=P("blk", None, None), check_vma=False
    )
```

```python
import functools

import jax
import jax.numpy as jnp
from jax import lax
from jax.experimental import pallas as pl
from jax.experimental.pallas import tpu as pltpu
from jax.sharding import PartitionSpec as P

REACH = 16
CHUNK = 16
AHEAD = 4
HELD = 3
LEAD = 3
STORES = 2
VMEM = pl.BlockSpec(memory_space=pltpu.VMEM)
SMEM = pl.BlockSpec(memory_space=pltpu.SMEM)
HBM = pl.BlockSpec(memory_space=pl.ANY)
NT = (((1,), (1,)), ((), ()))


def params(mib):
    return pltpu.CompilerParams(vmem_limit_bytes=mib * 2**20)


def in_hbm(x):
    return pltpu.with_memory_space_constraint(x, pltpu.HBM)


def passed_along(block, axis, distance):
    size = lax.axis_size(axis)
    return lax.ppermute(block, axis, [((i - distance) % size, i) for i in range(size)])


def earlier_matrix(blocks):
    row = lax.broadcasted_iota(jnp.int32, (blocks, blocks), 0)
    col = lax.broadcasted_iota(jnp.int32, (blocks, blocks), 1)
    return (row < col).astype(jnp.float32).astype(jnp.bfloat16)


def ranks_in(mask, blocks):
    chosen = mask.astype(jnp.float32).astype(jnp.bfloat16)
    return jnp.dot(chosen, earlier_matrix(blocks), preferred_element_type=jnp.float32).astype(jnp.int32)


def prep_kernel(ids_ref, probe_ref, sent_ref, tail_ref, scalars_ref, ids, sems):
    blocks = probe_ref.shape[0]
    ids_copy = pltpu.make_async_copy(ids_ref, ids, sems.at[0])
    tail_copy = pltpu.make_async_copy(probe_ref.at[pl.ds(blocks - REACH, REACH)], tail_ref, sems.at[1])
    scalars_copy = pltpu.make_async_copy(ids_ref, scalars_ref, sems.at[2])
    ids_copy.start()
    tail_copy.start()
    scalars_copy.start()
    ids_copy.wait()
    sent_ref[...] = jnp.broadcast_to(ids[3:4, :], sent_ref.shape)
    tail_copy.wait()
    scalars_copy.wait()


def pick_kernel(capacity, ids_ref, probe_ref, out_ref, picks_smem, probe, out, picks_ref, sems):
    groups, blocks = ids_ref.shape
    load = pltpu.make_async_copy(probe_ref, probe, sems.at[0])
    load.start()
    me = lax.axis_index("blk")
    local = ids_ref[...] - me * blocks
    mask = (local >= 0) & (local < blocks)
    rank = ranks_in(mask, blocks)
    row = lax.broadcasted_iota(jnp.int32, (picks_ref.shape[0], groups), 0)
    ones = jnp.ones((picks_ref.shape[0], blocks), jnp.bfloat16)
    picks = jnp.zeros(row.shape, jnp.float32)
    for r in range(capacity):
        chosen = jnp.where(mask & (rank == r), local + 1, 0).astype(jnp.float32).astype(jnp.bfloat16)
        found = lax.dot_general(ones, chosen, NT, preferred_element_type=jnp.float32)
        picks = jnp.where(row == r, found, picks)
    picks_ref[:, pl.ds(0, groups)] = picks.astype(jnp.int32)
    copy = pltpu.make_async_copy(picks_ref, picks_smem, sems.at[1])
    copy.start()
    copy.wait()
    load.wait()
    part = groups // STORES

    def store(p):
        rows = pl.ds(p * part * capacity, part * capacity)
        return pltpu.make_async_copy(out.at[rows], out_ref.at[rows], sems.at[2 + p])

    for p in range(STORES):

        @pl.loop(p * part, (p + 1) * part, unroll=8)
        def _(g):
            for r in range(capacity):
                out[g * capacity + r] = probe[jnp.maximum(picks_smem[r, g] - 1, 0)]

        store(p).start()
    for p in range(STORES):
        store(p).wait()


def stacked(mats):
    return mats.reshape(-1, mats.shape[-1])


def apart(left0, left1, mats):
    zero = jnp.zeros_like(left0)
    left = jnp.concatenate(
        [jnp.concatenate([left0, zero], axis=1), jnp.concatenate([zero, left1], axis=1)], axis=0
    )
    out = jnp.dot(left, mats, preferred_element_type=jnp.float32)
    return out.reshape((2,) + (left0.shape[0], mats.shape[1]))


def apart4(lefts, mats):
    zero = jnp.zeros_like(lefts[0])
    rows = zero.shape[0]
    left = jnp.concatenate(
        [jnp.concatenate([x, zero] if j % 2 == 0 else [zero, x], axis=1) for j, x in enumerate(lefts)], axis=0
    )
    right = jnp.concatenate(
        [jnp.concatenate([mats[0], mats[1]], axis=0), jnp.concatenate([mats[2], mats[3]], axis=0)], axis=1
    )
    out = jnp.dot(left, right, preferred_element_type=jnp.float32)
    half = right.shape[1] // 2
    return [out[j * rows : (j + 1) * rows, (j // 2) * half : (j // 2 + 1) * half] for j in range(4)]


def apart_back(lefts, mats):
    rows, half = lefts.shape[1], mats.shape[0] // 2
    out = lax.dot_general(lefts.reshape(2 * rows, lefts.shape[2]), mats, NT, preferred_element_type=jnp.float32)
    return out[:rows, :half], out[rows:, half:]


def near_place(ids_ref, k, i, first, count):
    place = ids_ref[k, i] - first + REACH
    return jnp.where(place >= count, place - count, place)


def near_forward_kernel(
    groups, capacity, ids_ref, ids_row_ref, halo_ref, probe_ref, coeffs_ref, prec_ref,
    part_ref, own_ref, slot_ref, first_ref, mats_ref, ext, coeffs, prec, part, fold, mats, slots, sems
):
    blocks = probe_ref.shape[0]
    chunks = blocks // CHUNK

    def loads(c):
        own = pl.ds(c * CHUNK, CHUNK)
        return (
            pltpu.make_async_copy(coeffs_ref.at[own], coeffs.at[own], sems.at[0, c]),
            pltpu.make_async_copy(prec_ref.at[own], prec.at[own], sems.at[1, c]),
        )

    def store_part(c):
        own = pl.ds(c * CHUNK, CHUNK)
        return pltpu.make_async_copy(part.at[own], part_ref.at[own], sems.at[2, c])

    def store_mats(c):
        own = pl.ds(c * CHUNK, CHUNK)
        return pltpu.make_async_copy(mats.at[own], mats_ref.at[own], sems.at[3, c])

    own_load = pltpu.make_async_copy(probe_ref, ext.at[pl.ds(REACH, blocks)], sems.at[2, 0])
    own_load.start()

    def fetch(c):
        for load in loads(c):
            load.start()

    def ready(c):
        for load in loads(c):
            load.wait()

    for c in range(LEAD):
        fetch(c)
    ext[pl.ds(0, REACH)] = halo_ref[...]
    owner = ids_row_ref[3:4, :] // blocks
    mask = lax.broadcasted_iota(jnp.int32, (groups, blocks), 0) == owner
    rank = jnp.sum(jnp.where(mask, ranks_in(mask, blocks), 0), axis=0, keepdims=True)
    slots[...] = owner * capacity + rank
    slot_copy = pltpu.make_async_copy(slots, slot_ref, sems.at[2, 1])
    slot_copy.start()
    first = lax.axis_index("blk") * blocks
    slot_copy.wait()
    own_load.wait()

    def make(c):
        for b in range(0, CHUNK, 2):
            i = c * CHUNK + b
            rows = []
            for j in range(2):
                tiles = [ext[near_place(ids_ref, k, i + j, first, groups * blocks)] for k in range(3)]
                rows.append(jnp.concatenate(tiles, axis=1))
            near = [stacked(coeffs[i + j, pl.ds(0, 3)]) for j in range(2)]
            mixed = apart(rows[0], rows[1], jnp.concatenate(near, axis=0))
            part[pl.ds(i, 2)] = ext[pl.ds(REACH + i, 2)].astype(jnp.float32) - mixed
            for j in range(2):
                folded = lax.dot_general(prec[i + j], coeffs[i + j, 3], NT, preferred_element_type=jnp.float32)
                fold[i + j] = folded.astype(jnp.bfloat16)
        store_part(c).start()

    def use(c):
        for b in range(0, CHUNK, 2):
            i = c * CHUNK + b
            halves = []
            for j in range(2):
                high = part[i + j].astype(jnp.bfloat16)
                low = (part[i + j] - high.astype(jnp.float32)).astype(jnp.bfloat16)
                halves.append(jnp.concatenate([high, low], axis=0))
            both = apart(halves[0], halves[1], stacked(fold[pl.ds(i, 2)]))
            rows = both.shape[1] // 2
            own_ref[pl.ds(i, 2)] = both[:, :rows] + both[:, rows:]
            for j in range(2):
                mat = jnp.dot(coeffs[i + j, 3], fold[i + j], preferred_element_type=jnp.float32)
                mats[i + j] = mat.astype(jnp.bfloat16)
        store_mats(c).start()

    ready(0)
    fetch(LEAD)
    make(0)

    @pl.loop(1, chunks)
    def _(c):
        ready(c)

        @pl.when(c + LEAD < chunks)
        def _():
            fetch(c + LEAD)

        use(c - 1)
        make(c)

    use(chunks - 1)
    first_ref[...] = mats[pl.ds(0, HELD * CHUNK)]
    for c in range(chunks):
        store_part(c).wait()
        store_mats(c).wait()


def far_kernel(slot, own_ref, far_ref, first_ref, mats_ref, parcel_ref, mats, sems):
    blocks = own_ref.shape[0]
    chunks = blocks // CHUNK

    def load(c):
        own = pl.ds(c * CHUNK, CHUNK)
        return pltpu.make_async_copy(mats_ref.at[own], mats.at[own], sems.at[c])

    for c in range(HELD, chunks):
        load(c).start()

    def send_back(c, pair):
        for b in range(0, CHUNK, 4):
            i = c * CHUNK + b
            mixed = apart4([far_ref[slot[0, i + j]] for j in range(4)], [pair[i + j] for j in range(4)])
            for j in range(4):
                parcel_ref[slot[0, i + j]] = (own_ref[i + j] - mixed[j]).astype(jnp.bfloat16)

    @pl.loop(0, HELD)
    def _(c):
        send_back(c, first_ref)

    @pl.loop(HELD, chunks)
    def _(c):
        load(c).wait()
        send_back(c, mats)


def near_back_kernel(
    groups, ids_ref, slot_ref, far_ref, part_ref, coeffs_ref, prec_ref,
    total, halo_ref, white, scaled, part, coeffs, prec, sems
):
    blocks, _, points = white.shape
    chunks = blocks // CHUNK

    def load(c, which):
        own = pl.ds(c * CHUNK, CHUNK)
        source, target = (
            (part_ref.at[own], part.at[own]),
            (coeffs_ref.at[own, 3], coeffs.at[own, 3]),
            (prec_ref.at[own], prec.at[own]),
            (coeffs_ref.at[own, pl.ds(0, 3)], coeffs.at[own, pl.ds(0, 3)]),
        )[which]
        return pltpu.make_async_copy(source, target, sems.at[which, c])

    def fetch(c):
        for which in range(4):
            load(c, which).start()

    for which in range(3):
        load(0, which).start()
    load(0, 3).start()
    for c in range(1, LEAD):
        fetch(c)
    total[pl.ds(0, REACH)] = jnp.zeros((REACH,) + total.shape[1:], jnp.float32)
    first = lax.axis_index("blk") * blocks

    def mix(c):
        load(c, 0).wait()
        load(c, 1).wait()
        for b in range(0, CHUNK, 4):
            i = c * CHUNK + b
            mixed = apart4([far_ref[slot_ref[0, i + j]] for j in range(4)], [coeffs[i + j, 3] for j in range(4)])
            for j in range(4):
                white[i + j] = (part[i + j] - mixed[j]).astype(jnp.bfloat16)

    def scale(c):
        load(c, 2).wait()
        for b in range(0, CHUNK, 4):
            i = c * CHUNK + b
            tiles = apart4([white[i + j] for j in range(4)], [prec[i + j] for j in range(4)])
            for j in range(4):
                scaled[i + j] = tiles[j].astype(jnp.bfloat16)
                total[REACH + i + j] = scaled[i + j].astype(jnp.float32)

    def back(c):
        load(c, 3).wait()
        terms = []
        for b in range(CHUNK + AHEAD):
            if b < CHUNK and b % 2 == 0:
                i = c * CHUNK + b
                mats = [stacked(coeffs[i + j, pl.ds(0, 3)]) for j in range(2)]
                terms.extend(apart_back(scaled[pl.ds(i, 2)], jnp.concatenate(mats, axis=0)))
            if b >= AHEAD:
                i = c * CHUNK + b - AHEAD
                places = [near_place(ids_ref, k, i, first, groups * blocks) for k in range(3)]
                olds = [total[place] for place in places]
                for k in range(3):
                    total[places[k]] = olds[k] - terms[b - AHEAD][:, k * points : (k + 1) * points]

    mix(0)
    fetch(LEAD)
    scale(0)
    mix(1)
    fetch(LEAD + 1)

    @pl.loop(0, chunks - 2)
    def _(c):
        @pl.when(c + LEAD + 2 < chunks)
        def _():
            fetch(c + LEAD + 2)

        back(c)
        scale(c + 1)
        mix(c + 2)

    back(chunks - 2)
    scale(chunks - 1)
    back(chunks - 1)
    halo_ref[...] = total[pl.ds(0, REACH)].astype(halo_ref.dtype)


def sum_kernel(capacity, picks_ref, base_ref, halo_ref, back_ref, out_ref, total, sem):
    groups = back_ref.shape[0] // capacity
    blocks = out_ref.shape[0]
    last = pl.ds(blocks, REACH)
    total[last] = base_ref[last] + halo_ref[...].astype(jnp.float32)

    @pl.loop(0, groups, unroll=8)
    def _(g):
        picks = [picks_ref[r, g] for r in range(capacity)]
        places = [jnp.where(pick > 0, pick + (REACH - 1), 0) for pick in picks]
        olds = [total[place] for place in places]
        for r in range(capacity):
            total[places[r]] = olds[r] - back_ref[g * capacity + r].astype(jnp.float32)

    store = pltpu.make_async_copy(total.at[pl.ds(REACH, blocks)], out_ref, sem)
    store.start()
    store.wait()


def per_device(probe_vecs, coeffs, cond_prec, neighbours):
    blocks, probes, points = probe_vecs.shape
    groups = lax.axis_size("blk")
    capacity = max(2, blocks // (groups - 1) + 1)
    slots = groups * capacity
    picks_shape = (-(-capacity // 8) * 8, -(-groups // 128) * 128)
    chunks = blocks // CHUNK
    bf16, f32 = jnp.bfloat16, jnp.float32
    tile = (probes, points)
    flops = 2 * blocks * probes * points * points

    def exchange(x):
        return lax.all_to_all(x, "blk", split_axis=0, concat_axis=0, tiled=True)

    ids = neighbours.T
    sent_ids, tail, scalar_ids = pl.pallas_call(
        prep_kernel,
        name="prep",
        out_shape=(
            jax.ShapeDtypeStruct((groups, blocks), jnp.int32),
            jax.ShapeDtypeStruct((REACH,) + tile, bf16),
            pltpu.SMEM(ids.shape, jnp.int32),
        ),
        in_specs=[HBM, HBM],
        out_specs=(VMEM, VMEM, SMEM),
        scratch_shapes=[pltpu.VMEM(ids.shape, jnp.int32), pltpu.SemaphoreType.DMA((3,))],
        compiler_params=params(8),
    )(in_hbm(ids), in_hbm(probe_vecs))
    halo = passed_along(tail, "blk", 1)
    all_ids = exchange(sent_ids)
    all_ids, halo = lax.optimization_barrier((all_ids, halo))
    outgoing, picks = pl.pallas_call(
        functools.partial(pick_kernel, capacity),
        name="pick_tiles",
        out_shape=(
            jax.ShapeDtypeStruct((slots,) + tile, bf16),
            pltpu.SMEM(picks_shape, jnp.int32),
        ),
        in_specs=[VMEM, HBM],
        out_specs=(HBM, SMEM),
        scratch_shapes=[
            pltpu.VMEM((blocks,) + tile, bf16),
            pltpu.VMEM((slots,) + tile, bf16),
            pltpu.VMEM(picks_shape, jnp.int32),
            pltpu.SemaphoreType.DMA((2 + STORES,)),
        ],
        compiler_params=params(8),
        cost_estimate=pl.CostEstimate(flops=0, bytes_accessed=2 * slots * 4096, transcendentals=0),
    )(all_ids, in_hbm(probe_vecs))
    arrived = exchange(outgoing.reshape(groups, capacity * probes, points)).reshape((slots,) + tile)
    mats = (blocks, points, points)
    all_mats = pltpu.VMEM((blocks, 4, points, points), bf16)
    tiles_f32 = jax.ShapeDtypeStruct((blocks,) + tile, f32)
    part, own_far, slot_of, first_mats, far_mats = pl.pallas_call(
        functools.partial(near_forward_kernel, groups, capacity),
        name="near_forward",
        out_shape=(
            pltpu.HBM((blocks,) + tile, f32),
            tiles_f32,
            pltpu.SMEM((1, blocks), jnp.int32),
            jax.ShapeDtypeStruct((HELD * CHUNK, points, points), bf16),
            pltpu.HBM(mats, bf16),
        ),
        in_specs=[SMEM, VMEM, VMEM, HBM, HBM, HBM],
        out_specs=(HBM, VMEM, SMEM, VMEM, HBM),
        scratch_shapes=[
            pltpu.VMEM((REACH + blocks,) + tile, bf16),
            all_mats,
            pltpu.VMEM(mats, bf16),
            pltpu.VMEM((blocks,) + tile, f32),
            pltpu.VMEM(mats, bf16),
            pltpu.VMEM(mats, bf16),
            pltpu.VMEM((1, blocks), jnp.int32),
            pltpu.SemaphoreType.DMA((4, chunks)),
        ],
        compiler_params=params(40),
        cost_estimate=pl.CostEstimate(flops=20 * flops, bytes_accessed=28 * 2**20, transcendentals=0),
    )(scalar_ids, ids, halo, in_hbm(probe_vecs), in_hbm(coeffs), in_hbm(cond_prec))
    parcel = pl.pallas_call(
        far_kernel,
        name="far_terms",
        out_shape=jax.ShapeDtypeStruct((slots,) + tile, bf16),
        in_specs=[SMEM, VMEM, VMEM, VMEM, HBM],
        out_specs=VMEM,
        scratch_shapes=[
            pltpu.VMEM(mats, bf16),
            pltpu.SemaphoreType.DMA((chunks,)),
        ],
        compiler_params=params(16),
        cost_estimate=pl.CostEstimate(flops=flops, bytes_accessed=6 * 2**20, transcendentals=0),
    )(slot_of, own_far, arrived, first_mats, in_hbm(far_mats))
    parcel, arrived = lax.optimization_barrier((parcel, arrived))
    returned = exchange(parcel.reshape(groups, capacity * probes, points)).reshape((slots,) + tile)
    base, halo_back = pl.pallas_call(
        functools.partial(near_back_kernel, groups),
        name="near_back",
        out_shape=(
            jax.ShapeDtypeStruct((REACH + blocks,) + tile, f32),
            jax.ShapeDtypeStruct((REACH,) + tile, bf16),
        ),
        in_specs=[SMEM, SMEM, VMEM, HBM, HBM, HBM],
        out_specs=(VMEM, VMEM),
        scratch_shapes=[
            pltpu.VMEM((blocks,) + tile, bf16),
            pltpu.VMEM((blocks,) + tile, bf16),
            pltpu.VMEM((blocks,) + tile, f32),
            all_mats,
            pltpu.VMEM(mats, bf16),
            pltpu.SemaphoreType.DMA((4, chunks)),
        ],
        compiler_params=params(36),
        cost_estimate=pl.CostEstimate(flops=5 * flops, bytes_accessed=23 * 2**20, transcendentals=0),
    )(scalar_ids, slot_of, arrived, in_hbm(part), in_hbm(coeffs), in_hbm(cond_prec))
    halo_sum = passed_along(halo_back, "blk", -1)
    result, _ = pl.pallas_call(
        functools.partial(sum_kernel, capacity),
        name="final_sum",
        out_shape=(
            jax.ShapeDtypeStruct((blocks,) + tile, f32),
            jax.ShapeDtypeStruct((REACH + blocks,) + tile, f32),
        ),
        in_specs=[SMEM, VMEM, VMEM, VMEM],
        out_specs=(HBM, VMEM),
        scratch_shapes=[pltpu.SemaphoreType.DMA],
        input_output_aliases={1: 1},
        compiler_params=params(8),
        cost_estimate=pl.CostEstimate(flops=0, bytes_accessed=3 * 2**20, transcendentals=0),
    )(picks, base, halo_sum, returned)
    return result


def solution(mesh):
    in_specs = (
        P("blk", None, None),
        P("blk", None, None, None),
        P("blk", None, None),
        P("blk", None),
    )
    return jax.shard_map(
        per_device, mesh=mesh, in_specs=in_specs, out_specs=P("blk", None, None), check_vma=False
    )
```
